32 devices in a mesh: mem: 16 (over z, y, x), sp: 2 (over core).
Axes of the slice: x: 2, y: 2, z: 4, core: 2. Of those that a mesh axis runs over, the one named last changes fastest.
Arguments:
- logarithmic_diffusivity: float32 [128, 16, 1024], P('mem', 'sp'), may hold values from -0.9 to 0.9
- starting_warmth: float32 [16, 1024], P('sp'), may hold values from -4 to 4
- thermal_supply: float32 [16, 1024], P('sp'), may hold values from -4 to 4
- probe_positions: int32 [128], P('sp'), may hold values from 0 to 8191, as said below
- recorded_temps: float32 [128], P('sp'), may hold values from -4 to 4
- probe_error_sigma: float32 [128], P('sp'), may hold values from 0.005 to 0.5
- perturb_draws: float32 [128, 128], P('mem', 'sp'), may hold values from -4 to 4
Outputs:
- revised_lncond: float32 [128, 16, 1024], P('mem', 'sp')
- predicted: float32 [128, 128], P('mem', 'sp')
The draws below stay inside these ranges and needn't reach their ends.
Inputs may be any that keep to these rules, and one draw needn't show every extreme that they name: `probe_positions`: each entry indexes a cell of its own device's slab, row-major over 8 rows of 1024 cells; entry j of a slab's block of 64 lies in row j * 8 // 64.
All inputs are finite; a program needn't handle non-finite values.
Results may differ from the reference program's by a relative error of at most 0.0042.
Values may be sent and summed in bfloat16 or wider, within the bound.
No kernel may reach another device: no remote copies, remote signals or barrier semaphores. Data moves between devices by JAX's collectives and lax.ppermute only.
A program may use at most 64 MiB of HBM per device.

```python
import math
import jax
import jax.numpy as jnp
from jax import lax

SX = 8
SITES_ACROSS = 1024
STEPS = 4
MEMBERS = 128
LATTICE_LINES = 16
OBS_DEV = 64
NOBS = 128


def draw_probe_positions(key, part):
    key = jax.random.fold_in(key, 11)
    position = jnp.arange(NOBS, dtype=jnp.int32) % OBS_DEV
    row_index = position * SX // OBS_DEV
    column = jax.random.randint(key, (NOBS,), 0, SITES_ACROSS, dtype=jnp.int32)
    return (row_index * SITES_ACROSS + column).astype(jnp.int32)


def shard_levels(rng, shape, split, smallest, high):
    def one(dim, blocks):
        steps = jax.random.uniform(jax.random.fold_in(jax.random.fold_in(rng, 6), dim), (blocks,), jnp.float32, smallest / len(split), high / len(split))
        return jnp.repeat(jnp.exp(steps), shape[dim] // blocks).reshape((-1,) + (1,) * (len(shape) - dim - 1))

    gain = one(*split[0])
    for cut in split[1:]:
        gain = gain * one(*cut)
    return gain


def gaussian(own_key, shape, scale, limit, pieces=(), kind=jnp.bfloat16):
    array = scale * jax.random.normal(own_key, shape, jnp.float32)
    if pieces:
        array = array * shard_levels(own_key, shape, pieces, -0.22, 0.18)
    return jnp.clip(array, -limit, limit).astype(kind)


def setup_inputs(seed: int = 0) -> dict:
    arg_keys = jax.random.split(jax.random.key(seed), 8)
    logarithmic_diffusivity = jnp.clip(jax.random.uniform(arg_keys[0], (MEMBERS, LATTICE_LINES, SITES_ACROSS), jnp.float32, -0.9, 0.9) * shard_levels(arg_keys[0], (MEMBERS, LATTICE_LINES, SITES_ACROSS), ((0, 16), (1, 2)), -0.4, 0.0), -0.9, 0.9)
    starting_warmth = gaussian(arg_keys[1], (LATTICE_LINES, SITES_ACROSS), 1.0, 4.0, ((0, 2),), jnp.float32)
    thermal_supply = gaussian(arg_keys[2], (LATTICE_LINES, SITES_ACROSS), 1.0, 4.0, ((0, 2),), jnp.float32)
    probe_positions = draw_probe_positions(jax.random.fold_in(arg_keys[7], 71), 0)
    recorded_temps = gaussian(arg_keys[4], (NOBS,), 1.0, 4.0, ((0, 2),), jnp.float32)
    probe_error_sigma = jnp.clip(jnp.exp(math.log(0.5) - 4.6051702 * jax.random.uniform(arg_keys[5], (NOBS,), jnp.float32) ** shard_levels(arg_keys[5], (NOBS,), ((0, 2),), -0.2, 0.2)), 0.005, 0.5)
    perturb_draws = gaussian(arg_keys[6], (MEMBERS, NOBS), 1.0, 4.0, ((0, 16), (1, 2)), jnp.float32)
    return dict(logarithmic_diffusivity=logarithmic_diffusivity, starting_warmth=starting_warmth, thermal_supply=thermal_supply, probe_positions=probe_positions, recorded_temps=recorded_temps, probe_error_sigma=probe_error_sigma, perturb_draws=perturb_draws)


time_step = 0.06
damping = 2.0
block_width = 16

def invert_block(matrix):
    augmented = jnp.concatenate([matrix, jnp.eye(block_width, dtype=matrix.dtype)], axis=1)
    for place in range(block_width):
        pivot_row = augmented[place] / augmented[place, place]
        augmented = augmented - augmented[:, place:place + 1] * pivot_row[None, :]
        augmented = jnp.concatenate([augmented[:place], pivot_row[None, :], augmented[place + 1:]], axis=0)
    return augmented[:, block_width:]

def eliminate(gram_matrix, cross_term):
    order = gram_matrix.shape[0]
    tableau = jnp.concatenate([gram_matrix, cross_term], axis=1)

    def one_turn(block_number, tableau):
        first_row = (block_number * block_width).astype(jnp.int32)
        row_band = lax.dynamic_slice_in_dim(tableau, first_row, block_width, 0)
        pivot_block = lax.dynamic_slice_in_dim(row_band, first_row, block_width, 1)
        inverse = invert_block(pivot_block)
        scaled_rows = jnp.dot(inverse, row_band, precision=lax.Precision.HIGHEST, preferred_element_type=tableau.dtype)
        column = lax.dynamic_slice_in_dim(tableau, first_row, block_width, 1)
        tableau = tableau - jnp.dot(column, scaled_rows, precision=lax.Precision.HIGHEST, preferred_element_type=tableau.dtype)
        return lax.dynamic_update_slice_in_dim(tableau, scaled_rows, first_row, 0)
    tableau = lax.fori_loop(0, order // block_width, one_turn, tableau)
    return tableau[:, order:]

def advance_solution(padded_warmth, padded_coefficient, thermal_supply):
    warmth_margin = jnp.pad(padded_warmth, ((0, 0), (0, 0), (1, 1)))
    field_pad = jnp.pad(padded_coefficient, ((0, 0), (0, 0), (1, 1)))
    conduct = jnp.exp(field_pad) * (1.0 + 0.5 * jnp.tanh(warmth_margin))
    center = warmth_margin[:, 1:-1, 1:-1]
    cond_mid = conduct[:, 1:-1, 1:-1]
    inflow = jnp.zeros_like(center)
    for row_cut, col_cut in ((slice(2, None), slice(1, -1)), (slice(None, -2), slice(1, -1)), (slice(1, -1), slice(2, None)), (slice(1, -1), slice(None, -2))):
        inflow = inflow + 0.5 * (cond_mid + conduct[:, row_cut, col_cut]) * (warmth_margin[:, row_cut, col_cut] - center)
    return center + time_step * (inflow + thermal_supply)

def reference(logarithmic_diffusivity, starting_warmth, thermal_supply, probe_positions, recorded_temps, probe_error_sigma, perturb_draws):
    member_list = logarithmic_diffusivity.shape[0]
    blank_line = jnp.zeros((member_list, 1, SITES_ACROSS), jnp.float32)
    padded_coefficient = jnp.concatenate([blank_line, logarithmic_diffusivity, blank_line], axis=1)
    thermal_snapshot = jnp.broadcast_to(starting_warmth, logarithmic_diffusivity.shape)
    for iteration in range(STEPS):
        padded_warmth = jnp.concatenate([blank_line, thermal_snapshot, blank_line], axis=1)
        thermal_snapshot = advance_solution(padded_warmth, padded_coefficient, thermal_supply)
    offsets = jnp.arange(NOBS, dtype=jnp.int32) // OBS_DEV * (SX * SITES_ACROSS)
    linear_index = (probe_positions + offsets).astype(jnp.int32)
    predicted = jnp.take(thermal_snapshot.reshape(member_list, LATTICE_LINES * SITES_ACROSS), linear_index, axis=1)
    norm_scale = 1.0 / math.sqrt(MEMBERS - 1)
    centered = predicted - lax.optimization_barrier(jnp.mean(predicted, axis=0, keepdims=True))
    scaled = centered * (norm_scale / probe_error_sigma)
    misfit = (recorded_temps - predicted) / probe_error_sigma + perturb_draws
    gram_matrix = jnp.dot(scaled, scaled.T, precision=lax.Precision.HIGHEST, preferred_element_type=jnp.float32)
    gram_matrix = gram_matrix + damping * jnp.eye(member_list, dtype=jnp.float32)
    cross_term = jnp.dot(scaled, misfit.T, precision=lax.Precision.HIGHEST, preferred_element_type=jnp.float32)
    coeffs = eliminate(gram_matrix, cross_term)
    coeff_round = coeffs.astype(jnp.bfloat16)
    field_round = logarithmic_diffusivity.reshape(member_list, LATTICE_LINES * SITES_ACROSS).astype(jnp.bfloat16)
    change = jnp.dot(coeff_round.T, field_round, preferred_element_type=jnp.float32)
    revised_lncond = logarithmic_diffusivity + (change * norm_scale).reshape(logarithmic_diffusivity.shape)
    return (revised_lncond, predicted)
```

```python
import math

import jax
import jax.numpy as jnp
from jax import lax
from jax.experimental import pallas as pl
from jax.experimental.pallas import tpu as pltpu
from jax.sharding import PartitionSpec as P

STEPS = 4


time_step = 0.06
damping = 2.0
block_width = 16
LANES = 128
ROWS = 8


def invert_block(matrix):
    augmented = jnp.concatenate([matrix, jnp.eye(block_width, dtype=matrix.dtype)], axis=1)
    for place in range(block_width):
        pivot_row = augmented[place] / augmented[place, place]
        augmented = augmented - augmented[:, place : place + 1] * pivot_row[None, :]
        augmented = jnp.concatenate(
            [augmented[:place], pivot_row[None, :], augmented[place + 1 :]], axis=0
        )
    return augmented[:, block_width:]


def eliminate(gram_matrix, cross_term):
    order = gram_matrix.shape[0]
    tableau = jnp.concatenate([gram_matrix, cross_term], axis=1)

    def one_turn(block_number, tableau):
        first_row = (block_number * block_width).astype(jnp.int32)
        row_band = lax.dynamic_slice_in_dim(tableau, first_row, block_width, 0)
        pivot_block = lax.dynamic_slice_in_dim(row_band, first_row, block_width, 1)
        inverse = invert_block(pivot_block)
        scaled_rows = jnp.dot(
            inverse, row_band, precision=lax.Precision.HIGHEST, preferred_element_type=tableau.dtype
        )
        column = lax.dynamic_slice_in_dim(tableau, first_row, block_width, 1)
        tableau = tableau - jnp.dot(
            column,
            scaled_rows,
            precision=lax.Precision.HIGHEST,
            preferred_element_type=tableau.dtype,
        )
        return lax.dynamic_update_slice_in_dim(tableau, scaled_rows, first_row, 0)

    tableau = lax.fori_loop(0, order // block_width, one_turn, tableau)
    return tableau[:, order:]


def conduct_kernel(
    flags_ref,
    columns_ref,
    field_ref,
    field_up_ref,
    field_down_ref,
    small_ref,
    small_up_ref,
    small_down_ref,
    recorded_ref,
    sigma_ref,
    draws_ref,
    predicted_ref,
    payload_ref,
    warmth,
    half_exp,
    supply,
):
    members, lines, width = predicted_ref.shape[0], small_ref.shape[0] // 2, small_ref.shape[1]
    tiles = width // LANES
    window = lines + 2 * STEPS
    lane = lax.broadcasted_iota(jnp.int32, (members, LANES), 1)
    first, last = lane == 0, lane == LANES - 1

    def place(row, ref, small, line, count, inside):
        coefficient = jnp.swapaxes(ref[...].reshape(members, lines, width), 0, 1)
        for step in range(count):
            part = coefficient[line + step]
            heat = small[pl.ds(line + step, 1), :]
            if inside is not None:
                part = jnp.where(inside, part, 0.0)
                heat = jnp.where(inside, heat, 0.0)
            half_exp[row + step] = 0.5 * jnp.exp(part)
            warmth[row + step] = jnp.broadcast_to(heat, (members, width))
        supply[pl.ds(row, count), :] = small[pl.ds(lines + line, count), :]

    above, below = flags_ref[0] > 0, flags_ref[1] > 0
    place(0, field_up_ref, small_up_ref, lines - STEPS, STEPS, above)
    place(STEPS, field_ref, small_ref, 0, lines, None)
    place(STEPS + lines, field_down_ref, small_down_ref, 0, STEPS, below)

    def cut(value):
        return [value[:, k * LANES : (k + 1) * LANES] for k in range(tiles)]

    def conductivity(row, warm):
        half = cut(half_exp[row])
        return [h * (1.0 + 0.5 * jnp.tanh(t)) for h, t in zip(half, warm)]

    half_one = jnp.full((members, LANES), 0.5, jnp.float32)
    zero = jnp.zeros((members, LANES), jnp.float32)

    for step in range(STEPS):
        low, high = step + 1, window - 1 - step
        t_up = cut(warmth[low - 1])
        c_up = conductivity(low - 1, t_up)
        t_here = cut(warmth[low])
        c_here = conductivity(low, t_here)
        flow_up = [(a + b) * (y - x) for a, b, x, y in zip(c_up, c_here, t_up, t_here)]

        def one_row(row, carry):
            t, c, up = carry
            t_next = cut(warmth[row + 1])
            c_next = conductivity(row + 1, t_next)
            down = [(a + b) * (y - x) for a, b, x, y in zip(c, c_next, t, t_next)]
            t_roll = [pltpu.roll(x, LANES - 1, 1) for x in t] + [zero]
            c_roll = [pltpu.roll(x, LANES - 1, 1) for x in c] + [half_one]
            right = []
            for k in range(tiles):
                t_right = jnp.where(last, t_roll[k + 1], t_roll[k])
                c_right = jnp.where(last, c_roll[k + 1], c_roll[k])
                right.append((c[k] + c_right) * (t_right - t[k]))
            back = [pltpu.roll(x, 1, 1) for x in right]
            outside = jnp.logical_or(
                jnp.logical_and(row < STEPS, flags_ref[0] <= 0),
                jnp.logical_and(row >= STEPS + lines, flags_ref[1] <= 0),
            )
            keep = jnp.where(outside, 0.0, 1.0)
            source = supply[pl.ds(row, 1), :]
            for k in range(tiles):
                edge = (c[0] + 0.5) * t[0] if k == 0 else back[k - 1]
                left = jnp.where(first, edge, back[k])
                inflow = (down[k] - up[k]) + (right[k] - left)
                heat = source[:, k * LANES : (k + 1) * LANES]
                warmth[row, :, k * LANES : (k + 1) * LANES] = keep * (
                    t[k] + time_step * (inflow + heat)
                )
            return t_next, c_next, down

        lax.fori_loop(low, high, one_row, (t_here, c_here, flow_up))

    probes = predicted_ref.shape[1]
    lane_probe = lax.broadcasted_iota(jnp.int32, (members, LANES), 1)
    picked = [zero for _ in range(4)]
    for probe in range(probes):
        line = probe * lines // probes
        column = columns_ref[probe] - line * width
        tile = column // LANES
        shift = lax.rem(probe - lax.rem(column, LANES) + LANES, LANES)
        values = warmth[STEPS + line, :, pl.ds(pl.multiple_of(tile * LANES, LANES), LANES)]
        moved = pltpu.roll(values, shift, 1)
        picked[probe % 4] = jnp.where(lane_probe == probe, moved, picked[probe % 4])
    total = (picked[0] + picked[1]) + (picked[2] + picked[3])
    predicted = total[:, :probes]
    predicted_ref[...] = predicted
    normal = (recorded_ref[...] - predicted) / sigma_ref[...]
    payload_ref[0:members, :] = normal
    payload_ref[members : 2 * members, :] = normal + draws_ref[...]


def update_kernel(norm_scale, slabs, place_ref, payload_ref, field_ref, gathered_ref, out_ref):
    devices = payload_ref.shape[0]
    owners = devices // slabs
    members = payload_ref.shape[1] // 2
    order = owners * members
    lines = field_ref.shape[0] // members
    mine = place_ref[0]
    dims = (((1,), (1,)), ((), ()))
    gram, cross = None, None
    for slab in range(slabs):
        normal = jnp.concatenate(
            [payload_ref[owner * slabs + slab, 0:members, :] for owner in range(owners)], axis=0
        )
        center = jnp.sum(normal, axis=0, keepdims=True) * (1.0 / order)
        scaled = (center - normal) * norm_scale
        misfit = payload_ref[mine * slabs + slab, members : 2 * members, :]
        one = lax.dot_general(
            scaled, scaled, dims, precision=lax.Precision.HIGHEST, preferred_element_type=jnp.float32
        )
        two = lax.dot_general(
            misfit, scaled, dims, precision=lax.Precision.HIGHEST, preferred_element_type=jnp.float32
        )
        gram = one if gram is None else gram + one
        cross = two if cross is None else cross + two
    row_id = lax.broadcasted_iota(jnp.int32, (ROWS, order), 0)
    lane_id = lax.broadcasted_iota(jnp.int32, (ROWS, order), 1)
    blocks = order // ROWS
    tableau = [
        gram[k * ROWS : (k + 1) * ROWS, :]
        + jnp.where(lane_id == row_id + k * ROWS, damping, 0.0)
        for k in range(blocks)
    ]
    tableau.append(cross)

    def lanes_of(value, at):
        return jnp.broadcast_to(value[:, at : at + 1], (ROWS, order))

    def row_of(value, at):
        return jnp.broadcast_to(value[at : at + 1, :], (ROWS, order))

    for block in range(blocks):
        base = block * ROWS
        inside = jnp.logical_and(lane_id >= base, lane_id < base + ROWS)
        band = tableau[block]
        column = [lanes_of(band, base + q) for q in range(ROWS)]
        band = jnp.where(inside, jnp.where(lane_id == row_id + base, -1.0, 0.0), band)
        for q in range(ROWS):
            here = row_id == q
            inverse = 1.0 / row_of(column[q], q)
            pivot_row = row_of(band, q) * inverse
            band = jnp.where(here, pivot_row, band - column[q] * pivot_row)
            for j in range(q + 1, ROWS):
                factor = row_of(column[j], q) * inverse
                column[j] = jnp.where(here, factor, column[j] - column[q] * factor)
        rows = [row_of(band, q) for q in range(ROWS)]
        for other in range(block + 1, blocks + 1):
            value = tableau[other]
            products = [lanes_of(value, base + q) * rows[q] for q in range(ROWS)]
            while len(products) > 1:
                products = [a + b for a, b in zip(products[::2], products[1::2])]
            tableau[other] = jnp.where(inside, 0.0, value) - products[0]
    solved = tableau[blocks].astype(jnp.bfloat16)

    wide = order * lines
    spread = (
        lax.broadcasted_iota(jnp.int32, (order, wide), 1) // lines
        == lax.broadcasted_iota(jnp.int32, (order, wide), 0)
    ).astype(jnp.bfloat16)
    stretched = jnp.dot(solved, spread, preferred_element_type=jnp.float32)
    on_line = lax.broadcasted_iota(jnp.int32, (lines, wide), 1) % lines == (
        lax.broadcasted_iota(jnp.int32, (lines, wide), 0)
    )
    weights = jnp.concatenate(
        [
            jnp.where(on_line, jnp.broadcast_to(stretched[j : j + 1, :], (lines, wide)), 0.0)
            for j in range(members)
        ],
        axis=0,
    ).astype(jnp.bfloat16)
    change = jnp.dot(weights, gathered_ref[...], preferred_element_type=jnp.float32)
    out_ref[...] = field_ref[...] + change * norm_scale


def body(
    logarithmic_diffusivity,
    starting_warmth,
    thermal_supply,
    probe_positions,
    recorded_temps,
    probe_error_sigma,
    perturb_draws,
):
    members, lines, width = logarithmic_diffusivity.shape
    owners, slabs = lax.axis_size("mem"), lax.axis_size("sp")
    order = members * owners
    norm_scale = 1.0 / math.sqrt(order - 1)
    probes = probe_positions.shape[0]
    slab = lax.axis_index("sp")

    field_flat = logarithmic_diffusivity.reshape(members * lines, width)
    gathered = lax.all_gather(field_flat.astype(jnp.bfloat16), "mem", axis=0, tiled=True)

    small = jnp.concatenate([starting_warmth, thermal_supply], axis=0)
    if slabs == 2:
        swap = [(0, 1), (1, 0)]
        field_up = field_down = lax.ppermute(field_flat, "sp", swap)
        small_up = small_down = lax.ppermute(small, "sp", swap)
    else:
        fall = [(i, i + 1) for i in range(slabs - 1)]
        rise = [(i + 1, i) for i in range(slabs - 1)]
        field_up, small_up = lax.ppermute((field_flat, small), "sp", fall)
        field_down, small_down = lax.ppermute((field_flat, small), "sp", rise)
    flags = jnp.stack([slab > 0, slab < slabs - 1]).astype(jnp.int32)
    vmem = pl.BlockSpec(memory_space=pltpu.VMEM)
    smem = pl.BlockSpec(memory_space=pltpu.SMEM)
    window = lines + 2 * STEPS
    predicted, payload = pl.pallas_call(
        conduct_kernel,
        out_shape=(
            jax.ShapeDtypeStruct((members, probes), jnp.float32),
            jax.ShapeDtypeStruct((2 * members, probes), jnp.float32),
        ),
        in_specs=[smem, smem] + [vmem] * 9,
        out_specs=(vmem, vmem),
        scratch_shapes=[
            pltpu.VMEM((window, members, width), jnp.float32),
            pltpu.VMEM((window, members, width), jnp.float32),
            pltpu.VMEM((window, width), jnp.float32),
        ],
        compiler_params=pltpu.CompilerParams(vmem_limit_bytes=16 * 1024 * 1024),
        cost_estimate=pl.CostEstimate(
            flops=30 * STEPS * window * members * width,
            bytes_accessed=4 * 3 * members * lines * width,
            transcendentals=STEPS * window * members * width,
        ),
        name="conduct",
    )(
        flags,
        probe_positions,
        field_flat,
        field_up,
        field_down,
        small,
        small_up,
        small_down,
        recorded_temps[None, :],
        probe_error_sigma[None, :],
        perturb_draws,
    )
    devices = owners * slabs
    everyone = lax.all_to_all(
        jnp.broadcast_to(payload[None], (devices,) + payload.shape), ("mem", "sp"), 0, 0
    )
    place = lax.axis_index("mem").astype(jnp.int32)[None]
    if order <= LANES:
        revised = pl.pallas_call(
            lambda *refs: update_kernel(norm_scale, slabs, *refs),
            out_shape=jax.ShapeDtypeStruct((members * lines, width), jnp.float32),
            in_specs=[smem] + [vmem] * 3,
            out_specs=vmem,
            compiler_params=pltpu.CompilerParams(vmem_limit_bytes=32 * 1024 * 1024),
            cost_estimate=pl.CostEstimate(
                flops=2 * order * order * order,
                bytes_accessed=2 * order * lines * width,
                transcendentals=0,
            ),
            name="update",
        )(place, everyone, field_flat, gathered)
    else:
        split = everyone.reshape(owners, slabs, 2, members, probes)
        normal = split[:, :, 0].transpose(0, 2, 1, 3).reshape(order, slabs * probes)
        misfit = lax.dynamic_index_in_dim(split[:, :, 1], place[0], 0, False)
        misfit = misfit.transpose(1, 0, 2).reshape(members, slabs * probes)
        scaled = (jnp.mean(normal, axis=0, keepdims=True) - normal) * norm_scale
        gram_matrix = jnp.dot(
            scaled, scaled.T, precision=lax.Precision.HIGHEST, preferred_element_type=jnp.float32
        ) + damping * jnp.eye(order, dtype=jnp.float32)
        cross_term = jnp.dot(
            scaled, misfit.T, precision=lax.Precision.HIGHEST, preferred_element_type=jnp.float32
        )
        coeff_round = eliminate(gram_matrix, cross_term).astype(jnp.bfloat16)
        change = lax.dot_general(
            coeff_round,
            gathered.reshape(order, lines * width),
            (((0,), (0,)), ((), ())),
            preferred_element_type=jnp.float32,
        ).reshape(field_flat.shape)
        revised = field_flat + change * norm_scale
    return (revised.reshape(logarithmic_diffusivity.shape), predicted)


def solution(mesh):
    in_specs = (
        P("mem", "sp", None),
        P("sp", None),
        P("sp", None),
        P("sp"),
        P("sp"),
        P("sp"),
        P("mem", "sp"),
    )
    out_specs = (P("mem", "sp", None), P("mem", "sp"))
    return jax.shard_map(body, mesh=mesh, in_specs=in_specs, out_specs=out_specs, check_vma=False)
```

```python
import math

import jax
import jax.numpy as jnp
from jax import lax
from jax.experimental import pallas as pl
from jax.experimental.pallas import tpu as pltpu
from jax.sharding import PartitionSpec as P

STEPS = 4


time_step = 0.06
damping = 2.0
block_width = 16
LANES = 128
ROWS = 8


def invert_block(matrix):
    augmented = jnp.concatenate([matrix, jnp.eye(block_width, dtype=matrix.dtype)], axis=1)
    for place in range(block_width):
        pivot_row = augmented[place] / augmented[place, place]
        augmented = augmented - augmented[:, place : place + 1] * pivot_row[None, :]
        augmented = jnp.concatenate(
            [augmented[:place], pivot_row[None, :], augmented[place + 1 :]], axis=0
        )
    return augmented[:, block_width:]


def eliminate(gram_matrix, cross_term):
    order = gram_matrix.shape[0]
    tableau = jnp.concatenate([gram_matrix, cross_term], axis=1)

    def one_turn(block_number, tableau):
        first_row = (block_number * block_width).astype(jnp.int32)
        row_band = lax.dynamic_slice_in_dim(tableau, first_row, block_width, 0)
        pivot_block = lax.dynamic_slice_in_dim(row_band, first_row, block_width, 1)
        inverse = invert_block(pivot_block)
        scaled_rows = jnp.dot(
            inverse, row_band, precision=lax.Precision.HIGHEST, preferred_element_type=tableau.dtype
        )
        column = lax.dynamic_slice_in_dim(tableau, first_row, block_width, 1)
        tableau = tableau - jnp.dot(
            column,
            scaled_rows,
            precision=lax.Precision.HIGHEST,
            preferred_element_type=tableau.dtype,
        )
        return lax.dynamic_update_slice_in_dim(tableau, scaled_rows, first_row, 0)

    tableau = lax.fori_loop(0, order // block_width, one_turn, tableau)
    return tableau[:, order:]


def conduct_kernel(
    flags_ref,
    columns_hbm,
    field_ref,
    up_ref,
    down_ref,
    warmth_hbm,
    supply_hbm,
    recorded_hbm,
    sigma_hbm,
    draws_hbm,
    predicted_ref,
    payload_ref,
    warmth,
    half_exp,
    supply,
    columns_ref,
    small_ref,
    recorded_ref,
    sigma_ref,
    draws_ref,
    sems,
):
    lines = warmth_hbm.shape[0]
    copies = [
        pltpu.make_async_copy(source, target, sems.at[k])
        for k, (source, target) in enumerate(
            (
                (warmth_hbm, small_ref.at[pl.ds(0, lines)]),
                (supply_hbm, small_ref.at[pl.ds(lines, lines)]),
                (columns_hbm, columns_ref),
                (recorded_hbm, recorded_ref),
                (sigma_hbm, sigma_ref),
                (draws_hbm, draws_ref),
            )
        )
    ]
    for copy in copies:
        copy.start()
    for copy in copies:
        copy.wait()
    members, width = predicted_ref.shape[0], small_ref.shape[1]
    tiles = width // LANES
    window = lines + 2 * STEPS
    lane = lax.broadcasted_iota(jnp.int32, (members, LANES), 1)
    first, last = lane == 0, lane == LANES - 1

    def place(row, ref, small, base, line, count, inside):
        coefficient = jnp.swapaxes(
            ref[0 : members * lines, :].reshape(members, lines, width), 0, 1
        )
        for step in range(count):
            part = coefficient[line + step]
            heat = small[pl.ds(base + line + step, 1), :]
            if inside is not None:
                part = jnp.where(inside, part, 0.0)
                heat = jnp.where(inside, heat, 0.0)
            half_exp[row + step] = 0.5 * jnp.exp(part)
            warmth[row + step] = jnp.broadcast_to(heat, (members, width))
        supply[pl.ds(row, count), :] = small[pl.ds(base + lines + line, count), :]

    above, below = flags_ref[0] > 0, flags_ref[1] > 0
    place(0, up_ref, up_ref, members * lines, lines - STEPS, STEPS, above)
    place(STEPS, field_ref, small_ref, 0, 0, lines, None)
    place(STEPS + lines, down_ref, down_ref, members * lines, 0, STEPS, below)

    def cut(value):
        return [value[:, k * LANES : (k + 1) * LANES] for k in range(tiles)]

    def conductivity(row, warm):
        half = cut(half_exp[row])
        return [h * (1.0 + 0.5 * jnp.tanh(t)) for h, t in zip(half, warm)]

    half_one = jnp.full((members, LANES), 0.5, jnp.float32)
    zero = jnp.zeros((members, LANES), jnp.float32)

    for step in range(STEPS):
        low, high = step + 1, window - 1 - step
        t_up = cut(warmth[low - 1])
        c_up = conductivity(low - 1, t_up)
        t_here = cut(warmth[low])
        c_here = conductivity(low, t_here)
        flow_up = [(a + b) * (y - x) for a, b, x, y in zip(c_up, c_here, t_up, t_here)]

        def one_row(row, carry):
            t, c, up = carry
            t_next = cut(warmth[row + 1])
            c_next = conductivity(row + 1, t_next)
            down = [(a + b) * (y - x) for a, b, x, y in zip(c, c_next, t, t_next)]
            t_roll = [pltpu.roll(x, LANES - 1, 1) for x in t] + [zero]
            c_roll = [pltpu.roll(x, LANES - 1, 1) for x in c] + [half_one]
            right = []
            for k in range(tiles):
                t_right = jnp.where(last, t_roll[k + 1], t_roll[k])
                c_right = jnp.where(last, c_roll[k + 1], c_roll[k])
                right.append((c[k] + c_right) * (t_right - t[k]))
            back = [pltpu.roll(x, 1, 1) for x in right]
            outside = jnp.logical_or(
                jnp.logical_and(row < STEPS, flags_ref[0] <= 0),
                jnp.logical_and(row >= STEPS + lines, flags_ref[1] <= 0),
            )
            keep = jnp.where(outside, 0.0, 1.0)
            source = supply[pl.ds(row, 1), :]
            for k in range(tiles):
                edge = (c[0] + 0.5) * t[0] if k == 0 else back[k - 1]
                left = jnp.where(first, edge, back[k])
                inflow = (down[k] - up[k]) + (right[k] - left)
                heat = source[:, k * LANES : (k + 1) * LANES]
                warmth[row, :, k * LANES : (k + 1) * LANES] = keep * (
                    t[k] + time_step * (inflow + heat)
                )
            return t_next, c_next, down

        lax.fori_loop(low, high, one_row, (t_here, c_here, flow_up))

    probes = predicted_ref.shape[1]
    lane_probe = lax.broadcasted_iota(jnp.int32, (members, LANES), 1)
    picked = [zero for _ in range(4)]
    for probe in range(probes):
        line = probe * lines // probes
        column = columns_ref[probe] - line * width
        tile = column // LANES
        shift = lax.rem(probe - lax.rem(column, LANES) + LANES, LANES)
        values = warmth[STEPS + line, :, pl.ds(pl.multiple_of(tile * LANES, LANES), LANES)]
        moved = pltpu.roll(values, shift, 1)
        picked[probe % 4] = jnp.where(lane_probe == probe, moved, picked[probe % 4])
    total = (picked[0] + picked[1]) + (picked[2] + picked[3])
    predicted = total[:, :probes]
    predicted_ref[...] = predicted
    normal = (recorded_ref[...] - predicted) / sigma_ref[...]
    payload = jnp.concatenate([normal, normal + draws_ref[...]], axis=1)
    for device in range(payload_ref.shape[0]):
        payload_ref[device] = payload


def solve_kernel(norm_scale, slabs, offsets, place_ref, payload_ref, solved_ref):
    members, probes = payload_ref.shape[1], payload_ref.shape[2] // 2
    order = len(offsets) * members
    mine = place_ref[0]
    dims = (((1,), (1,)), ((), ()))
    gram, cross = None, None
    for slab in range(slabs):
        blocks = [
            payload_ref[jnp.bitwise_xor(mine, offset) * slabs + slab] for offset in offsets
        ]
        normal = jnp.concatenate([block[:, :probes] for block in blocks], axis=0)
        center = jnp.sum(normal, axis=0, keepdims=True) * (1.0 / order)
        scaled = (center - normal) * norm_scale
        misfit = jnp.concatenate([block[:, probes:] for block in blocks[:2]], axis=0)
        one = lax.dot_general(
            scaled, scaled, dims, precision=lax.Precision.HIGHEST, preferred_element_type=jnp.float32
        )
        two = lax.dot_general(
            misfit, scaled, dims, precision=lax.Precision.HIGHEST, preferred_element_type=jnp.float32
        )
        gram = one if gram is None else gram + one
        cross = two if cross is None else cross + two
    row_id = lax.broadcasted_iota(jnp.int32, (ROWS, order), 0)
    lane_id = lax.broadcasted_iota(jnp.int32, (ROWS, order), 1)
    blocks = order // ROWS
    tableau = [
        gram[k * ROWS : (k + 1) * ROWS, :]
        + jnp.where(lane_id == row_id + k * ROWS, damping, 0.0)
        for k in range(blocks)
    ]
    tableau += [cross[k : k + ROWS, :] for k in range(0, 2 * members, ROWS)]

    def lanes_of(value, at):
        return jnp.broadcast_to(value[:, at : at + 1], (ROWS, order))

    def row_of(value, at):
        return jnp.broadcast_to(value[at : at + 1, :], (ROWS, order))

    for block in range(blocks):
        base = block * ROWS
        inside = jnp.logical_and(lane_id >= base, lane_id < base + ROWS)
        band = tableau[block]
        column = [lanes_of(band, base + q) for q in range(ROWS)]
        band = jnp.where(inside, jnp.where(lane_id == row_id + base, -1.0, 0.0), band)
        for q in range(ROWS):
            here = row_id == q
            inverse = 1.0 / row_of(column[q], q)
            pivot_row = row_of(band, q) * inverse
            band = jnp.where(here, pivot_row, band - column[q] * pivot_row)
            for j in range(q + 1, ROWS):
                factor = row_of(column[j], q) * inverse
                column[j] = jnp.where(here, factor, column[j] - column[q] * factor)
        rows = [row_of(band, q) for q in range(ROWS)]
        for other in range(block + 1, len(tableau)):
            value = tableau[other]
            products = [lanes_of(value, base + q) * rows[q] for q in range(ROWS)]
            while len(products) > 1:
                products = [a + b for a, b in zip(products[::2], products[1::2])]
            tableau[other] = jnp.where(inside, 0.0, value) - products[0]
    solved_ref[...] = jnp.concatenate(tableau[blocks:], axis=0).astype(jnp.bfloat16)


def apply_kernel(norm_scale, lines, solved_ref, *refs):
    part_refs, own_ref, give_ref = refs[:-2], refs[-2], refs[-1]
    solved = solved_ref[...]
    pair, order = solved.shape
    wide = order * lines
    spread = (
        lax.broadcasted_iota(jnp.int32, (order, wide), 1) // lines
        == lax.broadcasted_iota(jnp.int32, (order, wide), 0)
    ).astype(jnp.bfloat16)
    stretched = jnp.dot(solved, spread, preferred_element_type=jnp.float32)
    on_line = lax.broadcasted_iota(jnp.int32, (lines, wide), 1) % lines == (
        lax.broadcasted_iota(jnp.int32, (lines, wide), 0)
    )
    weights = jnp.concatenate(
        [
            jnp.where(on_line, jnp.broadcast_to(stretched[j : j + 1, :], (lines, wide)), 0.0)
            for j in range(pair)
        ],
        axis=0,
    ).astype(jnp.bfloat16)
    change, start = None, 0
    for ref in part_refs:
        deep = ref.shape[0]
        part = jnp.dot(
            weights[:, start : start + deep], ref[...], preferred_element_type=jnp.float32
        )
        change = part if change is None else change + part
        start += deep
    change = change * norm_scale
    rows = own_ref.shape[0]
    own_ref[...] = change[:rows]
    give_ref[...] = change[rows:].astype(give_ref.dtype)


def merge_kernel(odd_ref, field_ref, own_ref, got_ref, out_ref):
    own, got = own_ref[...], got_ref[...].astype(jnp.float32)
    half = own.shape[1]
    even = odd_ref[0] == 0
    out_ref[:, :half] = field_ref[:, :half] + jnp.where(even, own, got)
    out_ref[:, half:] = field_ref[:, half:] + jnp.where(even, got, own)


def body(
    logarithmic_diffusivity,
    starting_warmth,
    thermal_supply,
    probe_positions,
    recorded_temps,
    probe_error_sigma,
    perturb_draws,
):
    members, lines, width = logarithmic_diffusivity.shape
    owners, slabs = lax.axis_size("mem"), lax.axis_size("sp")
    order = members * owners
    norm_scale = 1.0 / math.sqrt(order - 1)
    probes = probe_positions.shape[0]
    slab = lax.axis_index("sp")

    mine = lax.axis_index("mem").astype(jnp.int32)
    odd = mine & 1
    half = width // 2

    def across(value, bit):
        return lax.ppermute(value, "mem", [(i, i ^ bit) for i in range(owners)])

    field_flat = logarithmic_diffusivity.reshape(members * lines, width)
    field_round = field_flat.astype(jnp.bfloat16)
    left, right = field_round[:, :half], field_round[:, half:]
    held = jnp.where(odd == 0, left, right)
    parts = [held, across(jnp.where(odd == 0, right, left), 1)]
    offsets = [0, 1]
    bit = owners // 2
    while bit > 1:
        held = jnp.concatenate(parts, axis=0)
        parts = [held, across(held, bit)]
        offsets = offsets + [offset ^ bit for offset in offsets]
        bit //= 2

    edges = jnp.concatenate([field_flat, starting_warmth, thermal_supply], axis=0)
    if slabs == 2:
        up = down = lax.ppermute(edges, "sp", [(0, 1), (1, 0)])
    else:
        up = lax.ppermute(edges, "sp", [(i, i + 1) for i in range(slabs - 1)])
        down = lax.ppermute(edges, "sp", [(i + 1, i) for i in range(slabs - 1)])
    flags = jnp.stack([slab > 0, slab < slabs - 1]).astype(jnp.int32)
    vmem = pl.BlockSpec(memory_space=pltpu.VMEM)
    smem = pl.BlockSpec(memory_space=pltpu.SMEM)
    anywhere = pl.BlockSpec(memory_space=pl.ANY)
    window = lines + 2 * STEPS
    devices = owners * slabs
    predicted, payload = pl.pallas_call(
        conduct_kernel,
        out_shape=(
            jax.ShapeDtypeStruct((members, probes), jnp.float32),
            jax.ShapeDtypeStruct((devices, members, 2 * probes), jnp.float32),
        ),
        in_specs=[smem, anywhere] + [vmem] * 3 + [anywhere] * 5,
        out_specs=(vmem, vmem),
        scratch_shapes=[
            pltpu.VMEM((window, members, width), jnp.float32),
            pltpu.VMEM((window, members, width), jnp.float32),
            pltpu.VMEM((window, width), jnp.float32),
            pltpu.SMEM((probes,), jnp.int32),
            pltpu.VMEM((2 * lines, width), jnp.float32),
            pltpu.VMEM((1, probes), jnp.float32),
            pltpu.VMEM((1, probes), jnp.float32),
            pltpu.VMEM((members, probes), jnp.float32),
            pltpu.SemaphoreType.DMA((6,)),
        ],
        compiler_params=pltpu.CompilerParams(vmem_limit_bytes=24 * 1024 * 1024),
        cost_estimate=pl.CostEstimate(
            flops=30 * STEPS * window * members * width,
            bytes_accessed=4 * 3 * members * lines * width,
            transcendentals=STEPS * window * members * width,
        ),
        name="conduct",
    )(
        flags,
        probe_positions,
        field_flat,
        up,
        down,
        starting_warmth,
        thermal_supply,
        recorded_temps[None, :],
        probe_error_sigma[None, :],
        perturb_draws,
    )
    everyone = lax.all_to_all(payload, ("mem", "sp"), 0, 0, tiled=True)
    if order <= LANES:
        solved = pl.pallas_call(
            lambda *refs: solve_kernel(norm_scale, slabs, offsets, *refs),
            out_shape=jax.ShapeDtypeStruct((2 * members, order), jnp.bfloat16),
            in_specs=[smem, vmem],
            out_specs=vmem,
            compiler_params=pltpu.CompilerParams(vmem_limit_bytes=16 * 1024 * 1024),
            cost_estimate=pl.CostEstimate(
                flops=2 * order * order * order,
                bytes_accessed=4 * devices * members * 2 * probes,
                transcendentals=0,
            ),
            name="solve",
        )(mine[None], everyone)
    else:
        owner = mine ^ jnp.array(offsets, jnp.int32)
        split = everyone.reshape(owners, slabs, members, 2, probes)[owner]
        split = split.transpose(3, 0, 2, 1, 4).reshape(2, order, slabs * probes)
        normal, misfit = split[0], split[1, : 2 * members]
        scaled = (jnp.mean(normal, axis=0, keepdims=True) - normal) * norm_scale
        gram_matrix = jnp.dot(
            scaled, scaled.T, precision=lax.Precision.HIGHEST, preferred_element_type=jnp.float32
        ) + damping * jnp.eye(order, dtype=jnp.float32)
        cross_term = jnp.dot(
            scaled, misfit.T, precision=lax.Precision.HIGHEST, preferred_element_type=jnp.float32
        )
        solved = eliminate(gram_matrix, cross_term).T.astype(jnp.bfloat16)
    own, give = pl.pallas_call(
        lambda *refs: apply_kernel(norm_scale, lines, *refs),
        out_shape=(
            jax.ShapeDtypeStruct((members * lines, half), jnp.float32),
            jax.ShapeDtypeStruct((members * lines, half), jnp.bfloat16),
        ),
        in_specs=[vmem] * (1 + len(parts)),
        out_specs=(vmem, vmem),
        compiler_params=pltpu.CompilerParams(vmem_limit_bytes=40 * 1024 * 1024),
        cost_estimate=pl.CostEstimate(
            flops=4 * members * lines * order * lines * half,
            bytes_accessed=2 * order * lines * half,
            transcendentals=0,
        ),
        name="apply",
    )(solved, *parts)
    got = across(give, 1)
    revised = pl.pallas_call(
        merge_kernel,
        out_shape=jax.ShapeDtypeStruct((members * lines, width), jnp.float32),
        in_specs=[smem] + [vmem] * 3,
        out_specs=vmem,
        name="merge",
    )(odd[None], field_flat, own, got)
    return (revised.reshape(logarithmic_diffusivity.shape), predicted)


def solution(mesh):
    in_specs = (
        P("mem", "sp", None),
        P("sp", None),
        P("sp", None),
        P("sp"),
        P("sp"),
        P("sp"),
        P("mem", "sp"),
    )
    out_specs = (P("mem", "sp", None), P("mem", "sp"))
    return jax.shard_map(body, mesh=mesh, in_specs=in_specs, out_specs=out_specs, check_vma=False)
```

```python
import math

import jax
import jax.numpy as jnp
from jax import lax
from jax.experimental import pallas as pl
from jax.experimental.pallas import tpu as pltpu
from jax.sharding import PartitionSpec as P

STEPS = 4


time_step = 0.06
damping = 2.0
block_width = 16
LANES = 128
ROWS = 8


def invert_block(matrix):
    augmented = jnp.concatenate([matrix, jnp.eye(block_width, dtype=matrix.dtype)], axis=1)
    for place in range(block_width):
        pivot_row = augmented[place] / augmented[place, place]
        augmented = augmented - augmented[:, place : place + 1] * pivot_row[None, :]
        augmented = jnp.concatenate(
            [augmented[:place], pivot_row[None, :], augmented[place + 1 :]], axis=0
        )
    return augmented[:, block_width:]


def eliminate(gram_matrix, cross_term):
    order = gram_matrix.shape[0]
    tableau = jnp.concatenate([gram_matrix, cross_term], axis=1)

    def one_turn(block_number, tableau):
        first_row = (block_number * block_width).astype(jnp.int32)
        row_band = lax.dynamic_slice_in_dim(tableau, first_row, block_width, 0)
        pivot_block = lax.dynamic_slice_in_dim(row_band, first_row, block_width, 1)
        inverse = invert_block(pivot_block)
        scaled_rows = jnp.dot(
            inverse, row_band, precision=lax.Precision.HIGHEST, preferred_element_type=tableau.dtype
        )
        column = lax.dynamic_slice_in_dim(tableau, first_row, block_width, 1)
        tableau = tableau - jnp.dot(
            column,
            scaled_rows,
            precision=lax.Precision.HIGHEST,
            preferred_element_type=tableau.dtype,
        )
        return lax.dynamic_update_slice_in_dim(tableau, scaled_rows, first_row, 0)

    tableau = lax.fori_loop(0, order // block_width, one_turn, tableau)
    return tableau[:, order:]


def conduct_kernel(
    flags_ref,
    columns_hbm,
    field_ref,
    up_ref,
    down_ref,
    warmth_hbm,
    supply_hbm,
    recorded_hbm,
    sigma_hbm,
    draws_hbm,
    predicted_ref,
    payload_ref,
    warmth,
    half_exp,
    supply,
    columns_ref,
    small_ref,
    recorded_ref,
    sigma_ref,
    draws_ref,
    sems,
):
    lines = warmth_hbm.shape[0]
    copies = [
        pltpu.make_async_copy(source, target, sems.at[k])
        for k, (source, target) in enumerate(
            (
                (warmth_hbm, small_ref.at[pl.ds(0, lines)]),
                (supply_hbm, small_ref.at[pl.ds(lines, lines)]),
                (columns_hbm, columns_ref),
                (recorded_hbm, recorded_ref),
                (sigma_hbm, sigma_ref),
                (draws_hbm, draws_ref),
            )
        )
    ]
    for copy in copies:
        copy.start()
    members, width = predicted_ref.shape[0], small_ref.shape[1]
    tiles = width // LANES
    window = lines + 2 * STEPS
    lane = lax.broadcasted_iota(jnp.int32, (members, LANES), 1)
    first, last = lane == 0, lane == LANES - 1

    above, below = flags_ref[0] > 0, flags_ref[1] > 0
    sides = (
        (0, up_ref, lines - STEPS, STEPS, above),
        (STEPS, field_ref, 0, lines, None),
        (STEPS + lines, down_ref, 0, STEPS, below),
    )
    for row, ref, line, count, inside in sides:
        coefficient = jnp.swapaxes(
            ref[0 : members * lines, :].reshape(members, lines, width), 0, 1
        )
        for step in range(count):
            part = coefficient[line + step]
            if inside is not None:
                part = jnp.where(inside, part, 0.0)
            half_exp[row + step] = 0.5 * jnp.exp(part)
    copies[0].wait()
    copies[1].wait()
    for row, ref, line, count, inside in sides:
        small, base = (small_ref, 0) if inside is None else (ref, members * lines)
        for step in range(count):
            heat = small[pl.ds(base + line + step, 1), :]
            if inside is not None:
                heat = jnp.where(inside, heat, 0.0)
            warmth[row + step] = jnp.broadcast_to(heat, (members, width))
        supply[pl.ds(row, count), :] = small[pl.ds(base + lines + line, count), :]

    def cut(value):
        return [value[:, k * LANES : (k + 1) * LANES] for k in range(tiles)]

    def conductivity(row, warm):
        half = cut(half_exp[row])
        return [h * (1.0 + 0.5 * jnp.tanh(t)) for h, t in zip(half, warm)]

    half_one = jnp.full((members, LANES), 0.5, jnp.float32)
    zero = jnp.zeros((members, LANES), jnp.float32)

    for step in range(STEPS):
        low, high = step + 1, window - 1 - step
        t_up = cut(warmth[low - 1])
        c_up = conductivity(low - 1, t_up)
        t_here = cut(warmth[low])
        c_here = conductivity(low, t_here)
        flow_up = [(a + b) * (y - x) for a, b, x, y in zip(c_up, c_here, t_up, t_here)]

        def one_row(row, carry):
            t, c, up = carry
            t_next = cut(warmth[row + 1])
            c_next = conductivity(row + 1, t_next)
            down = [(a + b) * (y - x) for a, b, x, y in zip(c, c_next, t, t_next)]
            t_roll = [pltpu.roll(x, LANES - 1, 1) for x in t] + [zero]
            c_roll = [pltpu.roll(x, LANES - 1, 1) for x in c] + [half_one]
            right = []
            for k in range(tiles):
                t_right = jnp.where(last, t_roll[k + 1], t_roll[k])
                c_right = jnp.where(last, c_roll[k + 1], c_roll[k])
                right.append((c[k] + c_right) * (t_right - t[k]))
            back = [pltpu.roll(x, 1, 1) for x in right]
            outside = jnp.logical_or(
                jnp.logical_and(row < STEPS, flags_ref[0] <= 0),
                jnp.logical_and(row >= STEPS + lines, flags_ref[1] <= 0),
            )
            keep = jnp.where(outside, 0.0, 1.0)
            source = supply[pl.ds(row, 1), :]
            for k in range(tiles):
                edge = (c[0] + 0.5) * t[0] if k == 0 else back[k - 1]
                left = jnp.where(first, edge, back[k])
                inflow = (down[k] - up[k]) + (right[k] - left)
                heat = source[:, k * LANES : (k + 1) * LANES]
                warmth[row, :, k * LANES : (k + 1) * LANES] = keep * (
                    t[k] + time_step * (inflow + heat)
                )
            return t_next, c_next, down

        lax.fori_loop(low, high, one_row, (t_here, c_here, flow_up), unroll=True)

    for copy in copies[2:]:
        copy.wait()
    probes = predicted_ref.shape[1]
    lane_probe = lax.broadcasted_iota(jnp.int32, (members, LANES), 1)
    picked = [zero for _ in range(4)]
    for probe in range(probes):
        line = probe * lines // probes
        column = columns_ref[probe] - line * width
        tile = column // LANES
        shift = lax.rem(probe - lax.rem(column, LANES) + LANES, LANES)
        values = warmth[STEPS + line, :, pl.ds(pl.multiple_of(tile * LANES, LANES), LANES)]
        moved = pltpu.roll(values, shift, 1)
        picked[probe % 4] = jnp.where(lane_probe == probe, moved, picked[probe % 4])
    total = (picked[0] + picked[1]) + (picked[2] + picked[3])
    predicted = total[:, :probes]
    predicted_ref[...] = predicted
    normal = (recorded_ref[...] - predicted) / sigma_ref[...]
    payload = jnp.concatenate([normal, normal + draws_ref[...]], axis=1)
    for device in range(payload_ref.shape[0]):
        payload_ref[device] = payload


def solve_kernel(norm_scale, slabs, offsets, place_ref, payload_ref, solved_ref):
    members, probes = payload_ref.shape[1], payload_ref.shape[2] // 2
    order = len(offsets) * members
    mine = place_ref[0]
    dims = (((1,), (1,)), ((), ()))
    gram, cross = None, None
    for slab in range(slabs):
        blocks = [
            payload_ref[jnp.bitwise_xor(mine, offset) * slabs + slab] for offset in offsets
        ]
        normal = jnp.concatenate([block[:, :probes] for block in blocks], axis=0)
        center = jnp.sum(normal, axis=0, keepdims=True) * (1.0 / order)
        scaled = (center - normal) * norm_scale
        misfit = jnp.concatenate([block[:, probes:] for block in blocks[:2]], axis=0)
        one = lax.dot_general(
            scaled, scaled, dims, precision=lax.Precision.HIGHEST, preferred_element_type=jnp.float32
        )
        two = lax.dot_general(
            misfit, scaled, dims, precision=lax.Precision.HIGHEST, preferred_element_type=jnp.float32
        )
        gram = one if gram is None else gram + one
        cross = two if cross is None else cross + two
    row_id = lax.broadcasted_iota(jnp.int32, (ROWS, order), 0)
    lane_id = lax.broadcasted_iota(jnp.int32, (ROWS, order), 1)
    blocks = order // ROWS
    tableau = [
        gram[k * ROWS : (k + 1) * ROWS, :]
        + jnp.where(lane_id == row_id + k * ROWS, damping, 0.0)
        for k in range(blocks)
    ]
    tableau += [cross[k : k + ROWS, :] for k in range(0, 2 * members, ROWS)]

    def lanes_of(value, at):
        return jnp.broadcast_to(value[:, at : at + 1], (ROWS, order))

    def row_of(value, at):
        return jnp.broadcast_to(value[at : at + 1, :], (ROWS, order))

    for block in range(blocks):
        base = block * ROWS
        inside = jnp.logical_and(lane_id >= base, lane_id < base + ROWS)
        band = tableau[block]
        column = [lanes_of(band, base + q) for q in range(ROWS)]
        band = jnp.where(inside, jnp.where(lane_id == row_id + base, -1.0, 0.0), band)
        for q in range(ROWS):
            here = row_id == q
            inverse = 1.0 / row_of(column[q], q)
            pivot_row = row_of(band, q) * inverse
            band = jnp.where(here, pivot_row, band - column[q] * pivot_row)
            for j in range(q + 1, ROWS):
                factor = row_of(column[j], q) * inverse
                column[j] = jnp.where(here, factor, column[j] - column[q] * factor)
        rows = [row_of(band, q) for q in range(ROWS)]
        for other in range(block + 1, len(tableau)):
            value = tableau[other]
            products = [lanes_of(value, base + q) * rows[q] for q in range(ROWS)]
            while len(products) > 1:
                products = [a + b for a, b in zip(products[::2], products[1::2])]
            tableau[other] = jnp.where(inside, 0.0, value) - products[0]
    solved_ref[...] = jnp.concatenate(tableau[blocks:], axis=0).astype(jnp.bfloat16)


def apply_kernel(norm_scale, lines, solved_ref, *refs):
    part_refs, own_ref, give_ref = refs[:-2], refs[-2], refs[-1]
    solved = solved_ref[...]
    pair, order = solved.shape
    wide = order * lines
    spread = (
        lax.broadcasted_iota(jnp.int32, (order, wide), 1) // lines
        == lax.broadcasted_iota(jnp.int32, (order, wide), 0)
    ).astype(jnp.bfloat16)
    stretched = jnp.dot(solved, spread, preferred_element_type=jnp.float32)
    on_line = lax.broadcasted_iota(jnp.int32, (lines, wide), 1) % lines == (
        lax.broadcasted_iota(jnp.int32, (lines, wide), 0)
    )
    weights = jnp.concatenate(
        [
            jnp.where(on_line, jnp.broadcast_to(stretched[j : j + 1, :], (lines, wide)), 0.0)
            for j in range(pair)
        ],
        axis=0,
    ).astype(jnp.bfloat16)
    change, start = None, 0
    for ref in part_refs:
        deep = ref.shape[0]
        part = jnp.dot(
            weights[:, start : start + deep], ref[...], preferred_element_type=jnp.float32
        )
        change = part if change is None else change + part
        start += deep
    change = change * norm_scale
    rows = own_ref.shape[0]
    own_ref[...] = change[:rows]
    give_ref[...] = change[rows:].astype(give_ref.dtype)


def merge_kernel(odd_ref, field_ref, own_ref, got_ref, out_ref):
    own, got = own_ref[...], got_ref[...].astype(jnp.float32)
    half = own.shape[1]
    even = odd_ref[0] == 0
    out_ref[:, :half] = field_ref[:, :half] + jnp.where(even, own, got)
    out_ref[:, half:] = field_ref[:, half:] + jnp.where(even, got, own)


def body(
    logarithmic_diffusivity,
    starting_warmth,
    thermal_supply,
    probe_positions,
    recorded_temps,
    probe_error_sigma,
    perturb_draws,
):
    members, lines, width = logarithmic_diffusivity.shape
    owners, slabs = lax.axis_size("mem"), lax.axis_size("sp")
    order = members * owners
    norm_scale = 1.0 / math.sqrt(order - 1)
    probes = probe_positions.shape[0]
    slab = lax.axis_index("sp")

    mine = lax.axis_index("mem").astype(jnp.int32)
    odd = mine & 1
    half = width // 2

    def across(value, bit):
        return lax.ppermute(value, "mem", [(i, i ^ bit) for i in range(owners)])

    field_flat = logarithmic_diffusivity.reshape(members * lines, width)
    field_round = field_flat.astype(jnp.bfloat16)
    left, right = field_round[:, :half], field_round[:, half:]
    held = jnp.where(odd == 0, left, right)
    parts = [held, across(jnp.where(odd == 0, right, left), 1)]
    offsets = [0, 1]
    bit = owners // 2

    def exchange(parts, offsets, bit):
        held = jnp.concatenate(parts, axis=0)
        return [held, across(held, bit)], offsets + [offset ^ bit for offset in offsets]

    if bit > 1:
        parts, offsets = exchange(parts, offsets, bit)
        bit //= 2

    edges = jnp.concatenate([field_flat, starting_warmth, thermal_supply], axis=0)
    if slabs == 2:
        up = down = lax.ppermute(edges, "sp", [(0, 1), (1, 0)])
    else:
        up = lax.ppermute(edges, "sp", [(i, i + 1) for i in range(slabs - 1)])
        down = lax.ppermute(edges, "sp", [(i + 1, i) for i in range(slabs - 1)])
    flags = jnp.stack([slab > 0, slab < slabs - 1]).astype(jnp.int32)
    vmem = pl.BlockSpec(memory_space=pltpu.VMEM)
    smem = pl.BlockSpec(memory_space=pltpu.SMEM)
    anywhere = pl.BlockSpec(memory_space=pl.ANY)
    window = lines + 2 * STEPS
    devices = owners * slabs
    predicted, payload = pl.pallas_call(
        conduct_kernel,
        out_shape=(
            jax.ShapeDtypeStruct((members, probes), jnp.float32),
            jax.ShapeDtypeStruct((devices, members, 2 * probes), jnp.float32),
        ),
        in_specs=[smem, anywhere] + [vmem] * 3 + [anywhere] * 5,
        out_specs=(vmem, vmem),
        scratch_shapes=[
            pltpu.VMEM((window, members, width), jnp.float32),
            pltpu.VMEM((window, members, width), jnp.float32),
            pltpu.VMEM((window, width), jnp.float32),
            pltpu.SMEM((probes,), jnp.int32),
            pltpu.VMEM((2 * lines, width), jnp.float32),
            pltpu.VMEM((1, probes), jnp.float32),
            pltpu.VMEM((1, probes), jnp.float32),
            pltpu.VMEM((members, probes), jnp.float32),
            pltpu.SemaphoreType.DMA((6,)),
        ],
        compiler_params=pltpu.CompilerParams(vmem_limit_bytes=24 * 1024 * 1024),
        cost_estimate=pl.CostEstimate(
            flops=30 * STEPS * window * members * width,
            bytes_accessed=4 * 3 * members * lines * width,
            transcendentals=STEPS * window * members * width,
        ),
        name="conduct",
    )(
        flags,
        probe_positions,
        field_flat,
        up,
        down,
        starting_warmth,
        thermal_supply,
        recorded_temps[None, :],
        probe_error_sigma[None, :],
        perturb_draws,
    )
    payload, *parts = lax.optimization_barrier((payload, *parts))
    while bit > 1:
        parts, offsets = exchange(parts, offsets, bit)
        bit //= 2
    everyone = lax.all_to_all(payload, ("mem", "sp"), 0, 0, tiled=True)
    if order <= LANES:
        solved = pl.pallas_call(
            lambda *refs: solve_kernel(norm_scale, slabs, offsets, *refs),
            out_shape=jax.ShapeDtypeStruct((2 * members, order), jnp.bfloat16),
            in_specs=[smem, vmem],
            out_specs=vmem,
            compiler_params=pltpu.CompilerParams(vmem_limit_bytes=16 * 1024 * 1024),
            cost_estimate=pl.CostEstimate(
                flops=2 * order * order * order,
                bytes_accessed=4 * devices * members * 2 * probes,
                transcendentals=0,
            ),
            name="solve",
        )(mine[None], everyone)
    else:
        owner = mine ^ jnp.array(offsets, jnp.int32)
        split = everyone.reshape(owners, slabs, members, 2, probes)[owner]
        split = split.transpose(3, 0, 2, 1, 4).reshape(2, order, slabs * probes)
        normal, misfit = split[0], split[1, : 2 * members]
        scaled = (jnp.mean(normal, axis=0, keepdims=True) - normal) * norm_scale
        gram_matrix = jnp.dot(
            scaled, scaled.T, precision=lax.Precision.HIGHEST, preferred_element_type=jnp.float32
        ) + damping * jnp.eye(order, dtype=jnp.float32)
        cross_term = jnp.dot(
            scaled, misfit.T, precision=lax.Precision.HIGHEST, preferred_element_type=jnp.float32
        )
        solved = eliminate(gram_matrix, cross_term).T.astype(jnp.bfloat16)
    own, give = pl.pallas_call(
        lambda *refs: apply_kernel(norm_scale, lines, *refs),
        out_shape=(
            jax.ShapeDtypeStruct((members * lines, half), jnp.float32),
            jax.ShapeDtypeStruct((members * lines, half), jnp.bfloat16),
        ),
        in_specs=[vmem] * (1 + len(parts)),
        out_specs=(vmem, vmem),
        compiler_params=pltpu.CompilerParams(vmem_limit_bytes=40 * 1024 * 1024),
        cost_estimate=pl.CostEstimate(
            flops=4 * members * lines * order * lines * half,
            bytes_accessed=2 * order * lines * half,
            transcendentals=0,
        ),
        name="apply",
    )(solved, *parts)
    got = across(give, 1)
    revised = pl.pallas_call(
        merge_kernel,
        out_shape=jax.ShapeDtypeStruct((members * lines, width), jnp.float32),
        in_specs=[smem] + [vmem] * 3,
        out_specs=vmem,
        compiler_params=pltpu.CompilerParams(vmem_limit_bytes=8 * 1024 * 1024),
        name="merge",
    )(odd[None], field_flat, own, got)
    return (revised.reshape(logarithmic_diffusivity.shape), predicted)


def solution(mesh):
    in_specs = (
        P("mem", "sp", None),
        P("sp", None),
        P("sp", None),
        P("sp"),
        P("sp"),
        P("sp"),
        P("mem", "sp"),
    )
    out_specs = (P("mem", "sp", None), P("mem", "sp"))
    return jax.shard_map(body, mesh=mesh, in_specs=in_specs, out_specs=out_specs, check_vma=False)
```

```python
import math

import jax
import jax.numpy as jnp
from jax import lax
from jax.experimental import pallas as pl
from jax.experimental.pallas import tpu as pltpu
from jax.sharding import PartitionSpec as P

STEPS = 4


time_step = 0.06
damping = 2.0
block_width = 16
LANES = 128
ROWS = 8


def invert_block(matrix):
    augmented = jnp.concatenate([matrix, jnp.eye(block_width, dtype=matrix.dtype)], axis=1)
    for place in range(block_width):
        pivot_row = augmented[place] / augmented[place, place]
        augmented = augmented - augmented[:, place : place + 1] * pivot_row[None, :]
        augmented = jnp.concatenate(
            [augmented[:place], pivot_row[None, :], augmented[place + 1 :]], axis=0
        )
    return augmented[:, block_width:]


def eliminate(gram_matrix, cross_term):
    order = gram_matrix.shape[0]
    tableau = jnp.concatenate([gram_matrix, cross_term], axis=1)

    def one_turn(block_number, tableau):
        first_row = (block_number * block_width).astype(jnp.int32)
        row_band = lax.dynamic_slice_in_dim(tableau, first_row, block_width, 0)
        pivot_block = lax.dynamic_slice_in_dim(row_band, first_row, block_width, 1)
        inverse = invert_block(pivot_block)
        scaled_rows = jnp.dot(
            inverse, row_band, precision=lax.Precision.HIGHEST, preferred_element_type=tableau.dtype
        )
        column = lax.dynamic_slice_in_dim(tableau, first_row, block_width, 1)
        tableau = tableau - jnp.dot(
            column,
            scaled_rows,
            precision=lax.Precision.HIGHEST,
            preferred_element_type=tableau.dtype,
        )
        return lax.dynamic_update_slice_in_dim(tableau, scaled_rows, first_row, 0)

    tableau = lax.fori_loop(0, order // block_width, one_turn, tableau)
    return tableau[:, order:]


def conduct_kernel(
    flags_ref,
    columns_hbm,
    field_ref,
    up_ref,
    down_ref,
    warmth_hbm,
    supply_hbm,
    recorded_hbm,
    sigma_hbm,
    draws_hbm,
    predicted_ref,
    payload_ref,
    warmth,
    half_exp,
    supply,
    columns_ref,
    small_ref,
    recorded_ref,
    sigma_ref,
    draws_ref,
    sems,
):
    lines = warmth_hbm.shape[0]
    copies = [
        pltpu.make_async_copy(source, target, sems.at[k])
        for k, (source, target) in enumerate(
            (
                (warmth_hbm, small_ref.at[pl.ds(0, lines)]),
                (supply_hbm, small_ref.at[pl.ds(lines, lines)]),
                (columns_hbm, columns_ref),
                (recorded_hbm, recorded_ref),
                (sigma_hbm, sigma_ref),
                (draws_hbm, draws_ref),
            )
        )
    ]
    for copy in copies:
        copy.start()
    members, width = predicted_ref.shape[0], small_ref.shape[1]
    tiles = width // LANES
    window = lines + 2 * STEPS
    lane = lax.broadcasted_iota(jnp.int32, (members, LANES), 1)
    first, last = lane == 0, lane == LANES - 1

    above, below = flags_ref[0] > 0, flags_ref[1] > 0
    sides = (
        (0, up_ref, lines - STEPS, STEPS, above),
        (STEPS, field_ref, 0, lines, None),
        (STEPS + lines, down_ref, 0, STEPS, below),
    )
    for row, ref, line, count, inside in sides:
        coefficient = jnp.swapaxes(
            ref[0 : members * lines, :].reshape(members, lines, width), 0, 1
        )
        for step in range(count):
            part = coefficient[line + step]
            if inside is not None:
                part = jnp.where(inside, part, 0.0)
            half_exp[row + step] = 0.5 * jnp.exp(part)
    copies[0].wait()
    copies[1].wait()
    for row, ref, line, count, inside in sides:
        small, base = (small_ref, 0) if inside is None else (ref, members * lines)
        for step in range(count):
            heat = small[pl.ds(base + line + step, 1), :]
            if inside is not None:
                heat = jnp.where(inside, heat, 0.0)
            warmth[row + step] = jnp.broadcast_to(heat, (members, width))
        supply[pl.ds(row, count), :] = small[pl.ds(base + lines + line, count), :]

    def cut(value):
        return [value[:, k * LANES : (k + 1) * LANES] for k in range(tiles)]

    def conductivity(row, warm):
        half = cut(half_exp[row])
        return [h * (1.0 + 0.5 * jnp.tanh(t)) for h, t in zip(half, warm)]

    half_one = jnp.full((members, LANES), 0.5, jnp.float32)
    zero = jnp.zeros((members, LANES), jnp.float32)

    for step in range(STEPS):
        low, high = step + 1, window - 1 - step
        t_up = cut(warmth[low - 1])
        c_up = conductivity(low - 1, t_up)
        t_here = cut(warmth[low])
        c_here = conductivity(low, t_here)
        flow_up = [(a + b) * (y - x) for a, b, x, y in zip(c_up, c_here, t_up, t_here)]

        def one_row(row, carry):
            t, c, up = carry
            t_next = cut(warmth[row + 1])
            c_next = conductivity(row + 1, t_next)
            down = [(a + b) * (y - x) for a, b, x, y in zip(c, c_next, t, t_next)]
            t_roll = [pltpu.roll(x, LANES - 1, 1) for x in t] + [zero]
            c_roll = [pltpu.roll(x, LANES - 1, 1) for x in c] + [half_one]
            right = []
            for k in range(tiles):
                t_right = jnp.where(last, t_roll[k + 1], t_roll[k])
                c_right = jnp.where(last, c_roll[k + 1], c_roll[k])
                right.append((c[k] + c_right) * (t_right - t[k]))
            back = [pltpu.roll(x, 1, 1) for x in right]
            outside = jnp.logical_or(
                jnp.logical_and(row < STEPS, flags_ref[0] <= 0),
                jnp.logical_and(row >= STEPS + lines, flags_ref[1] <= 0),
            )
            keep = jnp.where(outside, 0.0, 1.0)
            source = supply[pl.ds(row, 1), :]
            for k in range(tiles):
                edge = (c[0] + 0.5) * t[0] if k == 0 else back[k - 1]
                left = jnp.where(first, edge, back[k])
                inflow = (down[k] - up[k]) + (right[k] - left)
                heat = source[:, k * LANES : (k + 1) * LANES]
                warmth[row, :, k * LANES : (k + 1) * LANES] = keep * (
                    t[k] + time_step * (inflow + heat)
                )
            return t_next, c_next, down

        lax.fori_loop(low, high, one_row, (t_here, c_here, flow_up), unroll=True)

    for copy in copies[2:]:
        copy.wait()
    probes = predicted_ref.shape[1]
    lane_probe = lax.broadcasted_iota(jnp.int32, (members, LANES), 1)
    picked = [zero for _ in range(4)]
    for probe in range(probes):
        line = probe * lines // probes
        column = columns_ref[probe] - line * width
        tile = column // LANES
        shift = lax.rem(probe - lax.rem(column, LANES) + LANES, LANES)
        values = warmth[STEPS + line, :, pl.ds(pl.multiple_of(tile * LANES, LANES), LANES)]
        moved = pltpu.roll(values, shift, 1)
        picked[probe % 4] = jnp.where(lane_probe == probe, moved, picked[probe % 4])
    total = (picked[0] + picked[1]) + (picked[2] + picked[3])
    predicted = total[:, :probes]
    predicted_ref[...] = predicted
    normal = (recorded_ref[...] - predicted) / sigma_ref[...]
    payload = jnp.concatenate([normal, normal + draws_ref[...]], axis=1)
    for device in range(payload_ref.shape[0]):
        payload_ref[device] = payload


def solve_kernel(norm_scale, slabs, offsets, place_ref, payload_ref, solved_ref):
    members, probes = payload_ref.shape[1], payload_ref.shape[2] // 2
    order = len(offsets) * members
    mine = place_ref[0]
    dims = (((1,), (1,)), ((), ()))
    gram, cross = None, None
    for slab in range(slabs):
        blocks = [
            payload_ref[jnp.bitwise_xor(mine, offset) * slabs + slab] for offset in offsets
        ]
        normal = jnp.concatenate([block[:, :probes] for block in blocks], axis=0)
        center = jnp.sum(normal, axis=0, keepdims=True) * (1.0 / order)
        scaled = (center - normal) * norm_scale
        misfit = jnp.concatenate([block[:, probes:] for block in blocks[:2]], axis=0)
        one = lax.dot_general(
            scaled, scaled, dims, precision=lax.Precision.HIGHEST, preferred_element_type=jnp.float32
        )
        two = lax.dot_general(
            misfit, scaled, dims, precision=lax.Precision.HIGHEST, preferred_element_type=jnp.float32
        )
        gram = one if gram is None else gram + one
        cross = two if cross is None else cross + two
    row_id = lax.broadcasted_iota(jnp.int32, (ROWS, order), 0)
    lane_id = lax.broadcasted_iota(jnp.int32, (ROWS, order), 1)
    blocks = order // ROWS
    tableau = [
        gram[k * ROWS : (k + 1) * ROWS, :]
        + jnp.where(lane_id == row_id + k * ROWS, damping, 0.0)
        for k in range(blocks)
    ]
    tableau += [cross[k : k + ROWS, :] for k in range(0, 2 * members, ROWS)]

    def lanes_of(value, at):
        return jnp.broadcast_to(value[:, at : at + 1], (ROWS, order))

    def row_of(value, at):
        return jnp.broadcast_to(value[at : at + 1, :], (ROWS, order))

    for block in range(blocks):
        base = block * ROWS
        inside = jnp.logical_and(lane_id >= base, lane_id < base + ROWS)
        band = tableau[block]
        column = [lanes_of(band, base + q) for q in range(ROWS)]
        band = jnp.where(inside, jnp.where(lane_id == row_id + base, -1.0, 0.0), band)
        for q in range(ROWS):
            here = row_id == q
            inverse = 1.0 / row_of(column[q], q)
            pivot_row = row_of(band, q) * inverse
            band = jnp.where(here, pivot_row, band - column[q] * pivot_row)
            for j in range(q + 1, ROWS):
                factor = row_of(column[j], q) * inverse
                column[j] = jnp.where(here, factor, column[j] - column[q] * factor)
        rows = [row_of(band, q) for q in range(ROWS)]
        for other in range(block + 1, len(tableau)):
            value = tableau[other]
            products = [lanes_of(value, base + q) * rows[q] for q in range(ROWS)]
            while len(products) > 1:
                products = [a + b for a, b in zip(products[::2], products[1::2])]
            tableau[other] = jnp.where(inside, 0.0, value) - products[0]
    solved_ref[...] = jnp.concatenate(tableau[blocks:], axis=0).astype(jnp.bfloat16)


def apply_kernel(norm_scale, lines, solved_ref, *refs):
    part_refs, own_ref, give_ref = refs[:-2], refs[-2], refs[-1]
    solved = solved_ref[...]
    pair, order = solved.shape
    wide = order * lines
    spread = (
        lax.broadcasted_iota(jnp.int32, (order, wide), 1) // lines
        == lax.broadcasted_iota(jnp.int32, (order, wide), 0)
    ).astype(jnp.bfloat16)
    stretched = jnp.dot(solved, spread, preferred_element_type=jnp.float32)
    on_line = lax.broadcasted_iota(jnp.int32, (lines, wide), 1) % lines == (
        lax.broadcasted_iota(jnp.int32, (lines, wide), 0)
    )
    weights = jnp.concatenate(
        [
            jnp.where(on_line, jnp.broadcast_to(stretched[j : j + 1, :], (lines, wide)), 0.0)
            for j in range(pair)
        ],
        axis=0,
    ).astype(jnp.bfloat16)
    change, start = None, 0
    for ref in part_refs:
        deep = ref.shape[0]
        part = jnp.dot(
            weights[:, start : start + deep], ref[...], preferred_element_type=jnp.float32
        )
        change = part if change is None else change + part
        start += deep
    change = change * norm_scale
    rows = own_ref.shape[0]
    own_ref[...] = change[:rows]
    give_ref[...] = change[rows:].astype(give_ref.dtype)


def merge_kernel(odd_ref, field_ref, own_ref, got_ref, out_ref):
    own, got = own_ref[...], got_ref[...].astype(jnp.float32)
    half = own.shape[1]
    even = odd_ref[0] == 0
    out_ref[:, :half] = field_ref[:, :half] + jnp.where(even, own, got)
    out_ref[:, half:] = field_ref[:, half:] + jnp.where(even, got, own)


def body(
    logarithmic_diffusivity,
    starting_warmth,
    thermal_supply,
    probe_positions,
    recorded_temps,
    probe_error_sigma,
    perturb_draws,
):
    members, lines, width = logarithmic_diffusivity.shape
    owners, slabs = lax.axis_size("mem"), lax.axis_size("sp")
    order = members * owners
    norm_scale = 1.0 / math.sqrt(order - 1)
    probes = probe_positions.shape[0]
    slab = lax.axis_index("sp")

    mine = lax.axis_index("mem").astype(jnp.int32)
    odd = mine & 1
    half = width // 2

    def across(value, bit):
        return lax.ppermute(value, "mem", [(i, i ^ bit) for i in range(owners)])

    field_flat = logarithmic_diffusivity.reshape(members * lines, width)
    field_round = field_flat.astype(jnp.bfloat16)
    left, right = field_round[:, :half], field_round[:, half:]
    held = jnp.where(odd == 0, left, right)
    parts = [held, across(jnp.where(odd == 0, right, left), 1)]
    offsets = [0, 1]
    bit = owners // 2

    def exchange(parts, offsets, bit):
        held = jnp.concatenate(parts, axis=0)
        return [held, across(held, bit)], offsets + [offset ^ bit for offset in offsets]

    if bit > 1:
        parts, offsets = exchange(parts, offsets, bit)
        bit //= 2

    edges = jnp.concatenate([field_flat, starting_warmth, thermal_supply], axis=0)
    if slabs == 2:
        up = down = lax.ppermute(edges, "sp", [(0, 1), (1, 0)])
    else:
        up = lax.ppermute(edges, "sp", [(i, i + 1) for i in range(slabs - 1)])
        down = lax.ppermute(edges, "sp", [(i + 1, i) for i in range(slabs - 1)])
    flags = jnp.stack([slab > 0, slab < slabs - 1]).astype(jnp.int32)
    vmem = pl.BlockSpec(memory_space=pltpu.VMEM)
    smem = pl.BlockSpec(memory_space=pltpu.SMEM)
    anywhere = pl.BlockSpec(memory_space=pl.ANY)
    window = lines + 2 * STEPS
    devices = owners * slabs
    predicted, payload = pl.pallas_call(
        conduct_kernel,
        out_shape=(
            jax.ShapeDtypeStruct((members, probes), jnp.float32),
            jax.ShapeDtypeStruct((devices, members, 2 * probes), jnp.float32),
        ),
        in_specs=[smem, anywhere] + [vmem] * 3 + [anywhere] * 5,
        out_specs=(vmem, vmem),
        scratch_shapes=[
            pltpu.VMEM((window, members, width), jnp.float32),
            pltpu.VMEM((window, members, width), jnp.float32),
            pltpu.VMEM((window, width), jnp.float32),
            pltpu.SMEM((probes,), jnp.int32),
            pltpu.VMEM((2 * lines, width), jnp.float32),
            pltpu.VMEM((1, probes), jnp.float32),
            pltpu.VMEM((1, probes), jnp.float32),
            pltpu.VMEM((members, probes), jnp.float32),
            pltpu.SemaphoreType.DMA((6,)),
        ],
        compiler_params=pltpu.CompilerParams(vmem_limit_bytes=24 * 1024 * 1024),
        cost_estimate=pl.CostEstimate(
            flops=30 * STEPS * window * members * width,
            bytes_accessed=4 * 3 * members * lines * width,
            transcendentals=STEPS * window * members * width,
        ),
        name="conduct",
    )(
        flags,
        probe_positions,
        field_flat,
        up,
        down,
        starting_warmth,
        thermal_supply,
        recorded_temps[None, :],
        probe_error_sigma[None, :],
        perturb_draws,
    )
    payload, *parts = lax.optimization_barrier((payload, *parts))
    while bit > 4:
        parts, offsets = exchange(parts, offsets, bit)
        bit //= 2
    if bit == 4:
        held = jnp.concatenate(parts, axis=0)
        parts = [held, across(held, 4), across(held, 2)]
    everyone = lax.all_to_all(payload, ("mem", "sp"), 0, 0, tiled=True)
    if bit == 4:
        everyone, passed = lax.optimization_barrier((everyone, parts[1]))
        parts.append(across(passed, 2))
        offsets = [offset ^ turn for turn in (0, 4, 2, 6) for offset in offsets]
    elif bit == 2:
        parts, offsets = exchange(parts, offsets, bit)
    if order <= LANES:
        solved = pl.pallas_call(
            lambda *refs: solve_kernel(norm_scale, slabs, offsets, *refs),
            out_shape=jax.ShapeDtypeStruct((2 * members, order), jnp.bfloat16),
            in_specs=[smem, vmem],
            out_specs=vmem,
            compiler_params=pltpu.CompilerParams(vmem_limit_bytes=16 * 1024 * 1024),
            cost_estimate=pl.CostEstimate(
                flops=2 * order * order * order,
                bytes_accessed=4 * devices * members * 2 * probes,
                transcendentals=0,
            ),
            name="solve",
        )(mine[None], everyone)
    else:
        owner = mine ^ jnp.array(offsets, jnp.int32)
        split = everyone.reshape(owners, slabs, members, 2, probes)[owner]
        split = split.transpose(3, 0, 2, 1, 4).reshape(2, order, slabs * probes)
        normal, misfit = split[0], split[1, : 2 * members]
        scaled = (jnp.mean(normal, axis=0, keepdims=True) - normal) * norm_scale
        gram_matrix = jnp.dot(
            scaled, scaled.T, precision=lax.Precision.HIGHEST, preferred_element_type=jnp.float32
        ) + damping * jnp.eye(order, dtype=jnp.float32)
        cross_term = jnp.dot(
            scaled, misfit.T, precision=lax.Precision.HIGHEST, preferred_element_type=jnp.float32
        )
        solved = eliminate(gram_matrix, cross_term).T.astype(jnp.bfloat16)
    own, give = pl.pallas_call(
        lambda *refs: apply_kernel(norm_scale, lines, *refs),
        out_shape=(
            jax.ShapeDtypeStruct((members * lines, half), jnp.float32),
            jax.ShapeDtypeStruct((members * lines, half), jnp.bfloat16),
        ),
        in_specs=[vmem] * (1 + len(parts)),
        out_specs=(vmem, vmem),
        compiler_params=pltpu.CompilerParams(vmem_limit_bytes=40 * 1024 * 1024),
        cost_estimate=pl.CostEstimate(
            flops=4 * members * lines * order * lines * half,
            bytes_accessed=2 * order * lines * half,
            transcendentals=0,
        ),
        name="apply",
    )(solved, *parts)
    got = across(give, 1)
    revised = pl.pallas_call(
        merge_kernel,
        out_shape=jax.ShapeDtypeStruct((members * lines, width), jnp.float32),
        in_specs=[smem] + [vmem] * 3,
        out_specs=vmem,
        compiler_params=pltpu.CompilerParams(vmem_limit_bytes=8 * 1024 * 1024),
        name="merge",
    )(odd[None], field_flat, own, got)
    return (revised.reshape(logarithmic_diffusivity.shape), predicted)


def solution(mesh):
    in_specs = (
        P("mem", "sp", None),
        P("sp", None),
        P("sp", None),
        P("sp"),
        P("sp"),
        P("sp"),
        P("mem", "sp"),
    )
    out_specs = (P("mem", "sp", None), P("mem", "sp"))
    return jax.shard_map(body, mesh=mesh, in_specs=in_specs, out_specs=out_specs, check_vma=False)
```

```python
import math

import jax
import jax.numpy as jnp
from jax import lax
from jax.experimental import pallas as pl
from jax.experimental.pallas import tpu as pltpu
from jax.sharding import PartitionSpec as P

STEPS = 4


time_step = 0.06
damping = 2.0
block_width = 16
LANES = 128
ROWS = 8


def invert_block(matrix):
    augmented = jnp.concatenate([matrix, jnp.eye(block_width, dtype=matrix.dtype)], axis=1)
    for place in range(block_width):
        pivot_row = augmented[place] / augmented[place, place]
        augmented = augmented - augmented[:, place : place + 1] * pivot_row[None, :]
        augmented = jnp.concatenate(
            [augmented[:place], pivot_row[None, :], augmented[place + 1 :]], axis=0
        )
    return augmented[:, block_width:]


def eliminate(gram_matrix, cross_term):
    order = gram_matrix.shape[0]
    tableau = jnp.concatenate([gram_matrix, cross_term], axis=1)

    def one_turn(block_number, tableau):
        first_row = (block_number * block_width).astype(jnp.int32)
        row_band = lax.dynamic_slice_in_dim(tableau, first_row, block_width, 0)
        pivot_block = lax.dynamic_slice_in_dim(row_band, first_row, block_width, 1)
        inverse = invert_block(pivot_block)
        scaled_rows = jnp.dot(
            inverse, row_band, precision=lax.Precision.HIGHEST, preferred_element_type=tableau.dtype
        )
        column = lax.dynamic_slice_in_dim(tableau, first_row, block_width, 1)
        tableau = tableau - jnp.dot(
            column,
            scaled_rows,
            precision=lax.Precision.HIGHEST,
            preferred_element_type=tableau.dtype,
        )
        return lax.dynamic_update_slice_in_dim(tableau, scaled_rows, first_row, 0)

    tableau = lax.fori_loop(0, order // block_width, one_turn, tableau)
    return tableau[:, order:]


def conduct_kernel(
    flags_ref,
    columns_hbm,
    field_ref,
    up_ref,
    down_ref,
    warmth_hbm,
    supply_hbm,
    recorded_hbm,
    sigma_hbm,
    draws_hbm,
    predicted_ref,
    payload_ref,
    warmth,
    half_exp,
    supply,
    columns_ref,
    small_ref,
    recorded_ref,
    sigma_ref,
    draws_ref,
    sems,
):
    lines = warmth_hbm.shape[0]
    copies = [
        pltpu.make_async_copy(source, target, sems.at[k])
        for k, (source, target) in enumerate(
            (
                (warmth_hbm, small_ref.at[pl.ds(0, lines)]),
                (supply_hbm, small_ref.at[pl.ds(lines, lines)]),
                (columns_hbm, columns_ref),
                (recorded_hbm, recorded_ref),
                (sigma_hbm, sigma_ref),
                (draws_hbm, draws_ref),
            )
        )
    ]
    for copy in copies:
        copy.start()
    members, width = predicted_ref.shape[0], small_ref.shape[1]
    tiles = width // LANES
    window = lines + 2 * STEPS
    lane = lax.broadcasted_iota(jnp.int32, (members, LANES), 1)
    first, last = lane == 0, lane == LANES - 1

    above, below = flags_ref[0] > 0, flags_ref[1] > 0
    sides = (
        (0, up_ref, lines - STEPS, STEPS, above),
        (STEPS, field_ref, 0, lines, None),
        (STEPS + lines, down_ref, 0, STEPS, below),
    )
    for row, ref, line, count, inside in sides:
        coefficient = jnp.swapaxes(
            ref[0 : members * lines, :].reshape(members, lines, width), 0, 1
        )
        for step in range(count):
            part = coefficient[line + step]
            if inside is not None:
                part = jnp.where(inside, part, 0.0)
            half_exp[row + step] = 0.5 * jnp.exp(part)
    copies[0].wait()
    copies[1].wait()
    for row, ref, line, count, inside in sides:
        small, base = (small_ref, 0) if inside is None else (ref, members * lines)
        for step in range(count):
            heat = small[pl.ds(base + line + step, 1), :]
            if inside is not None:
                heat = jnp.where(inside, heat, 0.0)
            warmth[row + step] = jnp.broadcast_to(heat, (members, width))
        supply[pl.ds(row, count), :] = small[pl.ds(base + lines + line, count), :]

    def cut(value):
        return [value[:, k * LANES : (k + 1) * LANES] for k in range(tiles)]

    def conductivity(row, warm):
        half = cut(half_exp[row])
        return [h * (1.0 + 0.5 * jnp.tanh(t)) for h, t in zip(half, warm)]

    half_one = jnp.full((members, LANES), 0.5, jnp.float32)
    zero = jnp.zeros((members, LANES), jnp.float32)

    for step in range(STEPS):
        low, high = step + 1, window - 1 - step
        t_up = cut(warmth[low - 1])
        c_up = conductivity(low - 1, t_up)
        t_here = cut(warmth[low])
        c_here = conductivity(low, t_here)
        flow_up = [(a + b) * (y - x) for a, b, x, y in zip(c_up, c_here, t_up, t_here)]

        def one_row(row, carry):
            t, c, up = carry
            t_next = cut(warmth[row + 1])
            c_next = conductivity(row + 1, t_next)
            down = [(a + b) * (y - x) for a, b, x, y in zip(c, c_next, t, t_next)]
            t_roll = [pltpu.roll(x, LANES - 1, 1) for x in t] + [zero]
            c_roll = [pltpu.roll(x, LANES - 1, 1) for x in c] + [half_one]
            right = []
            for k in range(tiles):
                t_right = jnp.where(last, t_roll[k + 1], t_roll[k])
                c_right = jnp.where(last, c_roll[k + 1], c_roll[k])
                right.append((c[k] + c_right) * (t_right - t[k]))
            back = [pltpu.roll(x, 1, 1) for x in right]
            outside = jnp.logical_or(
                jnp.logical_and(row < STEPS, flags_ref[0] <= 0),
                jnp.logical_and(row >= STEPS + lines, flags_ref[1] <= 0),
            )
            keep = jnp.where(outside, 0.0, 1.0)
            source = supply[pl.ds(row, 1), :]
            for k in range(tiles):
                edge = (c[0] + 0.5) * t[0] if k == 0 else back[k - 1]
                left = jnp.where(first, edge, back[k])
                inflow = (down[k] - up[k]) + (right[k] - left)
                heat = source[:, k * LANES : (k + 1) * LANES]
                warmth[row, :, k * LANES : (k + 1) * LANES] = keep * (
                    t[k] + time_step * (inflow + heat)
                )
            return t_next, c_next, down

        lax.fori_loop(low, high, one_row, (t_here, c_here, flow_up), unroll=True)

    for copy in copies[2:]:
        copy.wait()
    probes = predicted_ref.shape[1]
    lane_probe = lax.broadcasted_iota(jnp.int32, (members, LANES), 1)
    picked = [zero for _ in range(4)]
    for probe in range(probes):
        line = probe * lines // probes
        column = columns_ref[probe] - line * width
        tile = column // LANES
        shift = lax.rem(probe - lax.rem(column, LANES) + LANES, LANES)
        values = warmth[STEPS + line, :, pl.ds(pl.multiple_of(tile * LANES, LANES), LANES)]
        moved = pltpu.roll(values, shift, 1)
        picked[probe % 4] = jnp.where(lane_probe == probe, moved, picked[probe % 4])
    total = (picked[0] + picked[1]) + (picked[2] + picked[3])
    predicted = total[:, :probes]
    predicted_ref[...] = predicted
    normal = (recorded_ref[...] - predicted) / sigma_ref[...]
    payload = jnp.concatenate([normal, normal + draws_ref[...]], axis=1)
    for device in range(payload_ref.shape[0]):
        payload_ref[device] = payload


def solve_kernel(norm_scale, slabs, offsets, turns, place_ref, payload_ref, solved_ref):
    members, probes = payload_ref.shape[1], payload_ref.shape[2] // 2
    order = len(offsets) * members
    mine = place_ref[0]
    dims = (((1,), (1,)), ((), ()))
    gram, cross = None, None
    for slab in range(slabs):
        blocks = [
            payload_ref[jnp.bitwise_xor(mine, offset) * slabs + slab] for offset in offsets
        ]
        normal = jnp.concatenate([block[:, :probes] for block in blocks], axis=0)
        center = jnp.sum(normal, axis=0, keepdims=True) * (1.0 / order)
        scaled = (center - normal) * norm_scale
        misfit = jnp.concatenate(
            [blocks[offsets.index(turn)][:, probes:] for turn in turns], axis=0
        )
        one = lax.dot_general(
            scaled, scaled, dims, precision=lax.Precision.HIGHEST, preferred_element_type=jnp.float32
        )
        two = lax.dot_general(
            misfit, scaled, dims, precision=lax.Precision.HIGHEST, preferred_element_type=jnp.float32
        )
        gram = one if gram is None else gram + one
        cross = two if cross is None else cross + two
    row_id = lax.broadcasted_iota(jnp.int32, (ROWS, order), 0)
    lane_id = lax.broadcasted_iota(jnp.int32, (ROWS, order), 1)
    blocks = order // ROWS
    tableau = [
        gram[k * ROWS : (k + 1) * ROWS, :]
        + jnp.where(lane_id == row_id + k * ROWS, damping, 0.0)
        for k in range(blocks)
    ]
    tableau += [cross[k : k + ROWS, :] for k in range(0, len(turns) * members, ROWS)]

    def lanes_of(value, at):
        return jnp.broadcast_to(value[:, at : at + 1], (ROWS, order))

    def row_of(value, at):
        return jnp.broadcast_to(value[at : at + 1, :], (ROWS, order))

    for block in range(blocks):
        base = block * ROWS
        inside = jnp.logical_and(lane_id >= base, lane_id < base + ROWS)
        band = tableau[block]
        column = [lanes_of(band, base + q) for q in range(ROWS)]
        band = jnp.where(inside, jnp.where(lane_id == row_id + base, -1.0, 0.0), band)
        for q in range(ROWS):
            here = row_id == q
            inverse = 1.0 / row_of(column[q], q)
            pivot_row = row_of(band, q) * inverse
            band = jnp.where(here, pivot_row, band - column[q] * pivot_row)
            for j in range(q + 1, ROWS):
                factor = row_of(column[j], q) * inverse
                column[j] = jnp.where(here, factor, column[j] - column[q] * factor)
        rows = [row_of(band, q) for q in range(ROWS)]
        for other in range(block + 1, len(tableau)):
            value = tableau[other]
            products = [lanes_of(value, base + q) * rows[q] for q in range(ROWS)]
            while len(products) > 1:
                products = [a + b for a, b in zip(products[::2], products[1::2])]
            tableau[other] = jnp.where(inside, 0.0, value) - products[0]
    solved_ref[...] = jnp.concatenate(tableau[blocks:], axis=0).astype(jnp.bfloat16)


def apply_kernel(norm_scale, lines, solved_ref, *refs):
    outs = refs[len(refs) // 2 :]
    part_refs = refs[: len(refs) // 2]
    solved = solved_ref[...]
    pair, order = solved.shape
    wide = order * lines
    spread = (
        lax.broadcasted_iota(jnp.int32, (order, wide), 1) // lines
        == lax.broadcasted_iota(jnp.int32, (order, wide), 0)
    ).astype(jnp.bfloat16)
    stretched = jnp.dot(solved, spread, preferred_element_type=jnp.float32)
    on_line = lax.broadcasted_iota(jnp.int32, (lines, wide), 1) % lines == (
        lax.broadcasted_iota(jnp.int32, (lines, wide), 0)
    )
    weights = jnp.concatenate(
        [
            jnp.where(on_line, jnp.broadcast_to(stretched[j : j + 1, :], (lines, wide)), 0.0)
            for j in range(pair)
        ],
        axis=0,
    ).astype(jnp.bfloat16)
    change, start = None, 0
    for ref in part_refs:
        deep = ref.shape[0]
        part = jnp.dot(
            weights[:, start : start + deep], ref[...], preferred_element_type=jnp.float32
        )
        change = part if change is None else change + part
        start += deep
    change = change * norm_scale
    rows = outs[0].shape[0]
    for turn, ref in enumerate(outs):
        ref[...] = change[turn * rows : (turn + 1) * rows].astype(ref.dtype)


def merge_kernel(place_ref, field_ref, *refs):
    pieces, out_ref = refs[:-1], refs[-1]
    share = pieces[0].shape[1]
    mine = jnp.bitwise_and(place_ref[0], len(pieces) - 1)
    for turn, piece in enumerate(pieces):
        start = pl.multiple_of(jnp.bitwise_xor(mine, turn) * share, LANES)
        columns = pl.ds(start, share)
        out_ref[:, columns] = field_ref[:, columns] + piece[...].astype(jnp.float32)


def body(
    logarithmic_diffusivity,
    starting_warmth,
    thermal_supply,
    probe_positions,
    recorded_temps,
    probe_error_sigma,
    perturb_draws,
):
    members, lines, width = logarithmic_diffusivity.shape
    owners, slabs = lax.axis_size("mem"), lax.axis_size("sp")
    order = members * owners
    norm_scale = 1.0 / math.sqrt(order - 1)
    probes = probe_positions.shape[0]
    slab = lax.axis_index("sp")

    mine = lax.axis_index("mem").astype(jnp.int32)
    turns = range(math.gcd(owners, 4))
    share = width // len(turns)

    def across(value, bit):
        return lax.ppermute(value, "mem", [(i, i ^ bit) for i in range(owners)])

    field_flat = logarithmic_diffusivity.reshape(members * lines, width)
    field_round = field_flat.astype(jnp.bfloat16)
    parts, offsets = [field_round], [0]
    bits = []
    while len(turns) << len(bits) < owners:
        bits.insert(0, len(turns) << len(bits))

    def exchange(parts, offsets, bit):
        held = jnp.concatenate(parts, axis=0)
        return [held, across(held, bit)], offsets + [offset ^ bit for offset in offsets]

    for bit in bits[:1]:
        parts, offsets = exchange(parts, offsets, bit)

    edges = jnp.concatenate([field_flat, starting_warmth, thermal_supply], axis=0)
    if slabs == 2:
        up = down = lax.ppermute(edges, "sp", [(0, 1), (1, 0)])
    else:
        up = lax.ppermute(edges, "sp", [(i, i + 1) for i in range(slabs - 1)])
        down = lax.ppermute(edges, "sp", [(i + 1, i) for i in range(slabs - 1)])
    flags = jnp.stack([slab > 0, slab < slabs - 1]).astype(jnp.int32)
    vmem = pl.BlockSpec(memory_space=pltpu.VMEM)
    smem = pl.BlockSpec(memory_space=pltpu.SMEM)
    anywhere = pl.BlockSpec(memory_space=pl.ANY)
    window = lines + 2 * STEPS
    devices = owners * slabs
    predicted, payload = pl.pallas_call(
        conduct_kernel,
        out_shape=(
            jax.ShapeDtypeStruct((members, probes), jnp.float32),
            jax.ShapeDtypeStruct((devices, members, 2 * probes), jnp.float32),
        ),
        in_specs=[smem, anywhere] + [vmem] * 3 + [anywhere] * 5,
        out_specs=(vmem, vmem),
        scratch_shapes=[
            pltpu.VMEM((window, members, width), jnp.float32),
            pltpu.VMEM((window, members, width), jnp.float32),
            pltpu.VMEM((window, width), jnp.float32),
            pltpu.SMEM((probes,), jnp.int32),
            pltpu.VMEM((2 * lines, width), jnp.float32),
            pltpu.VMEM((1, probes), jnp.float32),
            pltpu.VMEM((1, probes), jnp.float32),
            pltpu.VMEM((members, probes), jnp.float32),
            pltpu.SemaphoreType.DMA((6,)),
        ],
        compiler_params=pltpu.CompilerParams(vmem_limit_bytes=24 * 1024 * 1024),
        cost_estimate=pl.CostEstimate(
            flops=30 * STEPS * window * members * width,
            bytes_accessed=4 * 3 * members * lines * width,
            transcendentals=STEPS * window * members * width,
        ),
        name="conduct",
    )(
        flags,
        probe_positions,
        field_flat,
        up,
        down,
        starting_warmth,
        thermal_supply,
        recorded_temps[None, :],
        probe_error_sigma[None, :],
        perturb_draws,
    )
    payload, *parts = lax.optimization_barrier((payload, *parts))
    for bit in bits[1:]:
        parts, offsets = exchange(parts, offsets, bit)
    everyone = lax.all_to_all(payload, ("mem", "sp"), 0, 0, tiled=True)
    everyone, *parts = lax.optimization_barrier((everyone, *parts))
    held = jnp.concatenate(parts, axis=0)
    parts = []
    for turn in turns:
        columns = ((mine ^ turn) & (len(turns) - 1)) * share
        piece = lax.dynamic_slice_in_dim(held, columns, share, 1)
        parts.append(across(piece, turn) if turn else piece)
    offsets = [offset ^ turn for turn in turns for offset in offsets]
    if order <= LANES:
        solved = pl.pallas_call(
            lambda *refs: solve_kernel(norm_scale, slabs, offsets, turns, *refs),
            out_shape=jax.ShapeDtypeStruct((len(turns) * members, order), jnp.bfloat16),
            in_specs=[smem, vmem],
            out_specs=vmem,
            compiler_params=pltpu.CompilerParams(vmem_limit_bytes=16 * 1024 * 1024),
            cost_estimate=pl.CostEstimate(
                flops=2 * order * order * order,
                bytes_accessed=4 * devices * members * 2 * probes,
                transcendentals=0,
            ),
            name="solve",
        )(mine[None], everyone)
    else:
        owner = mine ^ jnp.array(offsets, jnp.int32)
        split = everyone.reshape(owners, slabs, members, 2, probes)[owner]
        split = split.transpose(3, 0, 2, 1, 4).reshape(2, order, slabs * probes)
        normal = split[0]
        misfit = split[1].reshape(owners, members, -1)
        misfit = jnp.concatenate([misfit[offsets.index(turn)] for turn in turns], axis=0)
        scaled = (jnp.mean(normal, axis=0, keepdims=True) - normal) * norm_scale
        gram_matrix = jnp.dot(
            scaled, scaled.T, precision=lax.Precision.HIGHEST, preferred_element_type=jnp.float32
        ) + damping * jnp.eye(order, dtype=jnp.float32)
        cross_term = jnp.dot(
            scaled, misfit.T, precision=lax.Precision.HIGHEST, preferred_element_type=jnp.float32
        )
        solved = eliminate(gram_matrix, cross_term).T.astype(jnp.bfloat16)
    rows = members * lines
    pieces = pl.pallas_call(
        lambda *refs: apply_kernel(norm_scale, lines, *refs),
        out_shape=[
            jax.ShapeDtypeStruct((rows, share), jnp.bfloat16 if turn else jnp.float32)
            for turn in turns
        ],
        in_specs=[vmem] * (1 + len(parts)),
        out_specs=[vmem] * len(turns),
        compiler_params=pltpu.CompilerParams(vmem_limit_bytes=40 * 1024 * 1024),
        cost_estimate=pl.CostEstimate(
            flops=2 * rows * order * lines * width,
            bytes_accessed=2 * order * lines * share,
            transcendentals=0,
        ),
        name="apply",
    )(solved, *parts)
    pieces = [across(piece, turn) if turn else piece for turn, piece in zip(turns, pieces)]
    revised = pl.pallas_call(
        merge_kernel,
        out_shape=jax.ShapeDtypeStruct((rows, width), jnp.float32),
        in_specs=[smem] + [vmem] * (1 + len(turns)),
        out_specs=vmem,
        compiler_params=pltpu.CompilerParams(vmem_limit_bytes=8 * 1024 * 1024),
        name="merge",
    )(mine[None], field_flat, *pieces)
    return (revised.reshape(logarithmic_diffusivity.shape), predicted)


def solution(mesh):
    in_specs = (
        P("mem", "sp", None),
        P("sp", None),
        P("sp", None),
        P("sp"),
        P("sp"),
        P("sp"),
        P("mem", "sp"),
    )
    out_specs = (P("mem", "sp", None), P("mem", "sp"))
    return jax.shard_map(body, mesh=mesh, in_specs=in_specs, out_specs=out_specs, check_vma=False)
```

```python
import math

import jax
import jax.numpy as jnp
from jax import lax
from jax.experimental import pallas as pl
from jax.experimental.pallas import tpu as pltpu
from jax.sharding import PartitionSpec as P

STEPS = 4


time_step = 0.06
damping = 2.0
block_width = 16
LANES = 128
ROWS = 8


def invert_block(matrix):
    augmented = jnp.concatenate([matrix, jnp.eye(block_width, dtype=matrix.dtype)], axis=1)
    for place in range(block_width):
        pivot_row = augmented[place] / augmented[place, place]
        augmented = augmented - augmented[:, place : place + 1] * pivot_row[None, :]
        augmented = jnp.concatenate(
            [augmented[:place], pivot_row[None, :], augmented[place + 1 :]], axis=0
        )
    return augmented[:, block_width:]


def eliminate(gram_matrix, cross_term):
    order = gram_matrix.shape[0]
    tableau = jnp.concatenate([gram_matrix, cross_term], axis=1)

    def one_turn(block_number, tableau):
        first_row = (block_number * block_width).astype(jnp.int32)
        row_band = lax.dynamic_slice_in_dim(tableau, first_row, block_width, 0)
        pivot_block = lax.dynamic_slice_in_dim(row_band, first_row, block_width, 1)
        inverse = invert_block(pivot_block)
        scaled_rows = jnp.dot(
            inverse, row_band, precision=lax.Precision.HIGHEST, preferred_element_type=tableau.dtype
        )
        column = lax.dynamic_slice_in_dim(tableau, first_row, block_width, 1)
        tableau = tableau - jnp.dot(
            column,
            scaled_rows,
            precision=lax.Precision.HIGHEST,
            preferred_element_type=tableau.dtype,
        )
        return lax.dynamic_update_slice_in_dim(tableau, scaled_rows, first_row, 0)

    tableau = lax.fori_loop(0, order // block_width, one_turn, tableau)
    return tableau[:, order:]


def conduct_kernel(
    flags_ref,
    columns_hbm,
    field_ref,
    up_ref,
    down_ref,
    start_ref,
    source_ref,
    recorded_hbm,
    sigma_hbm,
    draws_hbm,
    predicted_ref,
    payload_ref,
    warmth,
    half_exp,
    supply,
    columns_ref,
    recorded_ref,
    sigma_ref,
    draws_ref,
    sems,
):
    lines = start_ref.shape[0]
    copies = [
        pltpu.make_async_copy(source, target, sems.at[k])
        for k, (source, target) in enumerate(
            (
                (columns_hbm, columns_ref),
                (recorded_hbm, recorded_ref),
                (sigma_hbm, sigma_ref),
                (draws_hbm, draws_ref),
            )
        )
    ]
    for copy in copies:
        copy.start()
    members, width = predicted_ref.shape[0], start_ref.shape[1]
    tiles = width // LANES
    window = lines + 2 * STEPS
    lane = lax.broadcasted_iota(jnp.int32, (members, LANES), 1)
    first, last = lane == 0, lane == LANES - 1

    above, below = flags_ref[0] > 0, flags_ref[1] > 0
    sides = (
        (0, up_ref, lines - STEPS, STEPS, above),
        (STEPS, field_ref, 0, lines, None),
        (STEPS + lines, down_ref, 0, STEPS, below),
    )
    def by_rows(ref):
        return jnp.swapaxes(ref[0 : members * lines, :].reshape(members, lines, width), 0, 1)

    turned = {id(ref): by_rows(ref) for ref in (field_ref, up_ref, down_ref)}
    for row, ref, line, count, inside in sides:
        coefficient = turned[id(ref)]
        for step in range(count):
            part = coefficient[line + step]
            if inside is not None:
                part = jnp.where(inside, part, 0.0)
            half_exp[row + step] = 0.5 * jnp.exp(part)
    for row, ref, line, count, inside in sides:
        for step in range(count):
            if inside is None:
                heat = start_ref[pl.ds(line + step, 1), :]
            else:
                heat = jnp.where(inside, ref[pl.ds(members * lines + line + step, 1), :], 0.0)
            warmth[row + step] = jnp.broadcast_to(heat, (members, width))
        if inside is None:
            supply[pl.ds(row, count), :] = source_ref[...]
        else:
            base = (members + 1) * lines + line
            supply[pl.ds(row, count), :] = ref[pl.ds(base, count), :]

    def cut(value):
        return [value[:, k * LANES : (k + 1) * LANES] for k in range(tiles)]

    def conductivity(row, warm):
        half = cut(half_exp[row])
        return [h * (1.0 + 0.5 * jnp.tanh(t)) for h, t in zip(half, warm)]

    half_one = jnp.full((members, LANES), 0.5, jnp.float32)
    zero = jnp.zeros((members, LANES), jnp.float32)

    for step in range(STEPS):
        low, high = step + 1, window - 1 - step
        t_up = cut(warmth[low - 1])
        c_up = conductivity(low - 1, t_up)
        t_here = cut(warmth[low])
        c_here = conductivity(low, t_here)
        flow_up = [(a + b) * (y - x) for a, b, x, y in zip(c_up, c_here, t_up, t_here)]

        def one_row(row, carry):
            t, c, up = carry
            t_next = cut(warmth[row + 1])
            c_next = conductivity(row + 1, t_next)
            down = [(a + b) * (y - x) for a, b, x, y in zip(c, c_next, t, t_next)]
            t_roll = [pltpu.roll(x, LANES - 1, 1) for x in t] + [zero]
            c_roll = [pltpu.roll(x, LANES - 1, 1) for x in c] + [half_one]
            right = []
            for k in range(tiles):
                t_right = jnp.where(last, t_roll[k + 1], t_roll[k])
                c_right = jnp.where(last, c_roll[k + 1], c_roll[k])
                right.append((c[k] + c_right) * (t_right - t[k]))
            back = [pltpu.roll(x, 1, 1) for x in right]
            outside = jnp.logical_or(
                jnp.logical_and(row < STEPS, flags_ref[0] <= 0),
                jnp.logical_and(row >= STEPS + lines, flags_ref[1] <= 0),
            )
            keep = jnp.where(outside, 0.0, 1.0)
            source = supply[pl.ds(row, 1), :]
            for k in range(tiles):
                edge = (c[0] + 0.5) * t[0] if k == 0 else back[k - 1]
                left = jnp.where(first, edge, back[k])
                inflow = (down[k] - up[k]) + (right[k] - left)
                heat = source[:, k * LANES : (k + 1) * LANES]
                warmth[row, :, k * LANES : (k + 1) * LANES] = keep * (
                    t[k] + time_step * (inflow + heat)
                )
            return t_next, c_next, down

        lax.fori_loop(low, high, one_row, (t_here, c_here, flow_up), unroll=True)

    for copy in copies:
        copy.wait()
    probes = predicted_ref.shape[1]
    lane_probe = lax.broadcasted_iota(jnp.int32, (members, LANES), 1)
    picked = [zero for _ in range(4)]
    for probe in range(probes):
        line = probe * lines // probes
        column = columns_ref[probe] - line * width
        tile = column // LANES
        shift = lax.rem(probe - lax.rem(column, LANES) + LANES, LANES)
        values = warmth[STEPS + line, :, pl.ds(pl.multiple_of(tile * LANES, LANES), LANES)]
        moved = pltpu.roll(values, shift, 1)
        picked[probe % 4] = jnp.where(lane_probe == probe, moved, picked[probe % 4])
    total = (picked[0] + picked[1]) + (picked[2] + picked[3])
    predicted = total[:, :probes]
    predicted_ref[...] = predicted
    normal = (recorded_ref[...] - predicted) / sigma_ref[...]
    payload = jnp.concatenate([normal, normal + draws_ref[...]], axis=1)
    for device in range(payload_ref.shape[0]):
        payload_ref[device] = payload


def solve_kernel(norm_scale, slabs, offsets, turns, place_ref, payload_ref, solved_ref):
    members, probes = payload_ref.shape[1], payload_ref.shape[2] // 2
    order = len(offsets) * members
    mine = place_ref[0]
    dims = (((1,), (1,)), ((), ()))
    gram, cross = None, None
    for slab in range(slabs):
        blocks = [
            payload_ref[jnp.bitwise_xor(mine, offset) * slabs + slab] for offset in offsets
        ]
        normal = jnp.concatenate([block[:, :probes] for block in blocks], axis=0)
        center = jnp.sum(normal, axis=0, keepdims=True) * (1.0 / order)
        scaled = (center - normal) * norm_scale
        misfit = jnp.concatenate(
            [blocks[offsets.index(turn)][:, probes:] for turn in turns], axis=0
        )
        one = lax.dot_general(
            scaled, scaled, dims, precision=lax.Precision.HIGHEST, preferred_element_type=jnp.float32
        )
        two = lax.dot_general(
            misfit, scaled, dims, precision=lax.Precision.HIGHEST, preferred_element_type=jnp.float32
        )
        gram = one if gram is None else gram + one
        cross = two if cross is None else cross + two
    row_id = lax.broadcasted_iota(jnp.int32, (ROWS, order), 0)
    lane_id = lax.broadcasted_iota(jnp.int32, (ROWS, order), 1)
    blocks = order // ROWS
    tableau = [
        gram[k * ROWS : (k + 1) * ROWS, :]
        + jnp.where(lane_id == row_id + k * ROWS, damping, 0.0)
        for k in range(blocks)
    ]
    tableau += [cross[k : k + ROWS, :] for k in range(0, len(turns) * members, ROWS)]

    def lanes_of(value, at):
        return jnp.broadcast_to(value[:, at : at + 1], (ROWS, order))

    def row_of(value, at):
        return jnp.broadcast_to(value[at : at + 1, :], (ROWS, order))

    for block in range(blocks):
        base = block * ROWS
        inside = jnp.logical_and(lane_id >= base, lane_id < base + ROWS)
        band = tableau[block]
        column = [lanes_of(band, base + q) for q in range(ROWS)]
        band = jnp.where(inside, jnp.where(lane_id == row_id + base, -1.0, 0.0), band)
        for q in range(ROWS):
            here = row_id == q
            inverse = 1.0 / row_of(column[q], q)
            pivot_row = row_of(band, q) * inverse
            band = jnp.where(here, pivot_row, band - column[q] * pivot_row)
            for j in range(q + 1, ROWS):
                factor = row_of(column[j], q) * inverse
                column[j] = jnp.where(here, factor, column[j] - column[q] * factor)
        rows = [row_of(band, q) for q in range(ROWS)]
        for other in range(block + 1, len(tableau)):
            value = tableau[other]
            products = [lanes_of(value, base + q) * rows[q] for q in range(ROWS)]
            while len(products) > 1:
                products = [a + b for a, b in zip(products[::2], products[1::2])]
            tableau[other] = jnp.where(inside, 0.0, value) - products[0]
    solved_ref[...] = jnp.concatenate(tableau[blocks:], axis=0).astype(jnp.bfloat16)


def apply_kernel(norm_scale, lines, solved_ref, *refs):
    outs = refs[len(refs) // 2 :]
    part_refs = refs[: len(refs) // 2][::-1]
    solved = solved_ref[...]
    pair, order = solved.shape
    wide = order * lines
    spread = (
        lax.broadcasted_iota(jnp.int32, (order, wide), 1) // lines
        == lax.broadcasted_iota(jnp.int32, (order, wide), 0)
    ).astype(jnp.bfloat16)
    stretched = jnp.dot(solved, spread, preferred_element_type=jnp.float32)
    on_line = lax.broadcasted_iota(jnp.int32, (lines, wide), 1) % lines == (
        lax.broadcasted_iota(jnp.int32, (lines, wide), 0)
    )
    weights = jnp.concatenate(
        [
            jnp.where(on_line, jnp.broadcast_to(stretched[j : j + 1, :], (lines, wide)), 0.0)
            for j in range(pair)
        ],
        axis=0,
    ).astype(jnp.bfloat16)
    change, start = None, 0
    for ref in part_refs:
        deep = ref.shape[0]
        part = jnp.dot(
            weights[:, start : start + deep], ref[...], preferred_element_type=jnp.float32
        )
        change = part if change is None else change + part
        start += deep
    change = change * norm_scale
    rows = outs[0].shape[0]
    for turn, ref in enumerate(outs):
        ref[...] = change[turn * rows : (turn + 1) * rows].astype(ref.dtype)


def merge_kernel(place_ref, field_ref, *refs):
    pieces, out_ref = refs[:-1][::-1], refs[-1]
    share = pieces[0].shape[1]
    mine = jnp.bitwise_and(place_ref[0], len(pieces) - 1)
    for turn, piece in enumerate(pieces):
        start = pl.multiple_of(jnp.bitwise_xor(mine, turn) * share, LANES)
        columns = pl.ds(start, share)
        out_ref[:, columns] = field_ref[:, columns] + piece[...].astype(jnp.float32)


def body(
    logarithmic_diffusivity,
    starting_warmth,
    thermal_supply,
    probe_positions,
    recorded_temps,
    probe_error_sigma,
    perturb_draws,
):
    members, lines, width = logarithmic_diffusivity.shape
    owners, slabs = lax.axis_size("mem"), lax.axis_size("sp")
    order = members * owners
    norm_scale = 1.0 / math.sqrt(order - 1)
    probes = probe_positions.shape[0]
    slab = lax.axis_index("sp")

    mine = lax.axis_index("mem").astype(jnp.int32)
    turns = range(math.gcd(owners, 4))
    share = width // len(turns)

    def across(value, bit):
        return lax.ppermute(value, "mem", [(i, i ^ bit) for i in range(owners)])

    field_flat = logarithmic_diffusivity.reshape(members * lines, width)
    field_round = field_flat.astype(jnp.bfloat16)
    parts, offsets = [field_round], [0]
    bits = []
    while len(turns) << len(bits) < owners:
        bits.insert(0, len(turns) << len(bits))

    def exchange(parts, offsets, bit):
        held = jnp.concatenate(parts, axis=0)
        return [held, across(held, bit)], offsets + [offset ^ bit for offset in offsets]

    for bit in bits[:1]:
        parts, offsets = exchange(parts, offsets, bit)

    edges = jnp.concatenate([field_flat, starting_warmth, thermal_supply], axis=0)
    if slabs == 2:
        up = down = lax.ppermute(edges, "sp", [(0, 1), (1, 0)])
    else:
        up = lax.ppermute(edges, "sp", [(i, i + 1) for i in range(slabs - 1)])
        down = lax.ppermute(edges, "sp", [(i + 1, i) for i in range(slabs - 1)])
    flags = jnp.stack([slab > 0, slab < slabs - 1]).astype(jnp.int32)
    vmem = pl.BlockSpec(memory_space=pltpu.VMEM)
    smem = pl.BlockSpec(memory_space=pltpu.SMEM)
    anywhere = pl.BlockSpec(memory_space=pl.ANY)
    window = lines + 2 * STEPS
    devices = owners * slabs
    beside = [up] if slabs == 2 else [up, down]

    def kernel(flags_ref, columns_hbm, field_ref, *refs):
        neighbours, rest = refs[: len(beside)], refs[len(beside) :]
        conduct_kernel(
            flags_ref, columns_hbm, field_ref, neighbours[0], neighbours[-1], *rest
        )

    predicted, payload = pl.pallas_call(
        kernel,
        out_shape=(
            jax.ShapeDtypeStruct((members, probes), jnp.float32),
            jax.ShapeDtypeStruct((devices, members, 2 * probes), jnp.float32),
        ),
        in_specs=[smem, anywhere] + [vmem] * (3 + len(beside)) + [anywhere] * 3,
        out_specs=(vmem, vmem),
        scratch_shapes=[
            pltpu.VMEM((window, members, width), jnp.float32),
            pltpu.VMEM((window, members, width), jnp.float32),
            pltpu.VMEM((window, width), jnp.float32),
            pltpu.SMEM((probes,), jnp.int32),
            pltpu.VMEM((1, probes), jnp.float32),
            pltpu.VMEM((1, probes), jnp.float32),
            pltpu.VMEM((members, probes), jnp.float32),
            pltpu.SemaphoreType.DMA((4,)),
        ],
        compiler_params=pltpu.CompilerParams(vmem_limit_bytes=24 * 1024 * 1024),
        cost_estimate=pl.CostEstimate(
            flops=30 * STEPS * window * members * width,
            bytes_accessed=4 * 3 * members * lines * width,
            transcendentals=STEPS * window * members * width,
        ),
        name="conduct",
    )(
        flags,
        probe_positions,
        field_flat,
        *beside,
        starting_warmth,
        thermal_supply,
        recorded_temps[None, :],
        probe_error_sigma[None, :],
        perturb_draws,
    )
    payload, *parts = lax.optimization_barrier((payload, *parts))
    for bit in bits[1:]:
        parts, offsets = exchange(parts, offsets, bit)
    everyone = lax.all_to_all(payload, ("mem", "sp"), 0, 0, tiled=True)
    held = jnp.concatenate(parts, axis=0)
    parts = []
    for turn in reversed(turns):
        columns = ((mine ^ turn) & (len(turns) - 1)) * share
        piece = lax.dynamic_slice_in_dim(held, columns, share, 1)
        parts.insert(0, across(piece, turn) if turn else piece)
    offsets = [offset ^ turn for turn in turns for offset in offsets]
    if order <= LANES:
        solved = pl.pallas_call(
            lambda *refs: solve_kernel(norm_scale, slabs, offsets, turns, *refs),
            out_shape=jax.ShapeDtypeStruct((len(turns) * members, order), jnp.bfloat16),
            in_specs=[smem, vmem],
            out_specs=vmem,
            compiler_params=pltpu.CompilerParams(vmem_limit_bytes=16 * 1024 * 1024),
            cost_estimate=pl.CostEstimate(
                flops=2 * order * order * order,
                bytes_accessed=4 * devices * members * 2 * probes,
                transcendentals=0,
            ),
            name="solve",
        )(mine[None], everyone)
    else:
        owner = mine ^ jnp.array(offsets, jnp.int32)
        split = everyone.reshape(owners, slabs, members, 2, probes)[owner]
        split = split.transpose(3, 0, 2, 1, 4).reshape(2, order, slabs * probes)
        normal = split[0]
        misfit = split[1].reshape(owners, members, -1)
        misfit = jnp.concatenate([misfit[offsets.index(turn)] for turn in turns], axis=0)
        scaled = (jnp.mean(normal, axis=0, keepdims=True) - normal) * norm_scale
        gram_matrix = jnp.dot(
            scaled, scaled.T, precision=lax.Precision.HIGHEST, preferred_element_type=jnp.float32
        ) + damping * jnp.eye(order, dtype=jnp.float32)
        cross_term = jnp.dot(
            scaled, misfit.T, precision=lax.Precision.HIGHEST, preferred_element_type=jnp.float32
        )
        solved = eliminate(gram_matrix, cross_term).T.astype(jnp.bfloat16)
    rows = members * lines
    pieces = pl.pallas_call(
        lambda *refs: apply_kernel(norm_scale, lines, *refs),
        out_shape=[
            jax.ShapeDtypeStruct((rows, share), jnp.bfloat16 if turn else jnp.float32)
            for turn in turns
        ],
        in_specs=[vmem] * (1 + len(parts)),
        out_specs=[vmem] * len(turns),
        compiler_params=pltpu.CompilerParams(vmem_limit_bytes=40 * 1024 * 1024),
        cost_estimate=pl.CostEstimate(
            flops=2 * rows * order * lines * width,
            bytes_accessed=2 * order * lines * share,
            transcendentals=0,
        ),
        name="apply",
    )(solved, *parts[::-1])
    pieces = [
        across(pieces[turn], turn) if turn else pieces[turn] for turn in reversed(turns)
    ][::-1]
    revised = pl.pallas_call(
        merge_kernel,
        out_shape=jax.ShapeDtypeStruct((rows, width), jnp.float32),
        in_specs=[smem] + [vmem] * (1 + len(turns)),
        out_specs=vmem,
        compiler_params=pltpu.CompilerParams(vmem_limit_bytes=8 * 1024 * 1024),
        name="merge",
    )(mine[None], field_flat, *pieces[::-1])
    return (revised.reshape(logarithmic_diffusivity.shape), predicted)


def solution(mesh):
    in_specs = (
        P("mem", "sp", None),
        P("sp", None),
        P("sp", None),
        P("sp"),
        P("sp"),
        P("sp"),
        P("mem", "sp"),
    )
    out_specs = (P("mem", "sp", None), P("mem", "sp"))
    return jax.shard_map(body, mesh=mesh, in_specs=in_specs, out_specs=out_specs, check_vma=False)
```

```python
import math

import jax
import jax.numpy as jnp
from jax import lax
from jax.experimental import pallas as pl
from jax.experimental.pallas import tpu as pltpu
from jax.sharding import PartitionSpec as P

STEPS = 4


time_step = 0.06
damping = 2.0
block_width = 16
LANES = 128
ROWS = 8


def invert_block(matrix):
    augmented = jnp.concatenate([matrix, jnp.eye(block_width, dtype=matrix.dtype)], axis=1)
    for place in range(block_width):
        pivot_row = augmented[place] / augmented[place, place]
        augmented = augmented - augmented[:, place : place + 1] * pivot_row[None, :]
        augmented = jnp.concatenate(
            [augmented[:place], pivot_row[None, :], augmented[place + 1 :]], axis=0
        )
    return augmented[:, block_width:]


def eliminate(gram_matrix, cross_term):
    order = gram_matrix.shape[0]
    tableau = jnp.concatenate([gram_matrix, cross_term], axis=1)

    def one_turn(block_number, tableau):
        first_row = (block_number * block_width).astype(jnp.int32)
        row_band = lax.dynamic_slice_in_dim(tableau, first_row, block_width, 0)
        pivot_block = lax.dynamic_slice_in_dim(row_band, first_row, block_width, 1)
        inverse = invert_block(pivot_block)
        scaled_rows = jnp.dot(
            inverse, row_band, precision=lax.Precision.HIGHEST, preferred_element_type=tableau.dtype
        )
        column = lax.dynamic_slice_in_dim(tableau, first_row, block_width, 1)
        tableau = tableau - jnp.dot(
            column,
            scaled_rows,
            precision=lax.Precision.HIGHEST,
            preferred_element_type=tableau.dtype,
        )
        return lax.dynamic_update_slice_in_dim(tableau, scaled_rows, first_row, 0)

    tableau = lax.fori_loop(0, order // block_width, one_turn, tableau)
    return tableau[:, order:]


def conduct_kernel(
    columns_hbm,
    field_ref,
    up_ref,
    down_ref,
    start_ref,
    source_ref,
    recorded_hbm,
    sigma_hbm,
    draws_hbm,
    predicted_ref,
    payload_ref,
    warmth,
    half_exp,
    supply,
    columns_ref,
    recorded_ref,
    sigma_ref,
    draws_ref,
    sems,
):
    lines = start_ref.shape[0]
    copies = [
        pltpu.make_async_copy(source, target, sems.at[k])
        for k, (source, target) in enumerate(
            (
                (columns_hbm, columns_ref),
                (recorded_hbm, recorded_ref),
                (sigma_hbm, sigma_ref),
                (draws_hbm, draws_ref),
            )
        )
    ]
    for copy in copies:
        copy.start()
    members, width = predicted_ref.shape[0], start_ref.shape[1]
    tiles = width // LANES
    window = lines + 2 * STEPS
    lane = lax.broadcasted_iota(jnp.int32, (members, LANES), 1)
    first, last = lane == 0, lane == LANES - 1

    slab = lax.axis_index("sp")
    above, below = slab > 0, slab < lax.axis_size("sp") - 1
    sides = (
        (0, up_ref, lines - STEPS, STEPS, above),
        (STEPS, field_ref, 0, lines, None),
        (STEPS + lines, down_ref, 0, STEPS, below),
    )
    def by_rows(ref):
        return jnp.swapaxes(ref[0 : members * lines, :].reshape(members, lines, width), 0, 1)

    turned = {id(ref): by_rows(ref) for ref in (field_ref, up_ref, down_ref)}
    for row, ref, line, count, inside in sides:
        coefficient = turned[id(ref)]
        for step in range(count):
            part = coefficient[line + step]
            if inside is not None:
                part = jnp.where(inside, part, 0.0)
            half_exp[row + step] = 0.5 * jnp.exp(part)
    for row, ref, line, count, inside in sides:
        for step in range(count):
            if inside is None:
                heat = start_ref[pl.ds(line + step, 1), :]
            else:
                heat = jnp.where(inside, ref[pl.ds(members * lines + line + step, 1), :], 0.0)
            warmth[row + step] = jnp.broadcast_to(heat, (members, width))
        if inside is None:
            supply[pl.ds(row, count), :] = source_ref[...]
        else:
            base = (members + 1) * lines + line
            supply[pl.ds(row, count), :] = ref[pl.ds(base, count), :]

    def cut(value):
        return [value[:, k * LANES : (k + 1) * LANES] for k in range(tiles)]

    def conductivity(row, warm):
        half = cut(half_exp[row])
        return [h * (1.0 + 0.5 * jnp.tanh(t)) for h, t in zip(half, warm)]

    half_one = jnp.full((members, LANES), 0.5, jnp.float32)
    zero = jnp.zeros((members, LANES), jnp.float32)

    for step in range(STEPS):
        low, high = step + 1, window - 1 - step
        t_up = cut(warmth[low - 1])
        c_up = conductivity(low - 1, t_up)
        t_here = cut(warmth[low])
        c_here = conductivity(low, t_here)
        flow_up = [(a + b) * (y - x) for a, b, x, y in zip(c_up, c_here, t_up, t_here)]

        def one_row(row, carry):
            t, c, up = carry
            t_next = cut(warmth[row + 1])
            c_next = conductivity(row + 1, t_next)
            down = [(a + b) * (y - x) for a, b, x, y in zip(c, c_next, t, t_next)]
            t_roll = [pltpu.roll(x, LANES - 1, 1) for x in t] + [zero]
            c_roll = [pltpu.roll(x, LANES - 1, 1) for x in c] + [half_one]
            right = []
            for k in range(tiles):
                t_right = jnp.where(last, t_roll[k + 1], t_roll[k])
                c_right = jnp.where(last, c_roll[k + 1], c_roll[k])
                right.append((c[k] + c_right) * (t_right - t[k]))
            back = [pltpu.roll(x, 1, 1) for x in right]
            outside = jnp.logical_or(
                jnp.logical_and(row < STEPS, jnp.logical_not(above)),
                jnp.logical_and(row >= STEPS + lines, jnp.logical_not(below)),
            )
            keep = jnp.where(outside, 0.0, 1.0)
            source = supply[pl.ds(row, 1), :]
            for k in range(tiles):
                edge = (c[0] + 0.5) * t[0] if k == 0 else back[k - 1]
                left = jnp.where(first, edge, back[k])
                inflow = (down[k] - up[k]) + (right[k] - left)
                heat = source[:, k * LANES : (k + 1) * LANES]
                warmth[row, :, k * LANES : (k + 1) * LANES] = keep * (
                    t[k] + time_step * (inflow + heat)
                )
            return t_next, c_next, down

        lax.fori_loop(low, high, one_row, (t_here, c_here, flow_up), unroll=True)

    for copy in copies:
        copy.wait()
    probes = predicted_ref.shape[1]
    lane_probe = lax.broadcasted_iota(jnp.int32, (members, LANES), 1)
    picked = [zero for _ in range(4)]
    for probe in range(probes):
        line = probe * lines // probes
        column = columns_ref[probe] - line * width
        tile = column // LANES
        shift = lax.rem(probe - lax.rem(column, LANES) + LANES, LANES)
        values = warmth[STEPS + line, :, pl.ds(pl.multiple_of(tile * LANES, LANES), LANES)]
        moved = pltpu.roll(values, shift, 1)
        picked[probe % 4] = jnp.where(lane_probe == probe, moved, picked[probe % 4])
    total = (picked[0] + picked[1]) + (picked[2] + picked[3])
    predicted = total[:, :probes]
    predicted_ref[...] = predicted
    normal = (recorded_ref[...] - predicted) / sigma_ref[...]
    payload = jnp.concatenate([normal, normal + draws_ref[...]], axis=1)
    for device in range(payload_ref.shape[0]):
        payload_ref[device] = payload


def solve_kernel(norm_scale, slabs, offsets, turns, payload_ref, solved_ref):
    members, probes = payload_ref.shape[1], payload_ref.shape[2] // 2
    order = len(offsets) * members
    mine = lax.axis_index("mem")
    dims = (((1,), (1,)), ((), ()))
    gram, cross = None, None
    for slab in range(slabs):
        blocks = [
            payload_ref[jnp.bitwise_xor(mine, offset) * slabs + slab] for offset in offsets
        ]
        normal = jnp.concatenate([block[:, :probes] for block in blocks], axis=0)
        center = jnp.sum(normal, axis=0, keepdims=True) * (1.0 / order)
        scaled = (center - normal) * norm_scale
        misfit = jnp.concatenate(
            [blocks[offsets.index(turn)][:, probes:] for turn in turns], axis=0
        )
        one = lax.dot_general(
            scaled, scaled, dims, precision=lax.Precision.HIGHEST, preferred_element_type=jnp.float32
        )
        two = lax.dot_general(
            misfit, scaled, dims, precision=lax.Precision.HIGHEST, preferred_element_type=jnp.float32
        )
        gram = one if gram is None else gram + one
        cross = two if cross is None else cross + two
    row_id = lax.broadcasted_iota(jnp.int32, (ROWS, order), 0)
    lane_id = lax.broadcasted_iota(jnp.int32, (ROWS, order), 1)
    blocks = order // ROWS
    tableau = [
        gram[k * ROWS : (k + 1) * ROWS, :]
        + jnp.where(lane_id == row_id + k * ROWS, damping, 0.0)
        for k in range(blocks)
    ]
    tableau += [cross[k : k + ROWS, :] for k in range(0, len(turns) * members, ROWS)]

    def lanes_of(value, at):
        return jnp.broadcast_to(value[:, at : at + 1], (ROWS, order))

    def row_of(value, at):
        return jnp.broadcast_to(value[at : at + 1, :], (ROWS, order))

    for block in range(blocks):
        base = block * ROWS
        inside = jnp.logical_and(lane_id >= base, lane_id < base + ROWS)
        band = tableau[block]
        column = [lanes_of(band, base + q) for q in range(ROWS)]
        band = jnp.where(inside, jnp.where(lane_id == row_id + base, -1.0, 0.0), band)
        for q in range(ROWS):
            here = row_id == q
            inverse = 1.0 / row_of(column[q], q)
            pivot_row = row_of(band, q) * inverse
            band = jnp.where(here, pivot_row, band - column[q] * pivot_row)
            for j in range(q + 1, ROWS):
                factor = row_of(column[j], q) * inverse
                column[j] = jnp.where(here, factor, column[j] - column[q] * factor)
        rows = [row_of(band, q) for q in range(ROWS)]
        for other in range(block + 1, len(tableau)):
            value = tableau[other]
            products = [lanes_of(value, base + q) * rows[q] for q in range(ROWS)]
            while len(products) > 1:
                products = [a + b for a, b in zip(products[::2], products[1::2])]
            tableau[other] = jnp.where(inside, 0.0, value) - products[0]
    solved_ref[...] = jnp.concatenate(tableau[blocks:], axis=0).astype(jnp.bfloat16)


def apply_kernel(norm_scale, lines, solved_ref, *refs):
    outs = refs[len(refs) // 2 :]
    part_refs = refs[: len(refs) // 2][::-1]
    solved = solved_ref[...]
    pair, order = solved.shape
    wide = order * lines
    spread = (
        lax.broadcasted_iota(jnp.int32, (order, wide), 1) // lines
        == lax.broadcasted_iota(jnp.int32, (order, wide), 0)
    ).astype(jnp.bfloat16)
    stretched = jnp.dot(solved, spread, preferred_element_type=jnp.float32)
    on_line = lax.broadcasted_iota(jnp.int32, (lines, wide), 1) % lines == (
        lax.broadcasted_iota(jnp.int32, (lines, wide), 0)
    )
    weights = jnp.concatenate(
        [
            jnp.where(on_line, jnp.broadcast_to(stretched[j : j + 1, :], (lines, wide)), 0.0)
            for j in range(pair)
        ],
        axis=0,
    ).astype(jnp.bfloat16)
    change, start = None, 0
    for ref in part_refs:
        deep = ref.shape[0]
        part = jnp.dot(
            weights[:, start : start + deep], ref[...], preferred_element_type=jnp.float32
        )
        change = part if change is None else change + part
        start += deep
    change = change * norm_scale
    rows = outs[0].shape[0]
    for turn, ref in enumerate(outs):
        ref[...] = change[turn * rows : (turn + 1) * rows].astype(ref.dtype)


def merge_kernel(field_ref, *refs):
    pieces, out_ref = refs[:-1][::-1], refs[-1]
    share = pieces[0].shape[1]
    mine = jnp.bitwise_and(lax.axis_index("mem"), len(pieces) - 1)
    for turn, piece in enumerate(pieces):
        start = pl.multiple_of(jnp.bitwise_xor(mine, turn) * share, LANES)
        columns = pl.ds(start, share)
        out_ref[:, columns] = field_ref[:, columns] + piece[...].astype(jnp.float32)


def body(
    logarithmic_diffusivity,
    starting_warmth,
    thermal_supply,
    probe_positions,
    recorded_temps,
    probe_error_sigma,
    perturb_draws,
):
    members, lines, width = logarithmic_diffusivity.shape
    owners, slabs = lax.axis_size("mem"), lax.axis_size("sp")
    order = members * owners
    norm_scale = 1.0 / math.sqrt(order - 1)
    probes = probe_positions.shape[0]

    mine = lax.axis_index("mem").astype(jnp.int32)
    turns = range(math.gcd(owners, 4))
    share = width // len(turns)

    def across(value, bit):
        return lax.ppermute(value, "mem", [(i, i ^ bit) for i in range(owners)])

    field_flat = logarithmic_diffusivity.reshape(members * lines, width)
    field_round = field_flat.astype(jnp.bfloat16)
    parts, offsets = [field_round], [0]
    bits = []
    while len(turns) << len(bits) < owners:
        bits.insert(0, len(turns) << len(bits))

    def exchange(parts, offsets, bit):
        held = jnp.concatenate(parts, axis=0)
        return [held, across(held, bit)], offsets + [offset ^ bit for offset in offsets]

    for bit in bits[:2]:
        offsets = offsets + [offset ^ bit for offset in reversed(offsets)]
    parts = [across(field_round, offset) if offset else field_round for offset in offsets]

    start_tied, parts[0] = lax.optimization_barrier((starting_warmth, parts[0]))
    edges = jnp.concatenate([field_flat, start_tied, thermal_supply], axis=0)
    if slabs == 2:
        up = down = lax.ppermute(edges, "sp", [(0, 1), (1, 0)])
    else:
        up = lax.ppermute(edges, "sp", [(i, i + 1) for i in range(slabs - 1)])
        down = lax.ppermute(edges, "sp", [(i + 1, i) for i in range(slabs - 1)])
    vmem = pl.BlockSpec(memory_space=pltpu.VMEM)
    smem = pl.BlockSpec(memory_space=pltpu.SMEM)
    anywhere = pl.BlockSpec(memory_space=pl.ANY)
    window = lines + 2 * STEPS
    devices = owners * slabs
    beside = [up] if slabs == 2 else [up, down]

    def kernel(columns_hbm, field_ref, *refs):
        neighbours, rest = refs[: len(beside)], refs[len(beside) :]
        conduct_kernel(columns_hbm, field_ref, neighbours[0], neighbours[-1], *rest)

    predicted, payload = pl.pallas_call(
        kernel,
        out_shape=(
            jax.ShapeDtypeStruct((members, probes), jnp.float32),
            jax.ShapeDtypeStruct((devices, members, 2 * probes), jnp.float32),
        ),
        in_specs=[anywhere] + [vmem] * (3 + len(beside)) + [anywhere] * 3,
        out_specs=(vmem, vmem),
        scratch_shapes=[
            pltpu.VMEM((window, members, width), jnp.float32),
            pltpu.VMEM((window, members, width), jnp.float32),
            pltpu.VMEM((window, width), jnp.float32),
            pltpu.SMEM((probes,), jnp.int32),
            pltpu.VMEM((1, probes), jnp.float32),
            pltpu.VMEM((1, probes), jnp.float32),
            pltpu.VMEM((members, probes), jnp.float32),
            pltpu.SemaphoreType.DMA((4,)),
        ],
        compiler_params=pltpu.CompilerParams(vmem_limit_bytes=24 * 1024 * 1024),
        cost_estimate=pl.CostEstimate(
            flops=30 * STEPS * window * members * width,
            bytes_accessed=4 * 3 * members * lines * width,
            transcendentals=STEPS * window * members * width,
        ),
        name="conduct",
    )(
        probe_positions,
        field_flat,
        *beside,
        starting_warmth,
        thermal_supply,
        recorded_temps[None, :],
        probe_error_sigma[None, :],
        perturb_draws,
    )
    _, *parts = lax.optimization_barrier((payload, *parts))
    for bit in bits[2:]:
        parts, offsets = exchange(parts, offsets, bit)
    everyone = lax.all_to_all(payload, ("mem", "sp"), 0, 0, tiled=True)
    held = jnp.concatenate(parts, axis=0)
    parts = []
    for turn in reversed(turns):
        columns = ((mine ^ turn) & (len(turns) - 1)) * share
        piece = lax.dynamic_slice_in_dim(held, columns, share, 1)
        parts.insert(0, across(piece, turn) if turn else piece)
    offsets = [offset ^ turn for turn in turns for offset in offsets]
    if order <= LANES:
        solved = pl.pallas_call(
            lambda *refs: solve_kernel(norm_scale, slabs, offsets, turns, *refs),
            out_shape=jax.ShapeDtypeStruct((len(turns) * members, order), jnp.bfloat16),
            in_specs=[vmem],
            out_specs=vmem,
            compiler_params=pltpu.CompilerParams(vmem_limit_bytes=16 * 1024 * 1024),
            cost_estimate=pl.CostEstimate(
                flops=2 * order * order * order,
                bytes_accessed=4 * devices * members * 2 * probes,
                transcendentals=0,
            ),
            name="solve",
        )(everyone)
    else:
        owner = mine ^ jnp.array(offsets, jnp.int32)
        split = everyone.reshape(owners, slabs, members, 2, probes)[owner]
        split = split.transpose(3, 0, 2, 1, 4).reshape(2, order, slabs * probes)
        normal = split[0]
        misfit = split[1].reshape(owners, members, -1)
        misfit = jnp.concatenate([misfit[offsets.index(turn)] for turn in turns], axis=0)
        scaled = (jnp.mean(normal, axis=0, keepdims=True) - normal) * norm_scale
        gram_matrix = jnp.dot(
            scaled, scaled.T, precision=lax.Precision.HIGHEST, preferred_element_type=jnp.float32
        ) + damping * jnp.eye(order, dtype=jnp.float32)
        cross_term = jnp.dot(
            scaled, misfit.T, precision=lax.Precision.HIGHEST, preferred_element_type=jnp.float32
        )
        solved = eliminate(gram_matrix, cross_term).T.astype(jnp.bfloat16)
    rows = members * lines
    pieces = pl.pallas_call(
        lambda *refs: apply_kernel(norm_scale, lines, *refs),
        out_shape=[
            jax.ShapeDtypeStruct((rows, share), jnp.bfloat16 if turn else jnp.float32)
            for turn in turns
        ],
        in_specs=[vmem] * (1 + len(parts)),
        out_specs=[vmem] * len(turns),
        compiler_params=pltpu.CompilerParams(vmem_limit_bytes=40 * 1024 * 1024),
        cost_estimate=pl.CostEstimate(
            flops=2 * rows * order * lines * width,
            bytes_accessed=2 * order * lines * share,
            transcendentals=0,
        ),
        name="apply",
    )(solved, *parts[::-1])
    pieces = [
        across(pieces[turn], turn) if turn else pieces[turn] for turn in reversed(turns)
    ][::-1]
    revised = pl.pallas_call(
        merge_kernel,
        out_shape=jax.ShapeDtypeStruct((rows, width), jnp.float32),
        in_specs=[vmem] * (1 + len(turns)),
        out_specs=vmem,
        compiler_params=pltpu.CompilerParams(vmem_limit_bytes=8 * 1024 * 1024),
        name="merge",
    )(field_flat, *pieces[::-1])
    return (revised.reshape(logarithmic_diffusivity.shape), predicted)


def solution(mesh):
    in_specs = (
        P("mem", "sp", None),
        P("sp", None),
        P("sp", None),
        P("sp"),
        P("sp"),
        P("sp"),
        P("mem", "sp"),
    )
    out_specs = (P("mem", "sp", None), P("mem", "sp"))
    return jax.shard_map(body, mesh=mesh, in_specs=in_specs, out_specs=out_specs, check_vma=False)
```

```python
import math

import jax
import jax.numpy as jnp
from jax import lax
from jax.experimental import pallas as pl
from jax.experimental.pallas import tpu as pltpu
from jax.sharding import PartitionSpec as P

STEPS = 4


time_step = 0.06
damping = 2.0
block_width = 16
LANES = 128
ROWS = 8


def invert_block(matrix):
    augmented = jnp.concatenate([matrix, jnp.eye(block_width, dtype=matrix.dtype)], axis=1)
    for place in range(block_width):
        pivot_row = augmented[place] / augmented[place, place]
        augmented = augmented - augmented[:, place : place + 1] * pivot_row[None, :]
        augmented = jnp.concatenate(
            [augmented[:place], pivot_row[None, :], augmented[place + 1 :]], axis=0
        )
    return augmented[:, block_width:]


def eliminate(gram_matrix, cross_term):
    order = gram_matrix.shape[0]
    tableau = jnp.concatenate([gram_matrix, cross_term], axis=1)

    def one_turn(block_number, tableau):
        first_row = (block_number * block_width).astype(jnp.int32)
        row_band = lax.dynamic_slice_in_dim(tableau, first_row, block_width, 0)
        pivot_block = lax.dynamic_slice_in_dim(row_band, first_row, block_width, 1)
        inverse = invert_block(pivot_block)
        scaled_rows = jnp.dot(
            inverse, row_band, precision=lax.Precision.HIGHEST, preferred_element_type=tableau.dtype
        )
        column = lax.dynamic_slice_in_dim(tableau, first_row, block_width, 1)
        tableau = tableau - jnp.dot(
            column,
            scaled_rows,
            precision=lax.Precision.HIGHEST,
            preferred_element_type=tableau.dtype,
        )
        return lax.dynamic_update_slice_in_dim(tableau, scaled_rows, first_row, 0)

    tableau = lax.fori_loop(0, order // block_width, one_turn, tableau)
    return tableau[:, order:]


def conduct_kernel(
    columns_hbm,
    field_ref,
    up_ref,
    down_ref,
    start_ref,
    source_ref,
    recorded_hbm,
    sigma_hbm,
    draws_hbm,
    predicted_ref,
    payload_ref,
    warmth,
    half_exp,
    supply,
    columns_ref,
    recorded_ref,
    sigma_ref,
    draws_ref,
    sems,
):
    lines = start_ref.shape[0]
    copies = [
        pltpu.make_async_copy(source, target, sems.at[k])
        for k, (source, target) in enumerate(
            (
                (columns_hbm, columns_ref),
                (recorded_hbm, recorded_ref),
                (sigma_hbm, sigma_ref),
                (draws_hbm, draws_ref),
            )
        )
    ]
    for copy in copies:
        copy.start()
    members, width = predicted_ref.shape[0], start_ref.shape[1]
    tiles = width // LANES
    top = 0 if up_ref is None else STEPS
    window = top + lines + STEPS
    lane = lax.broadcasted_iota(jnp.int32, (members, LANES), 1)
    first, last = lane == 0, lane == LANES - 1

    slab = lax.axis_index("sp")
    def by_rows(ref):
        return jnp.swapaxes(ref[0 : members * lines, :].reshape(members, lines, width), 0, 1)

    def turn(line):
        return jnp.where(slab > 0, lines - 1 - line, line)

    if top:
        above, below = slab > 0, slab < lax.axis_size("sp") - 1
        sides = (
            (0, up_ref, lines - STEPS, STEPS, above),
            (STEPS, field_ref, 0, lines, None),
            (STEPS + lines, down_ref, 0, STEPS, below),
        )
        turned = {id(ref): by_rows(ref) for ref in (field_ref, up_ref, down_ref)}
        for row, ref, line, count, inside in sides:
            coefficient = turned[id(ref)]
            for step in range(count):
                part = coefficient[line + step]
                if inside is not None:
                    part = jnp.where(inside, part, 0.0)
                half_exp[row + step] = 0.5 * jnp.exp(part)
        for row, ref, line, count, inside in sides:
            for step in range(count):
                if inside is None:
                    heat = start_ref[pl.ds(line + step, 1), :]
                else:
                    heat = jnp.where(inside, ref[pl.ds(members * lines + line + step, 1), :], 0.0)
                warmth[row + step] = jnp.broadcast_to(heat, (members, width))
            if inside is None:
                supply[pl.ds(row, count), :] = source_ref[...]
            else:
                base = (members + 1) * lines + line
                supply[pl.ds(row, count), :] = ref[pl.ds(base, count), :]
    else:
        own, other = by_rows(field_ref), by_rows(down_ref)
        for line in range(lines):
            half_exp[turn(line)] = 0.5 * jnp.exp(own[line])
        for step in range(STEPS):
            part = jnp.where(slab > 0, other[lines - 1 - step], other[step])
            half_exp[lines + step] = 0.5 * jnp.exp(part)
        for row in range(lines + STEPS):
            if row < lines:
                heat = start_ref[pl.ds(turn(row), 1), :]
                source = source_ref[pl.ds(turn(row), 1), :]
            else:
                line = members * lines + turn(row - lines)
                heat = down_ref[pl.ds(line, 1), :]
                source = down_ref[pl.ds(line + lines, 1), :]
            warmth[row] = jnp.broadcast_to(heat, (members, width))
            supply[pl.ds(row, 1), :] = source

    def cut(value):
        return [value[:, k * LANES : (k + 1) * LANES] for k in range(tiles)]

    def conductivity(row, warm):
        half = cut(half_exp[row])
        return [h * (1.0 + 0.5 * jnp.tanh(t)) for h, t in zip(half, warm)]

    half_one = jnp.full((members, LANES), 0.5, jnp.float32)
    zero = jnp.zeros((members, LANES), jnp.float32)

    for step in range(STEPS):
        low, high = step + 1 if top else 0, window - 1 - step
        if top:
            t_up = cut(warmth[low - 1])
            c_up = conductivity(low - 1, t_up)
        else:
            t_up, c_up = [zero] * tiles, [half_one] * tiles
        t_here = cut(warmth[low])
        c_here = conductivity(low, t_here)
        flow_up = [(a + b) * (y - x) for a, b, x, y in zip(c_up, c_here, t_up, t_here)]

        def one_row(row, carry):
            t, c, up = carry
            t_next = cut(warmth[row + 1])
            c_next = conductivity(row + 1, t_next)
            down = [(a + b) * (y - x) for a, b, x, y in zip(c, c_next, t, t_next)]
            t_roll = [pltpu.roll(x, LANES - 1, 1) for x in t] + [zero]
            c_roll = [pltpu.roll(x, LANES - 1, 1) for x in c] + [half_one]
            right = []
            for k in range(tiles):
                t_right = jnp.where(last, t_roll[k + 1], t_roll[k])
                c_right = jnp.where(last, c_roll[k + 1], c_roll[k])
                right.append((c[k] + c_right) * (t_right - t[k]))
            back = [pltpu.roll(x, 1, 1) for x in right]
            keep = 1.0
            if top:
                outside = jnp.logical_or(
                    jnp.logical_and(row < STEPS, jnp.logical_not(above)),
                    jnp.logical_and(row >= STEPS + lines, jnp.logical_not(below)),
                )
                keep = jnp.where(outside, 0.0, 1.0)
            source = supply[pl.ds(row, 1), :]
            for k in range(tiles):
                edge = (c[0] + 0.5) * t[0] if k == 0 else back[k - 1]
                left = jnp.where(first, edge, back[k])
                inflow = (down[k] - up[k]) + (right[k] - left)
                heat = source[:, k * LANES : (k + 1) * LANES]
                fresh = t[k] + time_step * (inflow + heat)
                warmth[row, :, k * LANES : (k + 1) * LANES] = keep * fresh if top else fresh
            return t_next, c_next, down

        lax.fori_loop(low, high, one_row, (t_here, c_here, flow_up), unroll=True)

    for copy in copies:
        copy.wait()
    probes = predicted_ref.shape[1]
    lane_probe = lax.broadcasted_iota(jnp.int32, (members, LANES), 1)
    picked = [zero for _ in range(4)]
    for probe in range(probes):
        line = probe * lines // probes
        column = columns_ref[probe] - line * width
        offset = jnp.bitwise_and(column, LANES - 1)
        shift = jnp.bitwise_and(probe - offset, LANES - 1)
        start = pl.multiple_of(column - offset, LANES)
        place = STEPS + line if top else turn(line)
        values = warmth[place, :, pl.ds(start, LANES)]
        moved = pltpu.roll(values, shift, 1)
        picked[probe % 4] = jnp.where(lane_probe == probe, moved, picked[probe % 4])
    total = (picked[0] + picked[1]) + (picked[2] + picked[3])
    predicted = total[:, :probes]
    predicted_ref[...] = predicted
    normal = (recorded_ref[...] - predicted) / sigma_ref[...]
    payload = jnp.concatenate([normal, normal + draws_ref[...]], axis=1)
    for device in range(payload_ref.shape[0]):
        payload_ref[device] = payload


def solve_kernel(norm_scale, slabs, offsets, turns, payload_ref, solved_ref):
    members, probes = payload_ref.shape[1], payload_ref.shape[2] // 2
    order = len(offsets) * members
    mine = lax.axis_index("mem")
    dims = (((1,), (1,)), ((), ()))
    gram, cross = None, None
    for slab in range(slabs):
        blocks = [
            payload_ref[jnp.bitwise_xor(mine, offset) * slabs + slab] for offset in offsets
        ]
        normal = jnp.concatenate([block[:, :probes] for block in blocks], axis=0)
        center = jnp.sum(normal, axis=0, keepdims=True) * (1.0 / order)
        scaled = (center - normal) * norm_scale
        misfit = jnp.concatenate(
            [blocks[offsets.index(turn)][:, probes:] for turn in turns], axis=0
        )
        one = lax.dot_general(
            scaled, scaled, dims, precision=lax.Precision.HIGHEST, preferred_element_type=jnp.float32
        )
        two = lax.dot_general(
            misfit, scaled, dims, precision=lax.Precision.HIGHEST, preferred_element_type=jnp.float32
        )
        gram = one if gram is None else gram + one
        cross = two if cross is None else cross + two
    row_id = lax.broadcasted_iota(jnp.int32, (ROWS, order), 0)
    lane_id = lax.broadcasted_iota(jnp.int32, (ROWS, order), 1)
    blocks = order // ROWS
    tableau = [
        gram[k * ROWS : (k + 1) * ROWS, :]
        + jnp.where(lane_id == row_id + k * ROWS, damping, 0.0)
        for k in range(blocks)
    ]
    tableau += [cross[k : k + ROWS, :] for k in range(0, len(turns) * members, ROWS)]

    def lanes_of(value, at):
        return jnp.broadcast_to(value[:, at : at + 1], (ROWS, order))

    def row_of(value, at):
        return jnp.broadcast_to(value[at : at + 1, :], (ROWS, order))

    for block in range(blocks):
        base = block * ROWS
        inside = jnp.logical_and(lane_id >= base, lane_id < base + ROWS)
        band = tableau[block]
        column = [lanes_of(band, base + q) for q in range(ROWS)]
        band = jnp.where(inside, jnp.where(lane_id == row_id + base, -1.0, 0.0), band)
        for q in range(ROWS):
            here = row_id == q
            inverse = 1.0 / row_of(column[q], q)
            pivot_row = row_of(band, q) * inverse
            band = jnp.where(here, pivot_row, band - column[q] * pivot_row)
            for j in range(q + 1, ROWS):
                factor = row_of(column[j], q) * inverse
                column[j] = jnp.where(here, factor, column[j] - column[q] * factor)
        rows = [row_of(band, q) for q in range(ROWS)]
        for other in range(block + 1, len(tableau)):
            value = tableau[other]
            products = [lanes_of(value, base + q) * rows[q] for q in range(ROWS)]
            while len(products) > 1:
                products = [a + b for a, b in zip(products[::2], products[1::2])]
            tableau[other] = jnp.where(inside, 0.0, value) - products[0]
    solved_ref[...] = jnp.concatenate(tableau[blocks:], axis=0).astype(jnp.bfloat16)


def apply_kernel(norm_scale, lines, solved_ref, *refs):
    outs = refs[len(refs) // 2 :]
    part_refs = refs[: len(refs) // 2][::-1]
    solved = solved_ref[...]
    pair, order = solved.shape
    wide = order * lines
    spread = (
        lax.broadcasted_iota(jnp.int32, (order, wide), 1) // lines
        == lax.broadcasted_iota(jnp.int32, (order, wide), 0)
    ).astype(jnp.bfloat16)
    stretched = jnp.dot(solved, spread, preferred_element_type=jnp.float32)
    on_line = lax.broadcasted_iota(jnp.int32, (lines, wide), 1) % lines == (
        lax.broadcasted_iota(jnp.int32, (lines, wide), 0)
    )
    weights = jnp.concatenate(
        [
            jnp.where(on_line, jnp.broadcast_to(stretched[j : j + 1, :], (lines, wide)), 0.0)
            for j in range(pair)
        ],
        axis=0,
    ).astype(jnp.bfloat16)
    change, start = None, 0
    for ref in part_refs:
        deep = ref.shape[0]
        part = jnp.dot(
            weights[:, start : start + deep], ref[...], preferred_element_type=jnp.float32
        )
        change = part if change is None else change + part
        start += deep
    change = change * norm_scale
    rows = outs[0].shape[0]
    for turn, ref in enumerate(outs):
        ref[...] = change[turn * rows : (turn + 1) * rows].astype(ref.dtype)


def merge_kernel(field_ref, *refs):
    pieces, out_ref = refs[:-1][::-1], refs[-1]
    share = pieces[0].shape[1]
    mine = jnp.bitwise_and(lax.axis_index("mem"), len(pieces) - 1)
    for turn, piece in enumerate(pieces):
        start = pl.multiple_of(jnp.bitwise_xor(mine, turn) * share, LANES)
        columns = pl.ds(start, share)
        out_ref[:, columns] = field_ref[:, columns] + piece[...].astype(jnp.float32)


def body(
    logarithmic_diffusivity,
    starting_warmth,
    thermal_supply,
    probe_positions,
    recorded_temps,
    probe_error_sigma,
    perturb_draws,
):
    members, lines, width = logarithmic_diffusivity.shape
    owners, slabs = lax.axis_size("mem"), lax.axis_size("sp")
    order = members * owners
    norm_scale = 1.0 / math.sqrt(order - 1)
    probes = probe_positions.shape[0]

    mine = lax.axis_index("mem").astype(jnp.int32)
    turns = range(math.gcd(owners, 4))
    share = width // len(turns)

    def across(value, bit):
        return lax.ppermute(value, "mem", [(i, i ^ bit) for i in range(owners)])

    field_flat = logarithmic_diffusivity.reshape(members * lines, width)
    field_round = field_flat.astype(jnp.bfloat16)
    parts, offsets = [field_round], [0]
    bits = []
    while len(turns) << len(bits) < owners:
        bits.insert(0, len(turns) << len(bits))

    def exchange(parts, offsets, bit):
        held = jnp.concatenate(parts, axis=0)
        return [held, across(held, bit)], offsets + [offset ^ bit for offset in offsets]

    for bit in bits[:2]:
        offsets = offsets + [offset ^ bit for offset in reversed(offsets)]
    parts = [across(field_round, offset) if offset else field_round for offset in offsets]

    start_tied, parts[0] = lax.optimization_barrier((starting_warmth, parts[0]))
    edges = jnp.concatenate([field_flat, start_tied, thermal_supply], axis=0)
    if slabs == 2:
        up = down = lax.ppermute(edges, "sp", [(0, 1), (1, 0)])
    else:
        up = lax.ppermute(edges, "sp", [(i, i + 1) for i in range(slabs - 1)])
        down = lax.ppermute(edges, "sp", [(i + 1, i) for i in range(slabs - 1)])
    vmem = pl.BlockSpec(memory_space=pltpu.VMEM)
    smem = pl.BlockSpec(memory_space=pltpu.SMEM)
    anywhere = pl.BlockSpec(memory_space=pl.ANY)
    window = lines + 2 * STEPS
    devices = owners * slabs
    beside = [up] if slabs == 2 else [up, down]

    def kernel(columns_hbm, field_ref, *refs):
        neighbours, rest = refs[: len(beside)], refs[len(beside) :]
        above = neighbours[0] if len(beside) == 2 else None
        conduct_kernel(columns_hbm, field_ref, above, neighbours[-1], *rest)

    predicted, payload = pl.pallas_call(
        kernel,
        out_shape=(
            jax.ShapeDtypeStruct((members, probes), jnp.float32),
            jax.ShapeDtypeStruct((devices, members, 2 * probes), jnp.float32),
        ),
        in_specs=[anywhere] + [vmem] * (3 + len(beside)) + [anywhere] * 3,
        out_specs=(vmem, vmem),
        scratch_shapes=[
            pltpu.VMEM((window, members, width), jnp.float32),
            pltpu.VMEM((window, members, width), jnp.float32),
            pltpu.VMEM((window, width), jnp.float32),
            pltpu.SMEM((probes,), jnp.int32),
            pltpu.VMEM((1, probes), jnp.float32),
            pltpu.VMEM((1, probes), jnp.float32),
            pltpu.VMEM((members, probes), jnp.float32),
            pltpu.SemaphoreType.DMA((4,)),
        ],
        compiler_params=pltpu.CompilerParams(vmem_limit_bytes=24 * 1024 * 1024),
        cost_estimate=pl.CostEstimate(
            flops=30 * STEPS * window * members * width,
            bytes_accessed=4 * 3 * members * lines * width,
            transcendentals=STEPS * window * members * width,
        ),
        name="conduct",
    )(
        probe_positions,
        field_flat,
        *beside,
        starting_warmth,
        thermal_supply,
        recorded_temps[None, :],
        probe_error_sigma[None, :],
        perturb_draws,
    )
    _, *parts = lax.optimization_barrier((payload, *parts))
    for bit in bits[2:]:
        parts, offsets = exchange(parts, offsets, bit)
    everyone = lax.all_to_all(payload, ("mem", "sp"), 0, 0, tiled=True)
    held = jnp.concatenate(parts, axis=0)
    parts = []
    for turn in reversed(turns):
        columns = ((mine ^ turn) & (len(turns) - 1)) * share
        piece = lax.dynamic_slice_in_dim(held, columns, share, 1)
        parts.insert(0, across(piece, turn) if turn else piece)
    offsets = [offset ^ turn for turn in turns for offset in offsets]
    if order <= LANES:
        solved = pl.pallas_call(
            lambda *refs: solve_kernel(norm_scale, slabs, offsets, turns, *refs),
            out_shape=jax.ShapeDtypeStruct((len(turns) * members, order), jnp.bfloat16),
            in_specs=[vmem],
            out_specs=vmem,
            compiler_params=pltpu.CompilerParams(vmem_limit_bytes=16 * 1024 * 1024),
            cost_estimate=pl.CostEstimate(
                flops=2 * order * order * order,
                bytes_accessed=4 * devices * members * 2 * probes,
                transcendentals=0,
            ),
            name="solve",
        )(everyone)
    else:
        owner = mine ^ jnp.array(offsets, jnp.int32)
        split = everyone.reshape(owners, slabs, members, 2, probes)[owner]
        split = split.transpose(3, 0, 2, 1, 4).reshape(2, order, slabs * probes)
        normal = split[0]
        misfit = split[1].reshape(owners, members, -1)
        misfit = jnp.concatenate([misfit[offsets.index(turn)] for turn in turns], axis=0)
        scaled = (jnp.mean(normal, axis=0, keepdims=True) - normal) * norm_scale
        gram_matrix = jnp.dot(
            scaled, scaled.T, precision=lax.Precision.HIGHEST, preferred_element_type=jnp.float32
        ) + damping * jnp.eye(order, dtype=jnp.float32)
        cross_term = jnp.dot(
            scaled, misfit.T, precision=lax.Precision.HIGHEST, preferred_element_type=jnp.float32
        )
        solved = eliminate(gram_matrix, cross_term).T.astype(jnp.bfloat16)
    rows = members * lines
    pieces = pl.pallas_call(
        lambda *refs: apply_kernel(norm_scale, lines, *refs),
        out_shape=[
            jax.ShapeDtypeStruct((rows, share), jnp.bfloat16 if turn else jnp.float32)
            for turn in turns
        ],
        in_specs=[vmem] * (1 + len(parts)),
        out_specs=[vmem] * len(turns),
        compiler_params=pltpu.CompilerParams(vmem_limit_bytes=40 * 1024 * 1024),
        cost_estimate=pl.CostEstimate(
            flops=2 * rows * order * lines * width,
            bytes_accessed=2 * order * lines * share,
            transcendentals=0,
        ),
        name="apply",
    )(solved, *parts[::-1])
    pieces = [
        across(pieces[turn], turn) if turn else pieces[turn] for turn in reversed(turns)
    ][::-1]
    revised = pl.pallas_call(
        merge_kernel,
        out_shape=jax.ShapeDtypeStruct((rows, width), jnp.float32),
        in_specs=[vmem] * (1 + len(turns)),
        out_specs=vmem,
        compiler_params=pltpu.CompilerParams(vmem_limit_bytes=8 * 1024 * 1024),
        name="merge",
    )(field_flat, *pieces[::-1])
    return (revised.reshape(logarithmic_diffusivity.shape), predicted)


def solution(mesh):
    in_specs = (
        P("mem", "sp", None),
        P("sp", None),
        P("sp", None),
        P("sp"),
        P("sp"),
        P("sp"),
        P("mem", "sp"),
    )
    out_specs = (P("mem", "sp", None), P("mem", "sp"))
    return jax.shard_map(body, mesh=mesh, in_specs=in_specs, out_specs=out_specs, check_vma=False)
```

```python
import math

import jax
import jax.numpy as jnp
from jax import lax
from jax.experimental import pallas as pl
from jax.experimental.pallas import tpu as pltpu
from jax.sharding import PartitionSpec as P

STEPS = 4


time_step = 0.06
damping = 2.0
block_width = 16
LANES = 128
ROWS = 8


def invert_block(matrix):
    augmented = jnp.concatenate([matrix, jnp.eye(block_width, dtype=matrix.dtype)], axis=1)
    for place in range(block_width):
        pivot_row = augmented[place] / augmented[place, place]
        augmented = augmented - augmented[:, place : place + 1] * pivot_row[None, :]
        augmented = jnp.concatenate(
            [augmented[:place], pivot_row[None, :], augmented[place + 1 :]], axis=0
        )
    return augmented[:, block_width:]


def eliminate(gram_matrix, cross_term):
    order = gram_matrix.shape[0]
    tableau = jnp.concatenate([gram_matrix, cross_term], axis=1)

    def one_turn(block_number, tableau):
        first_row = (block_number * block_width).astype(jnp.int32)
        row_band = lax.dynamic_slice_in_dim(tableau, first_row, block_width, 0)
        pivot_block = lax.dynamic_slice_in_dim(row_band, first_row, block_width, 1)
        inverse = invert_block(pivot_block)
        scaled_rows = jnp.dot(
            inverse, row_band, precision=lax.Precision.HIGHEST, preferred_element_type=tableau.dtype
        )
        column = lax.dynamic_slice_in_dim(tableau, first_row, block_width, 1)
        tableau = tableau - jnp.dot(
            column,
            scaled_rows,
            precision=lax.Precision.HIGHEST,
            preferred_element_type=tableau.dtype,
        )
        return lax.dynamic_update_slice_in_dim(tableau, scaled_rows, first_row, 0)

    tableau = lax.fori_loop(0, order // block_width, one_turn, tableau)
    return tableau[:, order:]


def conduct_kernel(
    columns_hbm,
    field_ref,
    up_ref,
    down_ref,
    start_ref,
    source_ref,
    recorded_hbm,
    sigma_hbm,
    draws_hbm,
    predicted_ref,
    payload_ref,
    warmth,
    half_exp,
    supply,
    columns_ref,
    recorded_ref,
    sigma_ref,
    draws_ref,
    sems,
):
    lines = start_ref.shape[0]
    copies = [
        pltpu.make_async_copy(source, target, sems.at[k])
        for k, (source, target) in enumerate(
            (
                (columns_hbm, columns_ref),
                (recorded_hbm, recorded_ref),
                (sigma_hbm, sigma_ref),
                (draws_hbm, draws_ref),
            )
        )
    ]
    for copy in copies:
        copy.start()
    members, width = predicted_ref.shape[0], start_ref.shape[1]
    tiles = width // LANES
    top = 0 if up_ref is None else STEPS
    window = top + lines + STEPS
    lane = lax.broadcasted_iota(jnp.int32, (members, LANES), 1)
    first, last = lane == 0, lane == LANES - 1

    slab = lax.axis_index("sp")
    def by_rows(ref):
        return jnp.swapaxes(ref[0 : members * lines, :].reshape(members, lines, width), 0, 1)

    def turn(line):
        return jnp.where(slab > 0, lines - 1 - line, line)

    if top:
        above, below = slab > 0, slab < lax.axis_size("sp") - 1
        sides = (
            (0, up_ref, lines - STEPS, STEPS, above),
            (STEPS, field_ref, 0, lines, None),
            (STEPS + lines, down_ref, 0, STEPS, below),
        )
        turned = {id(ref): by_rows(ref) for ref in (field_ref, up_ref, down_ref)}
        for row, ref, line, count, inside in sides:
            coefficient = turned[id(ref)]
            for step in range(count):
                part = coefficient[line + step]
                if inside is not None:
                    part = jnp.where(inside, part, 0.0)
                half_exp[row + step] = 0.5 * jnp.exp(part)
        for row, ref, line, count, inside in sides:
            for step in range(count):
                if inside is None:
                    heat = start_ref[pl.ds(line + step, 1), :]
                else:
                    heat = jnp.where(inside, ref[pl.ds(members * lines + line + step, 1), :], 0.0)
                warmth[row + step] = jnp.broadcast_to(heat, (members, width))
            if inside is None:
                supply[pl.ds(row, count), :] = source_ref[...]
            else:
                base = (members + 1) * lines + line
                supply[pl.ds(row, count), :] = ref[pl.ds(base, count), :]
    else:
        own, other = by_rows(field_ref), by_rows(down_ref)
        for line in range(lines):
            half_exp[turn(line)] = 0.5 * jnp.exp(own[line])
        for step in range(STEPS):
            part = jnp.where(slab > 0, other[lines - 1 - step], other[step])
            half_exp[lines + step] = 0.5 * jnp.exp(part)
        for row in range(lines + STEPS):
            if row < lines:
                heat = start_ref[pl.ds(turn(row), 1), :]
                source = source_ref[pl.ds(turn(row), 1), :]
            else:
                line = members * lines + turn(row - lines)
                heat = down_ref[pl.ds(line, 1), :]
                source = down_ref[pl.ds(line + lines, 1), :]
            warmth[row] = jnp.broadcast_to(heat, (members, width))
            supply[pl.ds(row, 1), :] = source

    def cut(value):
        return [value[:, k * LANES : (k + 1) * LANES] for k in range(tiles)]

    def conductivity(row, warm):
        half = cut(half_exp[row])
        return [h * (1.0 + 0.5 * jnp.tanh(t)) for h, t in zip(half, warm)]

    half_one = jnp.full((members, LANES), 0.5, jnp.float32)
    zero = jnp.zeros((members, LANES), jnp.float32)

    for step in range(STEPS):
        low, high = step + 1 if top else 0, window - 1 - step
        if top:
            t_up = cut(warmth[low - 1])
            c_up = conductivity(low - 1, t_up)
        else:
            t_up, c_up = [zero] * tiles, [half_one] * tiles
        t_here = cut(warmth[low])
        c_here = conductivity(low, t_here)
        flow_up = [(a + b) * (y - x) for a, b, x, y in zip(c_up, c_here, t_up, t_here)]

        def one_row(row, carry):
            t, c, up = carry
            t_next = cut(warmth[row + 1])
            c_next = conductivity(row + 1, t_next)
            down = [(a + b) * (y - x) for a, b, x, y in zip(c, c_next, t, t_next)]
            t_roll = [pltpu.roll(x, LANES - 1, 1) for x in t] + [zero]
            c_roll = [pltpu.roll(x, LANES - 1, 1) for x in c] + [half_one]
            right = []
            for k in range(tiles):
                t_right = jnp.where(last, t_roll[k + 1], t_roll[k])
                c_right = jnp.where(last, c_roll[k + 1], c_roll[k])
                right.append((c[k] + c_right) * (t_right - t[k]))
            back = [pltpu.roll(x, 1, 1) for x in right]
            keep = 1.0
            if top:
                outside = jnp.logical_or(
                    jnp.logical_and(row < STEPS, jnp.logical_not(above)),
                    jnp.logical_and(row >= STEPS + lines, jnp.logical_not(below)),
                )
                keep = jnp.where(outside, 0.0, 1.0)
            source = supply[pl.ds(row, 1), :]
            for k in range(tiles):
                edge = (c[0] + 0.5) * t[0] if k == 0 else back[k - 1]
                left = jnp.where(first, edge, back[k])
                inflow = (down[k] - up[k]) + (right[k] - left)
                heat = source[:, k * LANES : (k + 1) * LANES]
                fresh = t[k] + time_step * (inflow + heat)
                warmth[row, :, k * LANES : (k + 1) * LANES] = keep * fresh if top else fresh
            return t_next, c_next, down

        lax.fori_loop(low, high, one_row, (t_here, c_here, flow_up), unroll=True)

    for copy in copies:
        copy.wait()
    probes = predicted_ref.shape[1]
    lane_probe = lax.broadcasted_iota(jnp.int32, (members, LANES), 1)
    picked = [zero for _ in range(4)]
    for probe in range(probes):
        line = probe * lines // probes
        column = columns_ref[probe] - line * width
        offset = jnp.bitwise_and(column, LANES - 1)
        shift = jnp.bitwise_and(probe - offset, LANES - 1)
        start = pl.multiple_of(column - offset, LANES)
        place = STEPS + line if top else turn(line)
        values = warmth[place, :, pl.ds(start, LANES)]
        moved = pltpu.roll(values, shift, 1)
        picked[probe % 4] = jnp.where(lane_probe == probe, moved, picked[probe % 4])
    total = (picked[0] + picked[1]) + (picked[2] + picked[3])
    predicted = total[:, :probes]
    predicted_ref[...] = predicted
    normal = (recorded_ref[...] - predicted) / sigma_ref[...]
    payload = jnp.concatenate([normal, normal + draws_ref[...]], axis=1)
    for device in range(payload_ref.shape[0]):
        payload_ref[device] = payload


def solve_kernel(norm_scale, slabs, offsets, turns, payload_ref, solved_ref):
    members, probes = payload_ref.shape[1], payload_ref.shape[2] // 2
    order = len(offsets) * members
    mine = lax.axis_index("mem")
    dims = (((1,), (1,)), ((), ()))
    normals, misfits = [], []
    for slab in range(slabs):
        blocks = [
            payload_ref[jnp.bitwise_xor(mine, offset) * slabs + slab] for offset in offsets
        ]
        normals.append(jnp.concatenate([block[:, :probes] for block in blocks], axis=0))
        misfits += [
            jnp.concatenate([blocks[offsets.index(turn)][:, probes:] for turn in turns], axis=0)
        ]
    normal, misfit = jnp.concatenate(normals, axis=1), jnp.concatenate(misfits, axis=1)
    center = jnp.sum(normal, axis=0, keepdims=True) * (1.0 / order)
    scaled = (center - normal) * norm_scale
    both = lax.dot_general(
        jnp.concatenate([scaled, misfit], axis=0),
        scaled,
        dims,
        precision=lax.Precision.HIGHEST,
        preferred_element_type=jnp.float32,
    )
    gram, cross = both[:order], both[order:]
    row_id = lax.broadcasted_iota(jnp.int32, (ROWS, order), 0)
    lane_id = lax.broadcasted_iota(jnp.int32, (ROWS, order), 1)
    blocks = order // ROWS
    tableau = [
        gram[k * ROWS : (k + 1) * ROWS, :]
        + jnp.where(lane_id == row_id + k * ROWS, damping, 0.0)
        for k in range(blocks)
    ]
    tableau += [cross[k : k + ROWS, :] for k in range(0, len(turns) * members, ROWS)]

    def lanes_of(value, at):
        return jnp.broadcast_to(value[:, at : at + 1], (ROWS, order))

    def row_of(value, at):
        return jnp.broadcast_to(value[at : at + 1, :], (ROWS, order))

    for block in range(blocks):
        base = block * ROWS
        inside = jnp.logical_and(lane_id >= base, lane_id < base + ROWS)
        band = tableau[block]
        column = [lanes_of(band, base + q) for q in range(ROWS)]
        band = jnp.where(inside, jnp.where(lane_id == row_id + base, -1.0, 0.0), band)
        for q in range(ROWS):
            here = row_id == q
            inverse = 1.0 / row_of(column[q], q)
            pivot_row = row_of(band, q) * inverse
            band = jnp.where(here, pivot_row, band - column[q] * pivot_row)
            for j in range(q + 1, ROWS):
                factor = row_of(column[j], q) * inverse
                column[j] = jnp.where(here, factor, column[j] - column[q] * factor)
        rows = [row_of(band, q) for q in range(ROWS)]
        for other in range(block + 1, len(tableau)):
            value = tableau[other]
            products = [lanes_of(value, base + q) * rows[q] for q in range(ROWS)]
            while len(products) > 1:
                products = [a + b for a, b in zip(products[::2], products[1::2])]
            tableau[other] = jnp.where(inside, 0.0, value) - products[0]
    solved_ref[...] = jnp.concatenate(tableau[blocks:], axis=0).astype(jnp.bfloat16)


def apply_kernel(norm_scale, lines, solved_ref, *refs):
    outs = refs[len(refs) // 2 :]
    part_refs = refs[: len(refs) // 2][::-1]
    solved = solved_ref[...]
    pair, order = solved.shape
    wide = order * lines
    spread = (
        lax.broadcasted_iota(jnp.int32, (order, wide), 1) // lines
        == lax.broadcasted_iota(jnp.int32, (order, wide), 0)
    ).astype(jnp.bfloat16)
    stretched = jnp.dot(solved, spread, preferred_element_type=jnp.float32)
    on_line = lax.broadcasted_iota(jnp.int32, (lines, wide), 1) % lines == (
        lax.broadcasted_iota(jnp.int32, (lines, wide), 0)
    )
    weights = jnp.concatenate(
        [
            jnp.where(on_line, jnp.broadcast_to(stretched[j : j + 1, :], (lines, wide)), 0.0)
            for j in range(pair)
        ],
        axis=0,
    ).astype(jnp.bfloat16)
    change, start = None, 0
    for ref in part_refs:
        deep = ref.shape[0]
        part = jnp.dot(
            weights[:, start : start + deep], ref[...], preferred_element_type=jnp.float32
        )
        change = part if change is None else change + part
        start += deep
    change = change * norm_scale
    rows = outs[0].shape[0]
    for turn, ref in enumerate(outs):
        ref[...] = change[turn * rows : (turn + 1) * rows].astype(ref.dtype)


def merge_kernel(field_ref, *refs):
    pieces, out_ref = refs[:-1][::-1], refs[-1]
    share = pieces[0].shape[1]
    mine = jnp.bitwise_and(lax.axis_index("mem"), len(pieces) - 1)
    for turn, piece in enumerate(pieces):
        start = pl.multiple_of(jnp.bitwise_xor(mine, turn) * share, LANES)
        columns = pl.ds(start, share)
        out_ref[:, columns] = field_ref[:, columns] + piece[...].astype(jnp.float32)


def body(
    logarithmic_diffusivity,
    starting_warmth,
    thermal_supply,
    probe_positions,
    recorded_temps,
    probe_error_sigma,
    perturb_draws,
):
    members, lines, width = logarithmic_diffusivity.shape
    owners, slabs = lax.axis_size("mem"), lax.axis_size("sp")
    order = members * owners
    norm_scale = 1.0 / math.sqrt(order - 1)
    probes = probe_positions.shape[0]

    mine = lax.axis_index("mem").astype(jnp.int32)
    turns = range(math.gcd(owners, 4))
    share = width // len(turns)

    def across(value, bit):
        return lax.ppermute(value, "mem", [(i, i ^ bit) for i in range(owners)])

    field_flat = logarithmic_diffusivity.reshape(members * lines, width)
    field_round = field_flat.astype(jnp.bfloat16)
    parts, offsets = [field_round], [0]
    bits = []
    while len(turns) << len(bits) < owners:
        bits.insert(0, len(turns) << len(bits))

    def exchange(parts, offsets, bit):
        held = jnp.concatenate(parts, axis=0)
        return [held, across(held, bit)], offsets + [offset ^ bit for offset in offsets]

    for bit in bits[:2]:
        offsets = offsets + [offset ^ bit for offset in reversed(offsets)]
    parts = [across(field_round, offset) if offset else field_round for offset in offsets]

    start_tied, parts[0] = lax.optimization_barrier((starting_warmth, parts[0]))
    edges = jnp.concatenate([field_flat, start_tied, thermal_supply], axis=0)
    if slabs == 2:
        up = down = lax.ppermute(edges, "sp", [(0, 1), (1, 0)])
    else:
        up = lax.ppermute(edges, "sp", [(i, i + 1) for i in range(slabs - 1)])
        down = lax.ppermute(edges, "sp", [(i + 1, i) for i in range(slabs - 1)])
    vmem = pl.BlockSpec(memory_space=pltpu.VMEM)
    smem = pl.BlockSpec(memory_space=pltpu.SMEM)
    anywhere = pl.BlockSpec(memory_space=pl.ANY)
    window = lines + 2 * STEPS
    devices = owners * slabs
    beside = [up] if slabs == 2 else [up, down]

    def kernel(columns_hbm, field_ref, *refs):
        neighbours, rest = refs[: len(beside)], refs[len(beside) :]
        above = neighbours[0] if len(beside) == 2 else None
        conduct_kernel(columns_hbm, field_ref, above, neighbours[-1], *rest)

    predicted, payload = pl.pallas_call(
        kernel,
        out_shape=(
            jax.ShapeDtypeStruct((members, probes), jnp.float32),
            jax.ShapeDtypeStruct((devices, members, 2 * probes), jnp.float32),
        ),
        in_specs=[anywhere] + [vmem] * (3 + len(beside)) + [anywhere] * 3,
        out_specs=(vmem, vmem),
        scratch_shapes=[
            pltpu.VMEM((window, members, width), jnp.float32),
            pltpu.VMEM((window, members, width), jnp.float32),
            pltpu.VMEM((window, width), jnp.float32),
            pltpu.SMEM((probes,), jnp.int32),
            pltpu.VMEM((1, probes), jnp.float32),
            pltpu.VMEM((1, probes), jnp.float32),
            pltpu.VMEM((members, probes), jnp.float32),
            pltpu.SemaphoreType.DMA((4,)),
        ],
        compiler_params=pltpu.CompilerParams(vmem_limit_bytes=24 * 1024 * 1024),
        cost_estimate=pl.CostEstimate(
            flops=30 * STEPS * window * members * width,
            bytes_accessed=4 * 3 * members * lines * width,
            transcendentals=STEPS * window * members * width,
        ),
        name="conduct",
    )(
        probe_positions,
        field_flat,
        *beside,
        starting_warmth,
        thermal_supply,
        recorded_temps[None, :],
        probe_error_sigma[None, :],
        perturb_draws,
    )
    _, *parts = lax.optimization_barrier((payload, *parts))
    for bit in bits[2:]:
        parts, offsets = exchange(parts, offsets, bit)
    everyone = lax.all_to_all(payload, ("mem", "sp"), 0, 0, tiled=True)
    held = jnp.concatenate(parts, axis=0)
    parts = []
    for turn in reversed(turns):
        columns = ((mine ^ turn) & (len(turns) - 1)) * share
        piece = lax.dynamic_slice_in_dim(held, columns, share, 1)
        parts.insert(0, across(piece, turn) if turn else piece)
    offsets = [offset ^ turn for turn in turns for offset in offsets]
    if order <= LANES:
        solved = pl.pallas_call(
            lambda *refs: solve_kernel(norm_scale, slabs, offsets, turns, *refs),
            out_shape=jax.ShapeDtypeStruct((len(turns) * members, order), jnp.bfloat16),
            in_specs=[vmem],
            out_specs=vmem,
            compiler_params=pltpu.CompilerParams(vmem_limit_bytes=16 * 1024 * 1024),
            cost_estimate=pl.CostEstimate(
                flops=2 * order * order * order,
                bytes_accessed=4 * devices * members * 2 * probes,
                transcendentals=0,
            ),
            name="solve",
        )(everyone)
    else:
        owner = mine ^ jnp.array(offsets, jnp.int32)
        split = everyone.reshape(owners, slabs, members, 2, probes)[owner]
        split = split.transpose(3, 0, 2, 1, 4).reshape(2, order, slabs * probes)
        normal = split[0]
        misfit = split[1].reshape(owners, members, -1)
        misfit = jnp.concatenate([misfit[offsets.index(turn)] for turn in turns], axis=0)
        scaled = (jnp.mean(normal, axis=0, keepdims=True) - normal) * norm_scale
        gram_matrix = jnp.dot(
            scaled, scaled.T, precision=lax.Precision.HIGHEST, preferred_element_type=jnp.float32
        ) + damping * jnp.eye(order, dtype=jnp.float32)
        cross_term = jnp.dot(
            scaled, misfit.T, precision=lax.Precision.HIGHEST, preferred_element_type=jnp.float32
        )
        solved = eliminate(gram_matrix, cross_term).T.astype(jnp.bfloat16)
    rows = members * lines
    pieces = pl.pallas_call(
        lambda *refs: apply_kernel(norm_scale, lines, *refs),
        out_shape=[
            jax.ShapeDtypeStruct((rows, share), jnp.bfloat16 if turn else jnp.float32)
            for turn in turns
        ],
        in_specs=[vmem] * (1 + len(parts)),
        out_specs=[vmem] * len(turns),
        compiler_params=pltpu.CompilerParams(vmem_limit_bytes=40 * 1024 * 1024),
        cost_estimate=pl.CostEstimate(
            flops=2 * rows * order * lines * width,
            bytes_accessed=2 * order * lines * share,
            transcendentals=0,
        ),
        name="apply",
    )(solved, *parts[::-1])
    pieces = [
        across(pieces[turn], turn) if turn else pieces[turn] for turn in reversed(turns)
    ][::-1]
    revised = pl.pallas_call(
        merge_kernel,
        out_shape=jax.ShapeDtypeStruct((rows, width), jnp.float32),
        in_specs=[vmem] * (1 + len(turns)),
        out_specs=vmem,
        compiler_params=pltpu.CompilerParams(vmem_limit_bytes=8 * 1024 * 1024),
        name="merge",
    )(field_flat, *pieces[::-1])
    return (revised.reshape(logarithmic_diffusivity.shape), predicted)


def solution(mesh):
    in_specs = (
        P("mem", "sp", None),
        P("sp", None),
        P("sp", None),
        P("sp"),
        P("sp"),
        P("sp"),
        P("mem", "sp"),
    )
    out_specs = (P("mem", "sp", None), P("mem", "sp"))
    return jax.shard_map(body, mesh=mesh, in_specs=in_specs, out_specs=out_specs, check_vma=False)
```

```python
import math

import jax
import jax.numpy as jnp
from jax import lax
from jax.experimental import pallas as pl
from jax.experimental.pallas import tpu as pltpu
from jax.sharding import PartitionSpec as P

STEPS = 4


time_step = 0.06
damping = 2.0
block_width = 16
LANES = 128
ROWS = 8


def invert_block(matrix):
    augmented = jnp.concatenate([matrix, jnp.eye(block_width, dtype=matrix.dtype)], axis=1)
    for place in range(block_width):
        pivot_row = augmented[place] / augmented[place, place]
        augmented = augmented - augmented[:, place : place + 1] * pivot_row[None, :]
        augmented = jnp.concatenate(
            [augmented[:place], pivot_row[None, :], augmented[place + 1 :]], axis=0
        )
    return augmented[:, block_width:]


def eliminate(gram_matrix, cross_term):
    order = gram_matrix.shape[0]
    tableau = jnp.concatenate([gram_matrix, cross_term], axis=1)

    def one_turn(block_number, tableau):
        first_row = (block_number * block_width).astype(jnp.int32)
        row_band = lax.dynamic_slice_in_dim(tableau, first_row, block_width, 0)
        pivot_block = lax.dynamic_slice_in_dim(row_band, first_row, block_width, 1)
        inverse = invert_block(pivot_block)
        scaled_rows = jnp.dot(
            inverse, row_band, precision=lax.Precision.HIGHEST, preferred_element_type=tableau.dtype
        )
        column = lax.dynamic_slice_in_dim(tableau, first_row, block_width, 1)
        tableau = tableau - jnp.dot(
            column,
            scaled_rows,
            precision=lax.Precision.HIGHEST,
            preferred_element_type=tableau.dtype,
        )
        return lax.dynamic_update_slice_in_dim(tableau, scaled_rows, first_row, 0)

    tableau = lax.fori_loop(0, order // block_width, one_turn, tableau)
    return tableau[:, order:]


def conduct_kernel(
    columns_hbm,
    field_ref,
    up_ref,
    down_ref,
    start_ref,
    source_ref,
    recorded_hbm,
    sigma_hbm,
    draws_hbm,
    predicted_ref,
    payload_ref,
    warmth,
    half_exp,
    supply,
    columns_ref,
    recorded_ref,
    sigma_ref,
    draws_ref,
    sems,
):
    lines = start_ref.shape[0]
    copies = [
        pltpu.make_async_copy(source, target, sems.at[k])
        for k, (source, target) in enumerate(
            (
                (columns_hbm, columns_ref),
                (recorded_hbm, recorded_ref),
                (sigma_hbm, sigma_ref),
                (draws_hbm, draws_ref),
            )
        )
    ]
    for copy in copies:
        copy.start()
    members, width = predicted_ref.shape[0], start_ref.shape[1]
    tiles = width // LANES
    top = 0 if up_ref is None else STEPS
    window = top + lines + STEPS
    lane = lax.broadcasted_iota(jnp.int32, (members, LANES), 1)
    first, last = lane == 0, lane == LANES - 1

    slab = lax.axis_index("sp")
    def by_rows(ref):
        return jnp.swapaxes(ref[0 : members * lines, :].reshape(members, lines, width), 0, 1)

    def turn(line):
        return jnp.where(slab > 0, lines - 1 - line, line)

    if top:
        above, below = slab > 0, slab < lax.axis_size("sp") - 1
        sides = (
            (0, up_ref, lines - STEPS, STEPS, above),
            (STEPS, field_ref, 0, lines, None),
            (STEPS + lines, down_ref, 0, STEPS, below),
        )
        turned = {id(ref): by_rows(ref) for ref in (field_ref, up_ref, down_ref)}
        for row, ref, line, count, inside in sides:
            coefficient = turned[id(ref)]
            for step in range(count):
                part = coefficient[line + step]
                if inside is not None:
                    part = jnp.where(inside, part, 0.0)
                half_exp[row + step] = 0.5 * jnp.exp(part)
        for row, ref, line, count, inside in sides:
            for step in range(count):
                if inside is None:
                    heat = start_ref[pl.ds(line + step, 1), :]
                else:
                    heat = jnp.where(inside, ref[pl.ds(members * lines + line + step, 1), :], 0.0)
                warmth[row + step] = jnp.broadcast_to(heat, (members, width))
            if inside is None:
                supply[pl.ds(row, count), :] = source_ref[...]
            else:
                base = (members + 1) * lines + line
                supply[pl.ds(row, count), :] = ref[pl.ds(base, count), :]
    else:
        own, other = by_rows(field_ref), by_rows(down_ref)
        for line in range(lines):
            half_exp[turn(line)] = 0.5 * jnp.exp(own[line])
        for step in range(STEPS):
            part = jnp.where(slab > 0, other[lines - 1 - step], other[step])
            half_exp[lines + step] = 0.5 * jnp.exp(part)
        for row in range(lines + STEPS):
            if row < lines:
                heat = start_ref[pl.ds(turn(row), 1), :]
                source = source_ref[pl.ds(turn(row), 1), :]
            else:
                line = members * lines + turn(row - lines)
                heat = down_ref[pl.ds(line, 1), :]
                source = down_ref[pl.ds(line + lines, 1), :]
            warmth[row] = jnp.broadcast_to(heat, (members, width))
            supply[pl.ds(row, 1), :] = source

    def cut(value):
        return [value[:, k * LANES : (k + 1) * LANES] for k in range(tiles)]

    def conductivity(row, warm):
        half = cut(half_exp[row])
        return [h * (1.0 + 0.5 * jnp.tanh(t)) for h, t in zip(half, warm)]

    half_one = jnp.full((members, LANES), 0.5, jnp.float32)
    zero = jnp.zeros((members, LANES), jnp.float32)

    for step in range(STEPS):
        low, high = step + 1 if top else 0, window - 1 - step
        if top:
            t_up = cut(warmth[low - 1])
            c_up = conductivity(low - 1, t_up)
        else:
            t_up, c_up = [zero] * tiles, [half_one] * tiles
        t_here = cut(warmth[low])
        c_here = conductivity(low, t_here)
        flow_up = [(a + b) * (y - x) for a, b, x, y in zip(c_up, c_here, t_up, t_here)]

        def one_row(row, carry):
            t, c, up = carry
            t_next = cut(warmth[row + 1])
            c_next = conductivity(row + 1, t_next)
            down = [(a + b) * (y - x) for a, b, x, y in zip(c, c_next, t, t_next)]
            t_roll = [pltpu.roll(x, LANES - 1, 1) for x in t] + [zero]
            c_roll = [pltpu.roll(x, LANES - 1, 1) for x in c] + [half_one]
            right = []
            for k in range(tiles):
                t_right = jnp.where(last, t_roll[k + 1], t_roll[k])
                c_right = jnp.where(last, c_roll[k + 1], c_roll[k])
                right.append((c[k] + c_right) * (t_right - t[k]))
            back = [pltpu.roll(x, 1, 1) for x in right]
            keep = 1.0
            if top:
                outside = jnp.logical_or(
                    jnp.logical_and(row < STEPS, jnp.logical_not(above)),
                    jnp.logical_and(row >= STEPS + lines, jnp.logical_not(below)),
                )
                keep = jnp.where(outside, 0.0, 1.0)
            source = supply[pl.ds(row, 1), :]
            for k in range(tiles):
                edge = (c[0] + 0.5) * t[0] if k == 0 else back[k - 1]
                left = jnp.where(first, edge, back[k])
                inflow = (down[k] - up[k]) + (right[k] - left)
                heat = source[:, k * LANES : (k + 1) * LANES]
                fresh = t[k] + time_step * (inflow + heat)
                warmth[row, :, k * LANES : (k + 1) * LANES] = keep * fresh if top else fresh
            return t_next, c_next, down

        lax.fori_loop(low, high, one_row, (t_here, c_here, flow_up), unroll=True)

    for copy in copies:
        copy.wait()
    probes = predicted_ref.shape[1]
    lane_probe = lax.broadcasted_iota(jnp.int32, (members, LANES), 1)
    picked = [zero for _ in range(4)]
    for probe in range(probes):
        line = probe * lines // probes
        column = columns_ref[probe] - line * width
        offset = jnp.bitwise_and(column, LANES - 1)
        shift = jnp.bitwise_and(probe - offset, LANES - 1)
        start = pl.multiple_of(column - offset, LANES)
        place = STEPS + line if top else turn(line)
        values = warmth[place, :, pl.ds(start, LANES)]
        moved = pltpu.roll(values, shift, 1)
        picked[probe % 4] = jnp.where(lane_probe == probe, moved, picked[probe % 4])
    total = (picked[0] + picked[1]) + (picked[2] + picked[3])
    predicted = total[:, :probes]
    predicted_ref[...] = predicted
    normal = (recorded_ref[...] - predicted) / sigma_ref[...]
    payload = jnp.concatenate([normal, normal + draws_ref[...]], axis=1)
    for device in range(payload_ref.shape[0]):
        payload_ref[device] = payload


def solve_kernel(norm_scale, slabs, offsets, turns, payload_ref, solved_ref):
    members, probes = payload_ref.shape[1], payload_ref.shape[2] // 2
    order = len(offsets) * members
    mine = lax.axis_index("mem")
    dims = (((1,), (1,)), ((), ()))
    normals, misfits = [], []
    for slab in range(slabs):
        blocks = [
            payload_ref[jnp.bitwise_xor(mine, offset) * slabs + slab] for offset in offsets
        ]
        normals.append(jnp.concatenate([block[:, :probes] for block in blocks], axis=0))
        misfits += [
            jnp.concatenate([blocks[offsets.index(turn)][:, probes:] for turn in turns], axis=0)
        ]
    normal, misfit = jnp.concatenate(normals, axis=1), jnp.concatenate(misfits, axis=1)
    center = jnp.sum(normal, axis=0, keepdims=True) * (1.0 / order)
    scaled = (center - normal) * norm_scale
    both = lax.dot_general(
        jnp.concatenate([scaled, misfit], axis=0),
        scaled,
        dims,
        precision=lax.Precision.HIGHEST,
        preferred_element_type=jnp.float32,
    )
    gram, cross = both[:order], both[order:]
    row_id = lax.broadcasted_iota(jnp.int32, (ROWS, order), 0)
    lane_id = lax.broadcasted_iota(jnp.int32, (ROWS, order), 1)
    blocks = order // ROWS
    tableau = [
        gram[k * ROWS : (k + 1) * ROWS, :]
        + jnp.where(lane_id == row_id + k * ROWS, damping, 0.0)
        for k in range(blocks)
    ]
    tableau += [cross[k : k + ROWS, :] for k in range(0, len(turns) * members, ROWS)]

    def lanes_of(value, at):
        return jnp.broadcast_to(value[:, at : at + 1], (ROWS, order))

    def row_of(value, at):
        return jnp.broadcast_to(value[at : at + 1, :], (ROWS, order))

    for block in range(blocks):
        base = block * ROWS
        inside = jnp.logical_and(lane_id >= base, lane_id < base + ROWS)
        band = tableau[block]
        column = [lanes_of(band, base + q) for q in range(ROWS)]
        band = jnp.where(inside, jnp.where(lane_id == row_id + base, -1.0, 0.0), band)
        for q in range(ROWS):
            here = row_id == q
            inverse = 1.0 / row_of(column[q], q)
            pivot_row = row_of(band, q) * inverse
            band = jnp.where(here, pivot_row, band - column[q] * pivot_row)
            for j in range(q + 1, ROWS):
                factor = row_of(column[j], q) * inverse
                column[j] = jnp.where(here, factor, column[j] - column[q] * factor)
        rows = [row_of(band, q) for q in range(ROWS)]
        for other in range(block + 1, len(tableau)):
            value = tableau[other]
            products = [lanes_of(value, base + q) * rows[q] for q in range(ROWS)]
            while len(products) > 1:
                products = [a + b for a, b in zip(products[::2], products[1::2])]
            tableau[other] = jnp.where(inside, 0.0, value) - products[0]
    solved_ref[...] = jnp.concatenate(tableau[blocks:], axis=0).astype(jnp.bfloat16)


def apply_kernel(norm_scale, lines, solved_ref, *refs):
    outs = refs[len(refs) // 2 :]
    part_refs = refs[: len(refs) // 2][::-1]
    solved = solved_ref[...]
    pair, order = solved.shape
    wide = order * lines
    column = lax.broadcasted_iota(jnp.int32, (order, wide), 1)
    begin = lax.broadcasted_iota(jnp.int32, (order, wide), 0) * lines
    spread = jnp.logical_and(column >= begin, column < begin + lines).astype(jnp.bfloat16)
    stretched = jnp.dot(solved, spread, preferred_element_type=jnp.float32)
    on_line = lax.broadcasted_iota(jnp.int32, (lines, wide), 1) % lines == (
        lax.broadcasted_iota(jnp.int32, (lines, wide), 0)
    )
    weights = jnp.concatenate(
        [
            jnp.where(on_line, jnp.broadcast_to(stretched[j : j + 1, :], (lines, wide)), 0.0)
            for j in range(pair)
        ],
        axis=0,
    ).astype(jnp.bfloat16)
    change, start = None, 0
    for ref in part_refs:
        deep = ref.shape[0]
        part = jnp.dot(
            weights[:, start : start + deep], ref[...], preferred_element_type=jnp.float32
        )
        change = part if change is None else change + part
        start += deep
    change = change * norm_scale
    rows = outs[0].shape[0]
    for turn, ref in enumerate(outs):
        ref[...] = change[turn * rows : (turn + 1) * rows].astype(ref.dtype)


def merge_kernel(field_ref, *refs):
    pieces, out_ref = refs[:-1][::-1], refs[-1]
    share = pieces[0].shape[1]
    mine = jnp.bitwise_and(lax.axis_index("mem"), len(pieces) - 1)
    for turn, piece in enumerate(pieces):
        start = pl.multiple_of(jnp.bitwise_xor(mine, turn) * share, LANES)
        columns = pl.ds(start, share)
        out_ref[:, columns] = field_ref[:, columns] + piece[...].astype(jnp.float32)


def body(
    logarithmic_diffusivity,
    starting_warmth,
    thermal_supply,
    probe_positions,
    recorded_temps,
    probe_error_sigma,
    perturb_draws,
):
    members, lines, width = logarithmic_diffusivity.shape
    owners, slabs = lax.axis_size("mem"), lax.axis_size("sp")
    order = members * owners
    norm_scale = 1.0 / math.sqrt(order - 1)
    probes = probe_positions.shape[0]

    mine = lax.axis_index("mem").astype(jnp.int32)
    turns = range(math.gcd(owners, 4))
    share = width // len(turns)

    def across(value, bit):
        return lax.ppermute(value, "mem", [(i, i ^ bit) for i in range(owners)])

    field_flat = logarithmic_diffusivity.reshape(members * lines, width)
    field_round = field_flat.astype(jnp.bfloat16)
    parts, offsets = [field_round], [0]
    bits = []
    while len(turns) << len(bits) < owners:
        bits.insert(0, len(turns) << len(bits))

    def exchange(parts, offsets, bit):
        held = jnp.concatenate(parts, axis=0)
        return [held, across(held, bit)], offsets + [offset ^ bit for offset in offsets]

    for bit in bits[:2]:
        offsets = offsets + [offset ^ bit for offset in reversed(offsets)]
    parts = [across(field_round, offset) if offset else field_round for offset in offsets]

    start_tied, parts[0] = lax.optimization_barrier((starting_warmth, parts[0]))
    edges = jnp.concatenate([field_flat, start_tied, thermal_supply], axis=0)
    if slabs == 2:
        up = down = lax.ppermute(edges, "sp", [(0, 1), (1, 0)])
    else:
        up = lax.ppermute(edges, "sp", [(i, i + 1) for i in range(slabs - 1)])
        down = lax.ppermute(edges, "sp", [(i + 1, i) for i in range(slabs - 1)])
    vmem = pl.BlockSpec(memory_space=pltpu.VMEM)
    smem = pl.BlockSpec(memory_space=pltpu.SMEM)
    anywhere = pl.BlockSpec(memory_space=pl.ANY)
    window = lines + 2 * STEPS
    devices = owners * slabs
    beside = [up] if slabs == 2 else [up, down]

    def kernel(columns_hbm, field_ref, *refs):
        neighbours, rest = refs[: len(beside)], refs[len(beside) :]
        above = neighbours[0] if len(beside) == 2 else None
        conduct_kernel(columns_hbm, field_ref, above, neighbours[-1], *rest)

    predicted, payload = pl.pallas_call(
        kernel,
        out_shape=(
            jax.ShapeDtypeStruct((members, probes), jnp.float32),
            jax.ShapeDtypeStruct((devices, members, 2 * probes), jnp.float32),
        ),
        in_specs=[anywhere] + [vmem] * (3 + len(beside)) + [anywhere] * 3,
        out_specs=(vmem, vmem),
        scratch_shapes=[
            pltpu.VMEM((window, members, width), jnp.float32),
            pltpu.VMEM((window, members, width), jnp.float32),
            pltpu.VMEM((window, width), jnp.float32),
            pltpu.SMEM((probes,), jnp.int32),
            pltpu.VMEM((1, probes), jnp.float32),
            pltpu.VMEM((1, probes), jnp.float32),
            pltpu.VMEM((members, probes), jnp.float32),
            pltpu.SemaphoreType.DMA((4,)),
        ],
        compiler_params=pltpu.CompilerParams(vmem_limit_bytes=24 * 1024 * 1024),
        cost_estimate=pl.CostEstimate(
            flops=30 * STEPS * window * members * width,
            bytes_accessed=4 * 3 * members * lines * width,
            transcendentals=STEPS * window * members * width,
        ),
        name="conduct",
    )(
        probe_positions,
        field_flat,
        *beside,
        starting_warmth,
        thermal_supply,
        recorded_temps[None, :],
        probe_error_sigma[None, :],
        perturb_draws,
    )
    _, *parts = lax.optimization_barrier((payload, *parts))
    for bit in bits[2:]:
        parts, offsets = exchange(parts, offsets, bit)
    everyone = lax.all_to_all(payload, ("mem", "sp"), 0, 0, tiled=True)
    held = jnp.concatenate(parts, axis=0)
    parts = []
    for turn in reversed(turns):
        columns = ((mine ^ turn) & (len(turns) - 1)) * share
        piece = lax.dynamic_slice_in_dim(held, columns, share, 1)
        parts.insert(0, across(piece, turn) if turn else piece)
    offsets = [offset ^ turn for turn in turns for offset in offsets]
    if order <= LANES:
        solved = pl.pallas_call(
            lambda *refs: solve_kernel(norm_scale, slabs, offsets, turns, *refs),
            out_shape=jax.ShapeDtypeStruct((len(turns) * members, order), jnp.bfloat16),
            in_specs=[vmem],
            out_specs=vmem,
            compiler_params=pltpu.CompilerParams(vmem_limit_bytes=16 * 1024 * 1024),
            cost_estimate=pl.CostEstimate(
                flops=2 * order * order * order,
                bytes_accessed=4 * devices * members * 2 * probes,
                transcendentals=0,
            ),
            name="solve",
        )(everyone)
    else:
        owner = mine ^ jnp.array(offsets, jnp.int32)
        split = everyone.reshape(owners, slabs, members, 2, probes)[owner]
        split = split.transpose(3, 0, 2, 1, 4).reshape(2, order, slabs * probes)
        normal = split[0]
        misfit = split[1].reshape(owners, members, -1)
        misfit = jnp.concatenate([misfit[offsets.index(turn)] for turn in turns], axis=0)
        scaled = (jnp.mean(normal, axis=0, keepdims=True) - normal) * norm_scale
        gram_matrix = jnp.dot(
            scaled, scaled.T, precision=lax.Precision.HIGHEST, preferred_element_type=jnp.float32
        ) + damping * jnp.eye(order, dtype=jnp.float32)
        cross_term = jnp.dot(
            scaled, misfit.T, precision=lax.Precision.HIGHEST, preferred_element_type=jnp.float32
        )
        solved = eliminate(gram_matrix, cross_term).T.astype(jnp.bfloat16)
    rows = members * lines
    pieces = pl.pallas_call(
        lambda *refs: apply_kernel(norm_scale, lines, *refs),
        out_shape=[
            jax.ShapeDtypeStruct((rows, share), jnp.bfloat16 if turn else jnp.float32)
            for turn in turns
        ],
        in_specs=[vmem] * (1 + len(parts)),
        out_specs=[vmem] * len(turns),
        compiler_params=pltpu.CompilerParams(vmem_limit_bytes=40 * 1024 * 1024),
        cost_estimate=pl.CostEstimate(
            flops=2 * rows * order * lines * width,
            bytes_accessed=2 * order * lines * share,
            transcendentals=0,
        ),
        name="apply",
    )(solved, *parts[::-1])
    pieces = [
        across(pieces[turn], turn) if turn else pieces[turn] for turn in reversed(turns)
    ][::-1]
    revised = pl.pallas_call(
        merge_kernel,
        out_shape=jax.ShapeDtypeStruct((rows, width), jnp.float32),
        in_specs=[vmem] * (1 + len(turns)),
        out_specs=vmem,
        compiler_params=pltpu.CompilerParams(vmem_limit_bytes=8 * 1024 * 1024),
        name="merge",
    )(field_flat, *pieces[::-1])
    return (revised.reshape(logarithmic_diffusivity.shape), predicted)


def solution(mesh):
    in_specs = (
        P("mem", "sp", None),
        P("sp", None),
        P("sp", None),
        P("sp"),
        P("sp"),
        P("sp"),
        P("mem", "sp"),
    )
    out_specs = (P("mem", "sp", None), P("mem", "sp"))
    return jax.shard_map(body, mesh=mesh, in_specs=in_specs, out_specs=out_specs, check_vma=False)
```
